32 devices in a mesh: ctx: 8 (over z, y), tp: 4 (over x, core).
Axes of the slice: x: 2, y: 2, z: 4, core: 2. Of those that a mesh axis runs over, the one named last changes fastest.
Arguments:
- queries: bfloat16 [4096, 4096], P('ctx', 'tp'), may hold values from -6 to 6
- keys: bfloat16 [4096, 512], P('ctx', 'tp'), may hold values from -6 to 6
- values: bfloat16 [4096, 512], P('ctx', 'tp'), may hold values from -6 to 6
- out_weight: bfloat16 [4096, 8192], P('tp'), may hold values from -0.75 to 0.75
- vertical: int32 [32, 16], P('tp'), may hold values from 0 to 63, as said below
- slash: int32 [32, 8], P('tp'), may hold values from 0 to 15, as said below
Outputs:
- projected: bfloat16 [4096, 8192], P(('ctx', 'tp'))
The draws below stay inside these ranges and needn't reach their ends.
Inputs may be any that keep to these rules, and one draw needn't show every extreme that they name: `vertical`: each head's 16 blocks are distinct. For each index of tp, the blocks named by its 8 heads include at most 2 blocks of any one ctx shard of 512 tokens, and exactly 2 of some shard. `slash`: each head's first offset is 0 and its 8 offsets are distinct.
All inputs are finite; a program needn't handle non-finite values.
Results may differ from the reference program's by a relative error of at most 0.013.
Values may be sent and summed in bfloat16 or wider, within the bound.
No kernel may reach another device: no remote copies, remote signals or barrier semaphores. Data moves between devices by JAX's collectives and lax.ppermute only.
A program may use at most 128 MiB of HBM per device.

```python
import jax
import jax.numpy as jnp
from jax import lax

D = 8192
QH = 32
KVH = 4
HS = 128
BLK = 64
NV = 16
NS = 8
VMOST = 2
TOKENS = 4096
BLK_DEV = 8
SPAN = 16
HEADS_DEV = 8
POOL = 16


def draw_keys(key, part):
    shape_full = (TOKENS, KVH * HS)
    result = jax.random.truncated_normal(jax.random.fold_in(key, 31), -6.0, 6.0, shape_full, jnp.float32)
    return result.astype(jnp.bfloat16)


def draw_queries(key, part):
    shape_full = (TOKENS, QH * HS)
    result = jax.random.truncated_normal(jax.random.fold_in(key, 21), -6.0, 6.0, shape_full, jnp.float32)
    return result.astype(jnp.bfloat16)


def draw_vertical(key, part):
    shard_count = POOL // VMOST
    groups = QH // HEADS_DEV
    local_scores = jax.random.randint(jax.random.fold_in(key, 3), (groups, shard_count, BLK_DEV), 0, 65536) * BLK_DEV + jnp.arange(BLK_DEV, dtype=jnp.int32)
    local_order = jnp.argsort(local_scores, axis=-1, stable=True)[:, :, :VMOST]
    pool_blocks = (jnp.arange(shard_count, dtype=jnp.int32)[None, :, None] * BLK_DEV + local_order).reshape(groups, POOL)
    pool_owner = jnp.arange(POOL, dtype=jnp.int32) // VMOST
    favored = jax.random.randint(jax.random.fold_in(key, 5), (groups,), 0, shard_count)
    pool_ids = jnp.arange(POOL, dtype=jnp.int32)
    head_scores = jax.random.randint(jax.random.fold_in(key, 9), (groups, HEADS_DEV, POOL), 0, 65536) * POOL + pool_ids
    first_head = jnp.arange(HEADS_DEV)[None, :, None] == 0
    forced = first_head & (pool_owner[None, None, :] == favored[:, None, None])
    head_scores = jnp.where(forced, pool_ids - POOL, head_scores)
    chosen = jnp.argsort(head_scores, axis=-1, stable=True)[:, :, :NV]
    picked = jnp.take_along_axis(jnp.broadcast_to(pool_blocks[:, None, :], (groups, HEADS_DEV, POOL)), chosen, axis=-1)
    return picked.reshape(QH, NV).astype(jnp.int32)


def draw_slash(key, part):
    row_keys = jax.random.split(jax.random.fold_in(key, 4), QH)

    def one_row(row_key):
        shuffled = jax.random.permutation(row_key, SPAN - 1) + 1
        return jnp.concatenate([jnp.zeros((1,), jnp.int32), shuffled[:NS - 1].astype(jnp.int32)])
    return jax.vmap(one_row)(row_keys).astype(jnp.int32)


def level_of(stream_key, shape, cuts, smallest, high):
    def one(axis_at, shards_of):
        draws = jax.random.uniform(jax.random.fold_in(jax.random.fold_in(stream_key, 6), axis_at), (shards_of,), jnp.float32, smallest / len(cuts), high / len(cuts))
        return jnp.repeat(jnp.exp(draws), shape[axis_at] // shards_of).reshape((-1,) + (1,) * (len(shape) - axis_at - 1))

    factor_of = one(*cuts[0])
    for cut in cuts[1:]:
        factor_of = factor_of * one(*cut)
    return factor_of


def scatter_about(rng, extent, deviation, reach, cuts=(), held_as=jnp.bfloat16):
    drawn = jax.random.normal(rng, extent, jnp.float32) * deviation
    if len(cuts) > 0:
        drawn = level_of(rng, extent, cuts, -0.22, 0.18) * drawn
    return jnp.clip(drawn, min=-reach, max=reach).astype(held_as)


def setup_inputs(seed: int = 0) -> dict:
    key_of = jax.random.split(jax.random.key(seed), 7)
    return {
        "queries": draw_queries(jax.random.fold_in(key_of[6], 71), 0),
        "keys": draw_keys(jax.random.fold_in(key_of[6], 71), 0),
        "values": scatter_about(key_of[2], (TOKENS, KVH * HS), 1.0, 6.0, ((0, 8), (1, 4))),
        "out_weight": scatter_about(key_of[3], (QH * HS, D), 64 ** -0.5, 0.75, ((0, 4),)),
        "vertical": draw_vertical(jax.random.fold_in(key_of[6], 71), 0),
        "slash": draw_slash(jax.random.fold_in(key_of[6], 71), 0),
    }


def slot_table(vert_row, slash_row, query_blocks):
    block_count = query_blocks.shape[0]
    column_ids = query_blocks[:, None]
    vert_blocks = jnp.broadcast_to(vert_row[None, :], (block_count, vert_row.shape[0]))
    vert_ok = vert_blocks <= column_ids
    slash_blocks = column_ids - slash_row[None, :]
    repeated = jnp.any(slash_blocks[:, :, None] == vert_row[None, None, :], axis=2)
    slash_ok = (slash_blocks >= 0) & jnp.logical_not(repeated)
    blocks = jnp.concatenate([vert_blocks, slash_blocks], axis=1).astype(jnp.int32)
    usable = jnp.concatenate([vert_ok, slash_ok], axis=1)
    return (blocks, usable)

def attend_ref(head_query, key_tiles, value_tiles, blocks, usable, query_blocks):
    block_len = head_query.shape[1]
    score_scale = 1.0 / jnp.sqrt(jnp.float32(head_query.shape[2]))
    scores = jnp.einsum('ibd,isjd->ibsj', head_query.astype(jnp.float32), key_tiles.astype(jnp.float32)) * score_scale
    diagonal = blocks == query_blocks[:, None]
    positions = jnp.arange(block_len, dtype=jnp.int32)
    above_diag = positions[None, :] > positions[:, None]
    blocked = jnp.logical_not(usable)[:, None, :, None] | diagonal[:, None, :, None] & above_diag[None, :, None, :]
    scores = jnp.where(blocked, jnp.float32(-1e+30), scores)
    row_max = lax.optimization_barrier(jnp.max(scores, axis=(2, 3), keepdims=True))
    weights = jnp.exp(scores - row_max)
    row_total = lax.optimization_barrier(jnp.sum(weights, axis=(2, 3)))
    rounded_probs = weights.astype(jnp.bfloat16)
    attended = jnp.einsum('ibsj,isjd->ibd', rounded_probs.astype(jnp.float32), value_tiles.astype(jnp.float32))
    return (attended / row_total[:, :, None]).astype(jnp.bfloat16)

def reference(queries, keys, values, out_weight, vertical, slash):
    total_blocks = TOKENS // BLK
    group_size = QH // KVH
    query_blocks = jnp.arange(total_blocks, dtype=jnp.int32)

    def one_head(head_index):
        kv_index = head_index // group_size
        key_head = lax.dynamic_slice_in_dim(keys, kv_index * HS, HS, 1).reshape(total_blocks, BLK, HS)
        value_head = lax.dynamic_slice_in_dim(values, kv_index * HS, HS, 1).reshape(total_blocks, BLK, HS)
        head_query = lax.dynamic_slice_in_dim(queries, head_index * HS, HS, 1).reshape(total_blocks, BLK, HS)
        blocks, usable = slot_table(vertical[head_index], slash[head_index], query_blocks)
        clipped = jnp.clip(blocks, 0, total_blocks - 1)
        return attend_ref(head_query, key_head[clipped], value_head[clipped], blocks, usable, query_blocks)
    heads_out = lax.map(one_head, jnp.arange(QH, dtype=jnp.int32))
    attended = heads_out.transpose(1, 2, 0, 3).reshape(TOKENS, QH * HS)
    width = HEADS_DEV * HS
    summed = jnp.zeros((TOKENS, D), jnp.float32)
    for group_index in range(QH // HEADS_DEV):
        product = jnp.dot(attended[:, group_index * width:(group_index + 1) * width], out_weight[group_index * width:(group_index + 1) * width], preferred_element_type=jnp.float32)
        rounded = lax.optimization_barrier(product.astype(jnp.bfloat16))
        summed = summed + rounded.astype(jnp.float32)
    return summed.astype(jnp.bfloat16)
```

```python
import functools

import jax
import jax.numpy as jnp
from jax import lax
from jax.experimental import pallas as pl
from jax.experimental.pallas import tpu as pltpu
from jax.sharding import PartitionSpec as P

HS = 128
BLK = 64
SPAN = 16
VMOST = 2
LANES = 128
MASKED = -1e30
EXP_SCALE = 1.4426950408889634 / (HS**0.5)
CHUNKS = 4
TILE = 512
VMEM_LIMIT = 56 * 1024 * 1024


def vmem():
    return pl.BlockSpec(memory_space=pltpu.VMEM)


def smem():
    return pl.BlockSpec(memory_space=pltpu.SMEM)


def params():
    return pltpu.CompilerParams(vmem_limit_bytes=VMEM_LIMIT)


def pick_kernel(rank_ref, vert_ref, k_ref, v_ref, out_ref):
    local_blocks = k_ref.shape[0] // BLK
    heads, count = vert_ref.shape
    base = rank_ref[0] * local_blocks
    used = jnp.int32(0)
    for head in range(heads):
        for slot in range(count):
            block = vert_ref[head, slot] - base
            inside = (block >= 0) & (block < local_blocks)
            bit = jnp.left_shift(jnp.int32(1), jnp.clip(block, 0, local_blocks - 1))
            used = used | jnp.where(inside, bit, 0)
    first = jnp.int32(local_blocks)
    second = jnp.int32(local_blocks)
    for block in reversed(range(local_blocks)):
        here = ((used >> block) & 1) == 1
        second = jnp.where(here, first, second)
        first = jnp.where(here, block, first)
    for slot, block in enumerate((first, second)):
        start = pl.multiple_of(jnp.minimum(block, local_blocks - 1) * BLK, BLK)
        out_ref[slot * BLK : (slot + 1) * BLK, :HS] = k_ref[pl.ds(start, BLK), :]
        out_ref[slot * BLK : (slot + 1) * BLK, HS:] = v_ref[pl.ds(start, BLK), :]


def pick(rank, vertical, keys, values):
    return pl.pallas_call(
        pick_kernel,
        out_shape=jax.ShapeDtypeStruct((VMOST * BLK, 2 * HS), keys.dtype),
        in_specs=[smem(), smem(), vmem(), vmem()],
        out_specs=vmem(),
        compiler_params=params(),
        name="pick",
    )(rank, vertical, keys, values)


def mask_kernel(local_blocks, rank_ref, vert_ref, slash_ref, win_ref, pool_ref):
    heads, vert_count = vert_ref.shape
    slash_count = slash_ref.shape[1]
    rank = rank_ref[0]
    lane = lax.broadcasted_iota(jnp.int32, (heads, LANES), 1)
    vert = [vert_ref[:, s : s + 1] for s in range(vert_count)]
    zero = jnp.zeros((heads, LANES), jnp.float32)

    def member(columns, blocks):
        found = columns[0] == blocks
        for column in columns[1:]:
            found = found | (column == blocks)
        return found

    offset_ok = member([slash_ref[:, s : s + 1] for s in range(slash_count)], SPAN - 1 - lane)
    shard = rank - 2 - lane // VMOST
    first = jnp.full((1, LANES), local_blocks, jnp.int32)
    second = first
    for j in reversed(range(local_blocks)):
        here = member(vert, shard * local_blocks + j)
        here = jnp.max(jnp.where(here, 1, 0), axis=0, keepdims=True) == 1
        second = jnp.where(here, first, second)
        first = jnp.where(here, j, first)
    picked = jnp.where(lane % VMOST == 0, first, second)
    block = shard * local_blocks + picked
    pool_ok = (picked < local_blocks) & (shard >= 0) & member(vert, block)
    for i in range(local_blocks):
        row = rank * local_blocks + i
        seen = row - (SPAN - 1) + lane
        ok = (seen >= 0) & (offset_ok | member(vert, seen))
        win_ref[i] = jnp.where(ok | (lane >= SPAN), zero, MASKED)
        pool_ref[i] = jnp.where(pool_ok & (block < row - (SPAN - 1)), zero, MASKED)


def masks(rank, vertical, slash, local_blocks):
    heads = vertical.shape[0]
    shape = jax.ShapeDtypeStruct((local_blocks, heads, LANES), jnp.float32)
    return pl.pallas_call(
        functools.partial(mask_kernel, local_blocks),
        out_shape=(shape, shape),
        in_specs=[smem(), vmem(), vmem()],
        out_specs=(vmem(), vmem()),
        compiler_params=params(),
        name="masks",
    )(rank, vertical, slash)


def attend_kernel(near, pools, ids_ref, q_ref, win_ref, pool_ref, *refs):
    kv_refs = refs[: 2 * near]
    pool_kv = refs[2 * near : 2 * near + pools]
    out_ref = refs[-7]
    k_win, v_win, e_win, k_pool, v_pool, e_pool = refs[-6:]
    step = pl.program_id(0)
    heads = win_ref.shape[1]
    rows = kv_refs[0].shape[0]

    @pl.when(step == 0)
    def _():
        for s in range(near):
            k_win[s * rows : (s + 1) * rows, :] = kv_refs[2 * s][...]
            v_win[s * rows : (s + 1) * rows, :] = kv_refs[2 * s + 1][...]
        for s in range(pools):
            at = slice(s * VMOST * BLK, (s + 1) * VMOST * BLK)
            k_pool[at, :] = pool_kv[s][:, :HS]
            v_pool[at, :] = pool_kv[s][:, HS:]
        key = lax.broadcasted_iota(jnp.int32, e_win.shape, 0)
        lane = lax.broadcasted_iota(jnp.int32, e_win.shape, 1)
        last = (key // BLK == SPAN - 1) & (key % BLK == lane - BLK)
        e_win[...] = jnp.where((key // BLK == lane) | last, 1.0, 0.0).astype(e_win.dtype)
        key = lax.broadcasted_iota(jnp.int32, e_pool.shape, 0)
        lane = lax.broadcasted_iota(jnp.int32, e_pool.shape, 1)
        e_pool[...] = jnp.where(key // BLK == lane, 1.0, 0.0).astype(e_pool.dtype)

    here = ids_ref[step]
    q = q_ref[...]
    q = jnp.concatenate([q[:, h * HS : (h + 1) * HS] for h in range(heads)], axis=0)
    row = lax.broadcasted_iota(jnp.int32, (BLK, LANES), 0)
    lane = lax.broadcasted_iota(jnp.int32, (BLK, LANES), 1)
    above = jnp.where(lane - BLK > row, MASKED, 0.0).astype(jnp.float32)
    win_mask = win_ref[0][:, None, :] + above[None]
    win_mask = win_mask.reshape(heads * BLK, LANES).astype(q.dtype)
    pool_mask = jnp.broadcast_to(pool_ref[0][:, None, :], (heads, BLK, LANES))
    pool_mask = pool_mask.reshape(heads * BLK, LANES).astype(q.dtype)

    start = pl.multiple_of((here + 1) * BLK, BLK)
    keys = jnp.concatenate([k_win[pl.ds(start, SPAN * BLK), :], e_win[...]], axis=1)
    contract = (((1,), (1,)), ((), ()))
    near_scores = lax.dot_general(
        jnp.concatenate([q, win_mask], axis=1), keys, contract, preferred_element_type=jnp.float32
    )
    far_keys = jnp.concatenate([k_pool[...], e_pool[...]], axis=1)
    far_scores = lax.dot_general(
        jnp.concatenate([q, pool_mask], axis=1),
        far_keys,
        contract,
        preferred_element_type=jnp.float32,
    )
    top = jnp.maximum(
        jnp.max(near_scores, axis=1, keepdims=True), jnp.max(far_scores, axis=1, keepdims=True)
    )
    near_probs = jnp.exp2((near_scores - top) * EXP_SCALE).astype(q.dtype)
    far_probs = jnp.exp2((far_scores - top) * EXP_SCALE).astype(q.dtype)
    near_values = jnp.concatenate(
        [v_win[pl.ds(start, SPAN * BLK), :], jnp.ones((SPAN * BLK, LANES), q.dtype)], axis=1
    )
    far_values = jnp.concatenate(
        [v_pool[...], jnp.ones((v_pool.shape[0], LANES), q.dtype)], axis=1
    )
    summed = jnp.dot(near_probs, near_values, preferred_element_type=jnp.float32)
    summed = summed + jnp.dot(far_probs, far_values, preferred_element_type=jnp.float32)
    out = (summed[:, :HS] / summed[:, HS:]).astype(out_ref.dtype)
    for h in range(heads):
        out_ref[:, h * HS : (h + 1) * HS] = out[h * BLK : (h + 1) * BLK]


def attend(ids, queries, win, pool, near_kv, pool_kv, after):
    steps = ids.shape[0]
    width = queries.shape[1]
    heads = win.shape[1]
    near, pools = len(near_kv), len(pool_kv)
    rows = near_kv[0][0].shape[0]
    dtype = queries.dtype

    def whole(x):
        return pl.BlockSpec(x.shape, lambda g, ids: (0,) * x.ndim)

    flat = [x for pair in near_kv for x in pair] + list(pool_kv)
    table = pl.BlockSpec((1, heads, LANES), lambda g, ids: (ids[g], 0, 0))
    keys_seen = SPAN * BLK + pools * VMOST * BLK
    flops = steps * heads * BLK * keys_seen * 256 * 4
    return pl.pallas_call(
        functools.partial(attend_kernel, near, pools),
        out_shape=jax.ShapeDtypeStruct((steps * BLK, width), dtype),
        grid_spec=pltpu.PrefetchScalarGridSpec(
            num_scalar_prefetch=1,
            grid=(steps,),
            in_specs=[pl.BlockSpec((BLK, width), lambda g, ids: (ids[g], 0)), table, table]
            + [whole(x) for x in flat]
            + [pl.BlockSpec(memory_space=pl.ANY) for _ in after],
            out_specs=pl.BlockSpec((BLK, width), lambda g, ids: (g, 0)),
            scratch_shapes=[
                pltpu.VMEM((near * rows, HS), dtype),
                pltpu.VMEM((near * rows, HS), dtype),
                pltpu.VMEM((SPAN * BLK, LANES), dtype),
                pltpu.VMEM((pools * VMOST * BLK, HS), dtype),
                pltpu.VMEM((pools * VMOST * BLK, HS), dtype),
                pltpu.VMEM((pools * VMOST * BLK, LANES), dtype),
            ],
        ),
        compiler_params=params(),
        cost_estimate=pl.CostEstimate(
            flops=flops, bytes_accessed=steps * BLK * width * 4, transcendentals=0
        ),
        name="attend",
    )(ids, queries, win, pool, *flat, *after)


def project_kernel(a_ref, w_ref, *refs):
    send_ref, keep_ref = refs[-2:]
    half = send_ref.shape[0]
    product = jnp.dot(a_ref[...], w_ref[...], preferred_element_type=jnp.float32)
    product = product.astype(send_ref.dtype)
    send_ref[...] = product[:half]
    keep_ref[...] = product[half:]


def project(attended, out_weight, chunk, after):
    rows, depth = attended.shape
    columns = out_weight.shape[1] // CHUNKS
    tiles = columns // TILE
    half = jax.ShapeDtypeStruct((rows // 2, columns), attended.dtype)
    return pl.pallas_call(
        project_kernel,
        out_shape=(half, half),
        grid=(tiles,),
        in_specs=[
            pl.BlockSpec((rows, depth), lambda g: (0, 0)),
            pl.BlockSpec((depth, TILE), lambda g: (0, chunk * tiles + g)),
        ]
        + [pl.BlockSpec(memory_space=pl.ANY) for _ in after],
        out_specs=(
            pl.BlockSpec((rows // 2, TILE), lambda g: (0, g)),
            pl.BlockSpec((rows // 2, TILE), lambda g: (0, g)),
        ),
        compiler_params=params(),
        cost_estimate=pl.CostEstimate(
            flops=2 * rows * depth * columns,
            bytes_accessed=2 * columns * (depth + rows),
            transcendentals=0,
        ),
        name="project",
    )(attended, out_weight, *after)


def add(*terms):
    total = terms[0].astype(jnp.float32)
    for term in terms[1:]:
        total = total + term.astype(jnp.float32)
    return total.astype(terms[0].dtype)


def shards(ctx_size, queries, keys, values, out_weight, vertical, slash):
    local_blocks = queries.shape[0] // BLK
    near = 1 + -(-(SPAN - 1) // local_blocks)
    ctx_rank = lax.axis_index("ctx")
    tp_rank = lax.axis_index("tp")
    rank = jnp.reshape(ctx_rank, (1,)).astype(jnp.int32)

    def shifted(x, by):
        return lax.ppermute(x, "ctx", [(r, r + by) for r in range(ctx_size - by)])

    near_kv = [(shifted(keys, s), shifted(values, s)) for s in range(near - 1, 0, -1)]
    near_kv.append((keys, values))
    own = pick(rank, vertical, keys, values)
    pool_kv = [shifted(own, s) for s in range(2, ctx_size)]
    win, pool = masks(rank, vertical, slash, local_blocks)

    quarter = local_blocks // 4
    inner = jnp.arange(quarter, dtype=jnp.int32)

    def blocks_of(first, second):
        return jnp.concatenate([first * quarter + inner, second * quarter + inner])

    def sibling(x):
        return lax.ppermute(x, "tp", [(j, j ^ 1) for j in range(4)])

    def across(x):
        return lax.ppermute(x, "tp", [(j, j ^ 2) for j in range(4)])

    other_ids = blocks_of(tp_rank ^ 3, tp_rank ^ 2)
    attended = attend(other_ids, queries, win, pool, near_kv, pool_kv, ())
    arrived = []
    after = ()
    for c in range(CHUNKS):
        send, keep = project(attended, out_weight, c, after)
        after = (send,)
        arrived.append(across(add(keep, sibling(send))))
    own_ids = blocks_of(tp_rank ^ 1, tp_rank)
    attended = attend(own_ids, queries, win, pool, near_kv, pool_kv, after)
    outs = []
    after = ()
    for c in range(CHUNKS):
        send, keep = project(attended, out_weight, c, after)
        after = (send,)
        outs.append(add(keep, sibling(send), arrived[c]))
    return jnp.concatenate(outs, axis=1)


def solution(mesh):
    assert mesh.shape["tp"] == 4
    return jax.shard_map(
        functools.partial(shards, mesh.shape["ctx"]),
        mesh=mesh,
        in_specs=(
            P("ctx", "tp"),
            P("ctx", "tp"),
            P("ctx", "tp"),
            P("tp", None),
            P("tp", None),
            P("tp", None),
        ),
        out_specs=P(("ctx", "tp"), None),
        check_vma=False,
    )
```

```python
import functools

import jax
import jax.numpy as jnp
from jax import lax
from jax.experimental import pallas as pl
from jax.experimental.pallas import tpu as pltpu
from jax.sharding import PartitionSpec as P

HS = 128
BLK = 64
SPAN = 16
VMOST = 2
LANES = 128
MASKED = -1e30
EXP_SCALE = 1.4426950408889634 / (HS**0.5)
CHUNKS = 4
TILE = 1024
WEIGHT_PARTS = 4
MIB = 1024 * 1024


def vmem():
    return pl.BlockSpec(memory_space=pltpu.VMEM)


def smem():
    return pl.BlockSpec(memory_space=pltpu.SMEM)


def params(mib):
    return pltpu.CompilerParams(vmem_limit_bytes=mib * MIB)


def pick_kernel(rank_ref, vert_ref, k_ref, v_ref, both_ref, out_ref):
    local_blocks = k_ref.shape[0] // BLK
    heads, count = vert_ref.shape
    base = rank_ref[0] * local_blocks
    used = jnp.int32(0)
    for head in range(heads):
        for slot in range(count):
            block = vert_ref[head, slot] - base
            inside = (block >= 0) & (block < local_blocks)
            bit = jnp.left_shift(jnp.int32(1), jnp.clip(block, 0, local_blocks - 1))
            used = used | jnp.where(inside, bit, 0)
    first = jnp.int32(local_blocks)
    second = jnp.int32(local_blocks)
    for block in reversed(range(local_blocks)):
        here = ((used >> block) & 1) == 1
        second = jnp.where(here, first, second)
        first = jnp.where(here, block, first)
    both_ref[:, :HS] = k_ref[...]
    both_ref[:, HS:] = v_ref[...]
    for slot, block in enumerate((first, second)):
        start = pl.multiple_of(jnp.minimum(block, local_blocks - 1) * BLK, BLK)
        rows = jnp.concatenate([k_ref[pl.ds(start, BLK), :], v_ref[pl.ds(start, BLK), :]], axis=1)
        for copy in range(out_ref.shape[0]):
            out_ref[copy, slot * BLK : (slot + 1) * BLK, :] = rows


def pick(rank, vertical, keys, values, copies):
    return pl.pallas_call(
        pick_kernel,
        out_shape=(
            jax.ShapeDtypeStruct((keys.shape[0], 2 * HS), keys.dtype),
            jax.ShapeDtypeStruct((copies, VMOST * BLK, 2 * HS), keys.dtype),
        ),
        in_specs=[smem(), smem(), vmem(), vmem()],
        out_specs=(vmem(), vmem()),
        compiler_params=params(8),
        name="pick",
    )(rank, vertical, keys, values)


def mask_kernel(local_blocks, rank_ref, vert_ref, slash_ref, win_ref, pool_ref):
    heads, vert_count = vert_ref.shape
    slash_count = slash_ref.shape[1]
    rank = rank_ref[0]
    lane = lax.broadcasted_iota(jnp.int32, (heads, LANES), 1)
    vert = [vert_ref[:, s : s + 1] for s in range(vert_count)]
    zero = jnp.zeros((heads, LANES), jnp.float32)

    def member(columns, blocks):
        found = columns[0] == blocks
        for column in columns[1:]:
            found = found | (column == blocks)
        return found

    offset_ok = member([slash_ref[:, s : s + 1] for s in range(slash_count)], SPAN - 1 - lane)
    shard = lane // VMOST
    first = jnp.full((1, LANES), local_blocks, jnp.int32)
    second = first
    for j in reversed(range(local_blocks)):
        here = member(vert, shard * local_blocks + j)
        here = jnp.max(jnp.where(here, 1, 0), axis=0, keepdims=True) == 1
        second = jnp.where(here, first, second)
        first = jnp.where(here, j, first)
    picked = jnp.where(lane % VMOST == 0, first, second)
    block = shard * local_blocks + picked
    pool_ok = (picked < local_blocks) & member(vert, block)
    for i in range(local_blocks):
        row = rank * local_blocks + i
        seen = row - (SPAN - 1) + lane
        ok = (seen >= 0) & (offset_ok | member(vert, seen))
        win_ref[i] = jnp.where(ok | (lane >= SPAN), zero, MASKED)
        pool_ref[i] = jnp.where(pool_ok & (block < row - (SPAN - 1)), zero, MASKED)


def masks(rank, vertical, slash, local_blocks):
    heads = vertical.shape[0]
    shape = jax.ShapeDtypeStruct((local_blocks, heads, LANES), jnp.float32)
    return pl.pallas_call(
        functools.partial(mask_kernel, local_blocks),
        out_shape=(shape, shape),
        in_specs=[smem(), vmem(), vmem()],
        out_specs=(vmem(), vmem()),
        compiler_params=params(8),
        name="masks",
    )(rank, vertical, slash)


def attend_kernel(near, pools, ids_ref, q_ref, win_ref, pool_ref, *refs):
    kv_refs = refs[:near]
    pool_kv = refs[near]
    out_ref = refs[-7]
    k_win, v_win, e_win, k_pool, v_pool, e_pool = refs[-6:]
    step = pl.program_id(0)
    heads = win_ref.shape[1]
    rows = kv_refs[0].shape[0]

    @pl.when(step == 0)
    def _():
        for s in range(near):
            k_win[s * rows : (s + 1) * rows, :] = kv_refs[s][:, :HS]
            v_win[s * rows : (s + 1) * rows, :] = kv_refs[s][:, HS:]
        for s in range(pools):
            at = slice(s * VMOST * BLK, (s + 1) * VMOST * BLK)
            k_pool[at, :] = pool_kv[s, :, :HS]
            v_pool[at, :] = pool_kv[s, :, HS:]
        key = lax.broadcasted_iota(jnp.int32, e_win.shape, 0)
        lane = lax.broadcasted_iota(jnp.int32, e_win.shape, 1)
        last = (key // BLK == SPAN - 1) & (key % BLK == lane - BLK)
        e_win[...] = jnp.where((key // BLK == lane) | last, 1.0, 0.0).astype(e_win.dtype)
        key = lax.broadcasted_iota(jnp.int32, e_pool.shape, 0)
        lane = lax.broadcasted_iota(jnp.int32, e_pool.shape, 1)
        e_pool[...] = jnp.where(key // BLK == lane, 1.0, 0.0).astype(e_pool.dtype)

    here = ids_ref[step]
    q = q_ref[...]
    q = jnp.concatenate([q[:, h * HS : (h + 1) * HS] for h in range(heads)], axis=0)
    row = lax.broadcasted_iota(jnp.int32, (BLK, LANES), 0)
    lane = lax.broadcasted_iota(jnp.int32, (BLK, LANES), 1)
    above = jnp.where(lane - BLK > row, MASKED, 0.0).astype(jnp.float32)
    win_mask = win_ref[0][:, None, :] + above[None]
    win_mask = win_mask.reshape(heads * BLK, LANES).astype(q.dtype)
    pool_mask = jnp.broadcast_to(pool_ref[0][:, None, :], (heads, BLK, LANES))
    pool_mask = pool_mask.reshape(heads * BLK, LANES).astype(q.dtype)

    start = pl.multiple_of((here + 1) * BLK, BLK)
    keys = jnp.concatenate([k_win[pl.ds(start, SPAN * BLK), :], e_win[...]], axis=1)
    contract = (((1,), (1,)), ((), ()))
    near_scores = lax.dot_general(
        jnp.concatenate([q, win_mask], axis=1), keys, contract, preferred_element_type=jnp.float32
    )
    far_keys = jnp.concatenate([k_pool[...], e_pool[...]], axis=1)
    far_scores = lax.dot_general(
        jnp.concatenate([q, pool_mask], axis=1),
        far_keys,
        contract,
        preferred_element_type=jnp.float32,
    )
    top = jnp.maximum(
        jnp.max(near_scores, axis=1, keepdims=True), jnp.max(far_scores, axis=1, keepdims=True)
    )
    near_probs = jnp.exp2((near_scores - top) * EXP_SCALE).astype(q.dtype)
    far_probs = jnp.exp2((far_scores - top) * EXP_SCALE).astype(q.dtype)
    near_values = jnp.concatenate(
        [v_win[pl.ds(start, SPAN * BLK), :], jnp.ones((SPAN * BLK, LANES), q.dtype)], axis=1
    )
    far_values = jnp.concatenate(
        [v_pool[...], jnp.ones((v_pool.shape[0], LANES), q.dtype)], axis=1
    )
    summed = jnp.dot(near_probs, near_values, preferred_element_type=jnp.float32)
    summed = summed + jnp.dot(far_probs, far_values, preferred_element_type=jnp.float32)
    out = (summed[:, :HS] / summed[:, HS:]).astype(out_ref.dtype)
    for h in range(heads):
        out_ref[:, h * HS : (h + 1) * HS] = out[h * BLK : (h + 1) * BLK]


def attend(ids, queries, win, pool, near_kv, pool_kv, after):
    steps = ids.shape[0]
    width = queries.shape[1]
    heads = win.shape[1]
    near, pools = len(near_kv), pool_kv.shape[0] - 2
    rows = near_kv[0].shape[0]
    dtype = queries.dtype

    def whole(x):
        return pl.BlockSpec(x.shape, lambda g, ids: (0,) * x.ndim)

    flat = [*near_kv, pool_kv]
    table = pl.BlockSpec((1, heads, LANES), lambda g, ids: (ids[g], 0, 0))
    keys_seen = SPAN * BLK + pools * VMOST * BLK
    flops = steps * heads * BLK * keys_seen * 256 * 4
    return pl.pallas_call(
        functools.partial(attend_kernel, near, pools),
        out_shape=jax.ShapeDtypeStruct((steps * BLK, width), dtype),
        grid_spec=pltpu.PrefetchScalarGridSpec(
            num_scalar_prefetch=1,
            grid=(steps,),
            in_specs=[pl.BlockSpec((BLK, width), lambda g, ids: (ids[g], 0)), table, table]
            + [whole(x) for x in near_kv]
            + [pl.BlockSpec((pools,) + pool_kv.shape[1:], lambda g, ids: (0, 0, 0))]
            + [pl.BlockSpec(memory_space=pl.ANY) for _ in after],
            out_specs=pl.BlockSpec((BLK, width), lambda g, ids: (g, 0)),
            scratch_shapes=[
                pltpu.VMEM((near * rows, HS), dtype),
                pltpu.VMEM((near * rows, HS), dtype),
                pltpu.VMEM((SPAN * BLK, LANES), dtype),
                pltpu.VMEM((pools * VMOST * BLK, HS), dtype),
                pltpu.VMEM((pools * VMOST * BLK, HS), dtype),
                pltpu.VMEM((pools * VMOST * BLK, LANES), dtype),
            ],
        ),
        compiler_params=params(28),
        cost_estimate=pl.CostEstimate(
            flops=flops, bytes_accessed=steps * BLK * width * 4, transcendentals=0
        ),
        name="attend",
    )(ids, queries, win, pool, *flat, *after)


def project_kernel(a_ref, *refs):
    send_ref, keep_ref = refs[-2:]
    half = send_ref.shape[0]
    product = None
    for part in range(WEIGHT_PARTS):
        w = refs[part][...]
        depth = w.shape[0]
        term = jnp.dot(
            a_ref[:, part * depth : (part + 1) * depth], w, preferred_element_type=jnp.float32
        )
        product = term if product is None else product + term
    product = product.astype(send_ref.dtype)
    send_ref[...] = product[:half]
    keep_ref[...] = product[half:]


def project(attended, out_weight, chunk, after):
    rows, depth = attended.shape
    columns = out_weight.shape[1] // CHUNKS
    tiles = columns // TILE
    half = jax.ShapeDtypeStruct((rows // 2, columns), attended.dtype)

    def weight(part):
        return pl.BlockSpec((depth // WEIGHT_PARTS, TILE), lambda g: (part, chunk * tiles + g))

    return pl.pallas_call(
        project_kernel,
        out_shape=(half, half),
        grid=(tiles,),
        in_specs=[pl.BlockSpec((rows, depth), lambda g: (0, 0))]
        + [weight(part) for part in range(WEIGHT_PARTS)]
        + [pl.BlockSpec(memory_space=pl.ANY) for _ in after],
        out_specs=(
            pl.BlockSpec((rows // 2, TILE), lambda g: (0, g)),
            pl.BlockSpec((rows // 2, TILE), lambda g: (0, g)),
        ),
        compiler_params=params(16),
        cost_estimate=pl.CostEstimate(
            flops=2 * rows * depth * columns,
            bytes_accessed=2 * columns * (depth + rows),
            transcendentals=0,
        ),
        name="project",
    )(attended, *[out_weight] * WEIGHT_PARTS, *after)


def add(*terms):
    total = terms[0].astype(jnp.float32)
    for term in terms[1:]:
        total = total + term.astype(jnp.float32)
    return total.astype(terms[0].dtype)


def shards(ctx_size, queries, keys, values, out_weight, vertical, slash):
    local_blocks = queries.shape[0] // BLK
    near = 1 + -(-(SPAN - 1) // local_blocks)
    ctx_rank = lax.axis_index("ctx")
    tp_rank = lax.axis_index("tp")
    rank = jnp.reshape(ctx_rank, (1,)).astype(jnp.int32)

    def shifted(x, by):
        return lax.ppermute(x, "ctx", [(r, r + by) for r in range(ctx_size - by)])

    own, pair = pick(rank, vertical, keys, values, ctx_size)
    near_kv = [shifted(own, s) for s in range(near - 1, 0, -1)] + [own]
    pool_kv = lax.all_to_all(pair, "ctx", split_axis=0, concat_axis=0, tiled=True)
    win, pool = masks(rank, vertical, slash, local_blocks)

    quarter = local_blocks // 4
    inner = jnp.arange(quarter, dtype=jnp.int32)

    def blocks_of(first, second):
        return jnp.concatenate([first * quarter + inner, second * quarter + inner])

    def sibling(x):
        return lax.ppermute(x, "tp", [(j, j ^ 1) for j in range(4)])

    def across(x):
        return lax.ppermute(x, "tp", [(j, j ^ 2) for j in range(4)])

    other_ids = blocks_of(tp_rank ^ 3, tp_rank ^ 2)
    attended = attend(other_ids, queries, win, pool, near_kv, pool_kv, ())
    arrived = []
    sums = []
    for c in range(CHUNKS):
        send, keep = project(attended, out_weight, c, sums[c - 2 : c - 1] if c > 1 else ())
        sums.append(add(keep, sibling(send)))
        arrived.append(across(sums[c]))
    own_ids = blocks_of(tp_rank ^ 1, tp_rank)
    attended = attend(own_ids, queries, win, pool, near_kv, pool_kv, (sums[-2],))
    outs = []
    after = (sums[-1],)
    for c in range(CHUNKS):
        send, keep = project(attended, out_weight, c, after)
        after = (send,)
        outs.append(add(add(keep, sibling(send)), arrived[c]))
    return jnp.concatenate(outs, axis=1)


def solution(mesh):
    assert mesh.shape["tp"] == 4
    return jax.shard_map(
        functools.partial(shards, mesh.shape["ctx"]),
        mesh=mesh,
        in_specs=(
            P("ctx", "tp"),
            P("ctx", "tp"),
            P("ctx", "tp"),
            P("tp", None),
            P("tp", None),
            P("tp", None),
        ),
        out_specs=P(("ctx", "tp"), None),
        check_vma=False,
    )
```

```python
import functools

import jax
import jax.numpy as jnp
from jax import lax
from jax.experimental import pallas as pl
from jax.experimental.pallas import tpu as pltpu
from jax.sharding import PartitionSpec as P

HS = 128
BLK = 64
SPAN = 16
VMOST = 2
LANES = 128
MASKED = -1e30
EXP_SCALE = 1.4426950408889634 / (HS**0.5)
TILE = 1024
ACROSS = ((0, 2), (4, 4), (2, 2))
WEIGHT_PARTS = 4
MIB = 1024 * 1024


SHORT = pl.CostEstimate(flops=0, bytes_accessed=0, transcendentals=0)


def vmem():
    return pl.BlockSpec(memory_space=pltpu.VMEM)


def smem():
    return pl.BlockSpec(memory_space=pltpu.SMEM)


def anywhere():
    return pl.BlockSpec(memory_space=pl.ANY)


def params(mib):
    return pltpu.CompilerParams(vmem_limit_bytes=mib * MIB)


def pick_kernel(rank_ref, vert_ref, k_ref, v_ref, _, out_ref):
    local_blocks = k_ref.shape[0] // BLK
    block = vert_ref[...] - rank_ref[0] * local_blocks
    block = jnp.where((block >= 0) & (block < local_blocks), block, local_blocks)
    first = jnp.min(block)
    second = jnp.min(jnp.where(block > first, block, local_blocks))
    for slot, block in enumerate((first, second)):
        start = pl.multiple_of(jnp.minimum(block, local_blocks - 1) * BLK, BLK)
        out_ref[slot * BLK : (slot + 1) * BLK, :HS] = k_ref[pl.ds(start, BLK), :]
        out_ref[slot * BLK : (slot + 1) * BLK, HS:] = v_ref[pl.ds(start, BLK), :]


def pick(rank, vertical, keys, values, after):
    return pl.pallas_call(
        pick_kernel,
        out_shape=jax.ShapeDtypeStruct((VMOST * BLK, 2 * HS), keys.dtype),
        in_specs=[smem(), vmem(), vmem(), vmem(), anywhere()],
        out_specs=vmem(),
        compiler_params=params(56),
        name="pick",
    )(rank, vertical, keys, values, after)


def mask_kernel(local_blocks, near, rank_ref, vert_ref, slash_ref, win_ref, pool_ref):
    heads, vert_count = vert_ref.shape
    slash_count = slash_ref.shape[1]
    rank = rank_ref[0]
    lane = lax.broadcasted_iota(jnp.int32, (heads, LANES), 1)
    vert = [vert_ref[:, s : s + 1] for s in range(vert_count)]
    zero = jnp.zeros((heads, LANES), jnp.float32)

    def member(columns, blocks):
        found = columns[0] == blocks
        for column in columns[1:]:
            found = found | (column == blocks)
        return found

    offset_ok = member([slash_ref[:, s : s + 1] for s in range(slash_count)], SPAN - 1 - lane)
    shard = rank - (near - 1) - lane // VMOST
    first = jnp.full((1, LANES), local_blocks, jnp.int32)
    second = first
    for j in reversed(range(local_blocks)):
        here = member(vert, shard * local_blocks + j)
        here = jnp.max(jnp.where(here, 1, 0), axis=0, keepdims=True) == 1
        second = jnp.where(here, first, second)
        first = jnp.where(here, j, first)
    picked = jnp.where(lane % VMOST == 0, first, second)
    block = shard * local_blocks + picked
    pool_ok = (picked < local_blocks) & (shard >= 0) & member(vert, block)
    for i in range(local_blocks):
        row = rank * local_blocks + i
        seen = row - (SPAN - 1) + lane
        ok = (seen >= 0) & (offset_ok | member(vert, seen))
        win_ref[i] = jnp.where(ok | (lane >= SPAN), zero, MASKED)
        pool_ref[i] = jnp.where(pool_ok & (block < row - (SPAN - 1)), zero, MASKED)


def masks(rank, vertical, slash, local_blocks, near):
    heads = vertical.shape[0]
    shape = jax.ShapeDtypeStruct((local_blocks, heads, LANES), jnp.float32)
    return pl.pallas_call(
        functools.partial(mask_kernel, local_blocks, near),
        out_shape=(shape, shape),
        in_specs=[smem(), vmem(), vmem()],
        out_specs=(vmem(), vmem()),
        compiler_params=params(56),
        name="masks",
    )(rank, vertical, slash)


def attend_kernel(near, pools, with_rows, ids_ref, q_ref, win_ref, pool_ref, *refs):
    kv_refs = refs[: 2 * near]
    pair_refs = refs[2 * near : 2 * near + pools]
    w_hbm = refs[2 * near + pools]
    k_win, v_win, e_win, k_pool, v_pool, e_pool, attended, weight, arrival = refs[-9:]
    step = pl.program_id(0)
    heads = win_ref.shape[1]
    rows = kv_refs[0].shape[0]
    tiles, _, tile = weight.shape
    outs = refs[-9 - 2 * tiles - with_rows : -9]

    def fetch(t):
        return pltpu.make_async_copy(
            w_hbm.at[:, pl.ds(t * tile, tile)], weight.at[t], arrival.at[t]
        )

    @pl.when(step == 0)
    def _():
        for t in range(tiles):
            fetch(t).start()
        for s in range(near):
            k_win[s * rows : (s + 1) * rows, :] = kv_refs[2 * s][...]
            v_win[s * rows : (s + 1) * rows, :] = kv_refs[2 * s + 1][...]
        for s in range(pools):
            at = slice(s * VMOST * BLK, (s + 1) * VMOST * BLK)
            k_pool[at, :] = pair_refs[s][:, :HS]
            v_pool[at, :] = pair_refs[s][:, HS:]
        key = lax.broadcasted_iota(jnp.int32, e_win.shape, 0)
        lane = lax.broadcasted_iota(jnp.int32, e_win.shape, 1)
        last = (key // BLK == SPAN - 1) & (key % BLK == lane - BLK)
        e_win[...] = jnp.where((key // BLK == lane) | last, 1.0, 0.0).astype(e_win.dtype)
        key = lax.broadcasted_iota(jnp.int32, e_pool.shape, 0)
        lane = lax.broadcasted_iota(jnp.int32, e_pool.shape, 1)
        e_pool[...] = jnp.where(key // BLK == lane, 1.0, 0.0).astype(e_pool.dtype)

    here = ids_ref[step]
    q = q_ref[...]
    q = jnp.concatenate([q[:, h * HS : (h + 1) * HS] for h in range(heads)], axis=0)
    row = lax.broadcasted_iota(jnp.int32, (BLK, LANES), 0)
    lane = lax.broadcasted_iota(jnp.int32, (BLK, LANES), 1)
    above = jnp.where(lane - BLK > row, MASKED, 0.0).astype(jnp.float32)
    win_mask = win_ref[0][:, None, :] + above[None]
    win_mask = win_mask.reshape(heads * BLK, LANES).astype(q.dtype)
    pool_mask = jnp.broadcast_to(pool_ref[0][:, None, :], (heads, BLK, LANES))
    pool_mask = pool_mask.reshape(heads * BLK, LANES).astype(q.dtype)

    start = pl.multiple_of((here + 1) * BLK, BLK)
    keys = jnp.concatenate([k_win[pl.ds(start, SPAN * BLK), :], e_win[...]], axis=1)
    contract = (((1,), (1,)), ((), ()))
    near_scores = lax.dot_general(
        jnp.concatenate([q, win_mask], axis=1), keys, contract, preferred_element_type=jnp.float32
    )
    far_keys = jnp.concatenate([k_pool[...], e_pool[...]], axis=1)
    far_scores = lax.dot_general(
        jnp.concatenate([q, pool_mask], axis=1),
        far_keys,
        contract,
        preferred_element_type=jnp.float32,
    )
    top = jnp.maximum(
        jnp.max(near_scores, axis=1, keepdims=True), jnp.max(far_scores, axis=1, keepdims=True)
    )
    near_probs = jnp.exp2((near_scores - top) * EXP_SCALE).astype(q.dtype)
    far_probs = jnp.exp2((far_scores - top) * EXP_SCALE).astype(q.dtype)
    near_values = jnp.concatenate(
        [v_win[pl.ds(start, SPAN * BLK), :], jnp.ones((SPAN * BLK, LANES), q.dtype)], axis=1
    )
    far_values = jnp.concatenate(
        [v_pool[...], jnp.ones((v_pool.shape[0], LANES), q.dtype)], axis=1
    )
    summed = jnp.dot(near_probs, near_values, preferred_element_type=jnp.float32)
    summed = summed + jnp.dot(far_probs, far_values, preferred_element_type=jnp.float32)
    out = (summed[:, :HS] / summed[:, HS:]).astype(q.dtype)
    out_rows = pl.ds(pl.multiple_of(step * BLK, BLK), BLK)
    for h in range(heads):
        attended[out_rows, h * HS : (h + 1) * HS] = out[h * BLK : (h + 1) * BLK]

    @pl.when(step == pl.num_programs(0) - 1)
    def _():
        half = outs[0].shape[0]
        if with_rows:
            outs[-1][...] = attended[...]
        for t in range(tiles):
            fetch(t).wait()
            product = jnp.dot(attended[...], weight[t], preferred_element_type=jnp.float32)
            product = product.astype(q.dtype)
            outs[t][...] = product[:half]
            outs[tiles + t][...] = product[half:]


def attend(ids, queries, win, pool, near_kv, pairs, out_weight, tiles, with_rows, after):
    steps = ids.shape[0]
    width = queries.shape[1]
    heads = win.shape[1]
    near, pools = len(near_kv) // 2, len(pairs)
    rows = near_kv[0].shape[0]
    dtype = queries.dtype
    far = pools * VMOST * BLK

    def whole(shape):
        return pl.BlockSpec(shape, lambda g, ids: (0,) * len(shape))

    table = pl.BlockSpec((1, heads, LANES), lambda g, ids: (ids[g], 0, 0))
    out_shapes = [(steps * BLK // 2, TILE)] * (2 * tiles)
    if with_rows:
        out_shapes.append((steps * BLK, width))
    return pl.pallas_call(
        functools.partial(attend_kernel, near, pools, with_rows),
        out_shape=[jax.ShapeDtypeStruct(shape, dtype) for shape in out_shapes],
        grid_spec=pltpu.PrefetchScalarGridSpec(
            num_scalar_prefetch=1,
            grid=(steps,),
            in_specs=[pl.BlockSpec((BLK, width), lambda g, ids: (ids[g], 0)), table, table]
            + [whole(x.shape) for x in [*near_kv, *pairs]]
            + [anywhere() for _ in range(1 + len(after))],
            out_specs=[whole(shape) for shape in out_shapes],
            scratch_shapes=[
                pltpu.VMEM((near * rows, HS), dtype),
                pltpu.VMEM((near * rows, HS), dtype),
                pltpu.VMEM((SPAN * BLK, LANES), dtype),
                pltpu.VMEM((far, HS), dtype),
                pltpu.VMEM((far, HS), dtype),
                pltpu.VMEM((far, LANES), dtype),
                pltpu.VMEM((steps * BLK, width), dtype),
                pltpu.VMEM((tiles, out_weight.shape[0], TILE), dtype),
                pltpu.SemaphoreType.DMA((tiles,)),
            ],
        ),
        compiler_params=params(58),
        cost_estimate=SHORT,
        name="attend",
    )(ids, queries, win, pool, *near_kv, *pairs, out_weight, *after)


def project_kernel(a_ref, *refs):
    send_ref, keep_ref = refs[-2:]
    half = send_ref.shape[0]
    product = None
    for part in range(WEIGHT_PARTS):
        w = refs[part][...]
        depth = w.shape[0]
        term = jnp.dot(
            a_ref[:, part * depth : (part + 1) * depth], w, preferred_element_type=jnp.float32
        )
        product = term if product is None else product + term
    product = product.astype(send_ref.dtype)
    send_ref[...] = product[:half]
    keep_ref[...] = product[half:]


def project(attended, out_weight, tile, after):
    rows, depth = attended.shape
    half = jax.ShapeDtypeStruct((rows // 2, TILE), attended.dtype)

    def weight(part):
        return pl.BlockSpec((depth // WEIGHT_PARTS, TILE), lambda g: (part, tile))

    return pl.pallas_call(
        project_kernel,
        out_shape=(half, half),
        grid=(1,),
        in_specs=[pl.BlockSpec((rows, depth), lambda g: (0, 0))]
        + [weight(part) for part in range(WEIGHT_PARTS)]
        + [anywhere() for _ in after],
        out_specs=(vmem(), vmem()),
        compiler_params=params(50),
        cost_estimate=SHORT,
        name="project",
    )(attended, *[out_weight] * WEIGHT_PARTS, *after)


def add_kernel(*refs):
    out_ref = refs[-1]
    tiles = len(refs) // 2
    for t in range(tiles):
        total = refs[t][...].astype(jnp.float32) + refs[tiles + t][...].astype(jnp.float32)
        out_ref[:, t * TILE : (t + 1) * TILE] = total.astype(out_ref.dtype)


def add(keep, got):
    rows = keep[0].shape[0]
    return pl.pallas_call(
        add_kernel,
        out_shape=jax.ShapeDtypeStruct((rows, len(keep) * TILE), keep[0].dtype),
        in_specs=[vmem()] * (2 * len(keep)),
        out_specs=vmem(),
        compiler_params=params(50),
        cost_estimate=SHORT,
        name="add",
    )(*keep, *got)


def finish_kernel(tiles, *refs):
    arrived_ref, out_ref = refs[2 * tiles], refs[-1]
    for t in range(tiles):
        at = slice(t * TILE, (t + 1) * TILE)
        total = refs[t][...].astype(jnp.float32) + refs[tiles + t][...].astype(jnp.float32)
        out_ref[:, at] = (total + arrived_ref[:, at].astype(jnp.float32)).astype(out_ref.dtype)


def finish(keep, got, arrived, place, width, out):
    rows, columns = arrived.shape
    before = [] if out is None else [out]
    return pl.pallas_call(
        functools.partial(finish_kernel, len(keep)),
        out_shape=jax.ShapeDtypeStruct((rows, width), arrived.dtype),
        grid=(1,),
        in_specs=[vmem()] * (2 * len(keep) + 1) + [anywhere() for _ in before],
        out_specs=pl.BlockSpec((rows, columns), lambda g: (0, place)),
        input_output_aliases={2 * len(keep) + 1: 0} if before else {},
        compiler_params=params(50),
        cost_estimate=SHORT,
        name="finish",
    )(*keep, *got, arrived, *before)


def shards(ctx_size, queries, keys, values, out_weight, vertical, slash):
    local_blocks = queries.shape[0] // BLK
    near = 1 + -(-(SPAN - 1) // local_blocks)
    assert near == 3 and ctx_size % 2 == 0
    ctx_rank = lax.axis_index("ctx")
    tp_rank = lax.axis_index("tp")
    rank = jnp.reshape(ctx_rank, (1,)).astype(jnp.int32)
    odd = ctx_rank % 2 == 1

    def shifted(x, by):
        return lax.ppermute(x, "ctx", [(r, r + by) for r in range(ctx_size - by)])

    def swapped(x):
        return lax.ppermute(x, "ctx", [(r, r ^ 1) for r in range(ctx_size)])

    keys_2, values_2 = shifted(keys, 2), shifted(values, 2)
    keys_1 = swapped(jnp.where(odd, keys_2, keys))
    values_1 = swapped(jnp.where(odd, values_2, values))
    near_kv = [keys_2, values_2, keys_1, values_1, keys, values]
    own = pick(rank, vertical, keys, values, keys_2)
    pairs = [pick(rank - 2, vertical, keys_2, values_2, own)]
    pairs += [shifted(own, s) for s in range(near, ctx_size)]
    win, pool = masks(rank, vertical, slash, local_blocks, near)

    quarter = local_blocks // 4
    inner = jnp.arange(quarter, dtype=jnp.int32)

    def blocks_of(first, second):
        return jnp.concatenate([first * quarter + inner, second * quarter + inner])

    def sibling(x):
        return lax.ppermute(x, "tp", [(j, j ^ 1) for j in range(4)])

    def across(x):
        return lax.ppermute(x, "tp", [(j, j ^ 2) for j in range(4)])

    def attention(first, second, tiles, with_rows, after):
        ids = blocks_of(first, second)
        return attend(ids, queries, win, pool, near_kv, pairs, out_weight, tiles, with_rows, after)

    width = out_weight.shape[1]
    tiles = width // TILE
    head = ACROSS[0][1]
    assert ACROSS[0][0] == 0 and sum(count for _, count in ACROSS) == tiles
    *parts, attended = attention(tp_rank ^ 3, tp_rank ^ 2, head, True, ())
    keep = parts[head:]
    total = add(keep, [sibling(x) for x in parts[:head]])
    arrived = [across(total)]
    after = (total,)
    for first, count in ACROSS[1:]:
        keep, got = [], []
        for t in range(first, first + count):
            send, mine = project(attended, out_weight, t, after)
            keep.append(mine)
            got.append(sibling(send))
        total = add(keep, got)
        arrived.append(across(total))
        after = (total, arrived[0])
    parts = attention(tp_rank ^ 1, tp_rank, tiles, False, (total,))
    keep = parts[tiles:]
    got = [sibling(x) for x in parts[:tiles]]
    out = None
    for part, (first, count) in zip(arrived, ACROSS):
        assert first % count == 0
        at = slice(first, first + count)
        out = finish(keep[at], got[at], part, first // count, width, out)
    return out


def solution(mesh):
    assert mesh.shape["tp"] == 4
    return jax.shard_map(
        functools.partial(shards, mesh.shape["ctx"]),
        mesh=mesh,
        in_specs=(
            P("ctx", "tp"),
            P("ctx", "tp"),
            P("ctx", "tp"),
            P("tp", None),
            P("tp", None),
            P("tp", None),
        ),
        out_specs=P(("ctx", "tp"), None),
        check_vma=False,
    )
```

```python
import functools

import jax
import jax.numpy as jnp
from jax import lax
from jax.experimental import pallas as pl
from jax.experimental.pallas import tpu as pltpu
from jax.sharding import PartitionSpec as P

HS = 128
BLK = 64
SPAN = 16
VMOST = 2
LANES = 128
MASKED = -1e30
EXP_SCALE = 1.4426950408889634 / (HS**0.5)
TILE = 1024
ACROSS = ((0, 2), (4, 4), (2, 2))
MIB = 1024 * 1024


SHORT = pl.CostEstimate(flops=0, bytes_accessed=0, transcendentals=0)


def vmem():
    return pl.BlockSpec(memory_space=pltpu.VMEM)


def smem():
    return pl.BlockSpec(memory_space=pltpu.SMEM)


def anywhere():
    return pl.BlockSpec(memory_space=pl.ANY)


def params(mib):
    return pltpu.CompilerParams(vmem_limit_bytes=mib * MIB)


def picked_blocks(vertical, shard, local_blocks):
    block = vertical - shard * local_blocks
    block = jnp.where((block >= 0) & (block < local_blocks), block, local_blocks)
    first = jnp.min(block)
    second = jnp.min(jnp.where(block > first, block, local_blocks))
    return [
        pl.ds(pl.multiple_of(jnp.minimum(x, local_blocks - 1) * BLK, BLK), BLK)
        for x in (first, second)
    ]


def pick_kernel(rank_ref, vert_ref, k_ref, v_ref, both_ref, pair_ref):
    both_ref[:, :HS] = k_ref[...]
    both_ref[:, HS:] = v_ref[...]
    blocks = picked_blocks(vert_ref[...], rank_ref[0], k_ref.shape[0] // BLK)
    for slot, rows in enumerate(blocks):
        pair_ref[slot * BLK : (slot + 1) * BLK, :] = both_ref[rows, :]


def pick(rank, vertical, keys, values):
    return pl.pallas_call(
        pick_kernel,
        out_shape=(
            jax.ShapeDtypeStruct((keys.shape[0], 2 * HS), keys.dtype),
            jax.ShapeDtypeStruct((VMOST * BLK, 2 * HS), keys.dtype),
        ),
        in_specs=[smem(), vmem(), vmem(), vmem()],
        out_specs=(vmem(), vmem()),
        compiler_params=params(60),
        name="pick",
    )(rank, vertical, keys, values)


def mask_kernel(local_blocks, near, rank_ref, vert_ref, slash_ref, win_ref, pool_ref):
    heads, vert_count = vert_ref.shape
    slash_count = slash_ref.shape[1]
    rank = rank_ref[0]
    lane = lax.broadcasted_iota(jnp.int32, (heads, LANES), 1)
    vert = [vert_ref[:, s : s + 1] for s in range(vert_count)]
    zero = jnp.zeros((heads, LANES), jnp.float32)

    def member(columns, blocks):
        found = columns[0] == blocks
        for column in columns[1:]:
            found = found | (column == blocks)
        return found

    offset_ok = member([slash_ref[:, s : s + 1] for s in range(slash_count)], SPAN - 1 - lane)
    shard = rank - (near - 1) - lane // VMOST
    first = jnp.full((1, LANES), local_blocks, jnp.int32)
    second = first
    for j in reversed(range(local_blocks)):
        here = member(vert, shard * local_blocks + j)
        here = jnp.max(jnp.where(here, 1, 0), axis=0, keepdims=True) == 1
        second = jnp.where(here, first, second)
        first = jnp.where(here, j, first)
    picked = jnp.where(lane % VMOST == 0, first, second)
    block = shard * local_blocks + picked
    pool_ok = (picked < local_blocks) & (shard >= 0) & member(vert, block)
    for i in range(local_blocks):
        row = rank * local_blocks + i
        seen = row - (SPAN - 1) + lane
        ok = (seen >= 0) & (offset_ok | member(vert, seen))
        win_ref[i] = jnp.where(ok | (lane >= SPAN), zero, MASKED)
        pool_ref[i] = jnp.where(pool_ok & (block < row - (SPAN - 1)), zero, MASKED)


def masks(rank, vertical, slash, local_blocks, near):
    heads = vertical.shape[0]
    shape = jax.ShapeDtypeStruct((local_blocks, heads, LANES), jnp.float32)
    return pl.pallas_call(
        functools.partial(mask_kernel, local_blocks, near),
        out_shape=(shape, shape),
        in_specs=[smem(), vmem(), vmem()],
        out_specs=(vmem(), vmem()),
        compiler_params=params(60),
        name="masks",
    )(rank, vertical, slash)


def attend_kernel(
    near, pools, with_rows, here_of, tp_ref, ctx_ref, q_ref, win_ref, pool_ref, vert_ref, *refs
):
    kv_refs = refs[:near]
    pair_refs = refs[near : near + pools - 1]
    w_hbm = refs[near + pools - 1]
    k_win, v_win, e_win, k_pool, v_pool, e_pool, attended, weight, arrival = refs[-9:]
    step = pl.program_id(0)
    heads = win_ref.shape[1]
    rows = kv_refs[0].shape[0]
    tiles, _, tile = weight.shape
    outs = refs[-9 - 2 * tiles - with_rows : -9]

    def fetch(t):
        return pltpu.make_async_copy(
            w_hbm.at[:, pl.ds(t * tile, tile)], weight.at[t], arrival.at[t]
        )

    @pl.when(step == 0)
    def _():
        for t in range(tiles):
            fetch(t).start()
        for s in range(near):
            k_win[s * rows : (s + 1) * rows, :] = kv_refs[s][:, :HS]
            v_win[s * rows : (s + 1) * rows, :] = kv_refs[s][:, HS:]
        blocks = picked_blocks(vert_ref[...], ctx_ref[0] - (near - 1), rows // BLK)
        for slot, block in enumerate(blocks):
            k_pool[slot * BLK : (slot + 1) * BLK, :] = kv_refs[0][block, :HS]
            v_pool[slot * BLK : (slot + 1) * BLK, :] = kv_refs[0][block, HS:]
        for s in range(1, pools):
            at = slice(s * VMOST * BLK, (s + 1) * VMOST * BLK)
            k_pool[at, :] = pair_refs[s - 1][:, :HS]
            v_pool[at, :] = pair_refs[s - 1][:, HS:]
        key = lax.broadcasted_iota(jnp.int32, e_win.shape, 0)
        lane = lax.broadcasted_iota(jnp.int32, e_win.shape, 1)
        last = (key // BLK == SPAN - 1) & (key % BLK == lane - BLK)
        e_win[...] = jnp.where((key // BLK == lane) | last, 1.0, 0.0).astype(e_win.dtype)
        key = lax.broadcasted_iota(jnp.int32, e_pool.shape, 0)
        lane = lax.broadcasted_iota(jnp.int32, e_pool.shape, 1)
        e_pool[...] = jnp.where(key // BLK == lane, 1.0, 0.0).astype(e_pool.dtype)

    here = here_of(step, tp_ref)
    q = q_ref[...]
    q = jnp.concatenate([q[:, h * HS : (h + 1) * HS] for h in range(heads)], axis=0)
    row = lax.broadcasted_iota(jnp.int32, (BLK, LANES), 0)
    lane = lax.broadcasted_iota(jnp.int32, (BLK, LANES), 1)
    above = jnp.where(lane - BLK > row, MASKED, 0.0).astype(jnp.float32)
    win_mask = win_ref[0][:, None, :] + above[None]
    win_mask = win_mask.reshape(heads * BLK, LANES).astype(q.dtype)
    pool_mask = jnp.broadcast_to(pool_ref[0][:, None, :], (heads, BLK, LANES))
    pool_mask = pool_mask.reshape(heads * BLK, LANES).astype(q.dtype)

    start = pl.multiple_of((here + 1) * BLK, BLK)
    keys = jnp.concatenate([k_win[pl.ds(start, SPAN * BLK), :], e_win[...]], axis=1)
    contract = (((1,), (1,)), ((), ()))
    near_scores = lax.dot_general(
        jnp.concatenate([q, win_mask], axis=1), keys, contract, preferred_element_type=jnp.float32
    )
    far_keys = jnp.concatenate([k_pool[...], e_pool[...]], axis=1)
    far_scores = lax.dot_general(
        jnp.concatenate([q, pool_mask], axis=1),
        far_keys,
        contract,
        preferred_element_type=jnp.float32,
    )
    top = jnp.maximum(
        jnp.max(near_scores, axis=1, keepdims=True), jnp.max(far_scores, axis=1, keepdims=True)
    )
    near_probs = jnp.exp2((near_scores - top) * EXP_SCALE).astype(q.dtype)
    far_probs = jnp.exp2((far_scores - top) * EXP_SCALE).astype(q.dtype)
    near_values = jnp.concatenate(
        [v_win[pl.ds(start, SPAN * BLK), :], jnp.ones((SPAN * BLK, LANES), q.dtype)], axis=1
    )
    far_values = jnp.concatenate(
        [v_pool[...], jnp.ones((v_pool.shape[0], LANES), q.dtype)], axis=1
    )
    summed = jnp.dot(near_probs, near_values, preferred_element_type=jnp.float32)
    summed = summed + jnp.dot(far_probs, far_values, preferred_element_type=jnp.float32)
    out = (summed[:, :HS] / summed[:, HS:]).astype(q.dtype)
    out_rows = pl.ds(pl.multiple_of(step * BLK, BLK), BLK)
    for h in range(heads):
        attended[out_rows, h * HS : (h + 1) * HS] = out[h * BLK : (h + 1) * BLK]

    @pl.when(step == pl.num_programs(0) - 1)
    def _():
        half = outs[0].shape[0]
        if with_rows:
            outs[-1][...] = attended[...]
        for t in range(tiles):
            fetch(t).wait()
            product = jnp.dot(attended[...], weight[t], preferred_element_type=jnp.float32)
            product = product.astype(q.dtype)
            outs[t][...] = product[:half]
            outs[tiles + t][...] = product[half:]


def attend(flips, tp, ctx, queries, win, pool, vertical, near_kv, pairs, out_weight, tiles, with_rows, after):
    width = queries.shape[1]
    local_blocks, heads, _ = win.shape
    quarter = local_blocks // 4
    steps = len(flips) * quarter
    near, pools = len(near_kv), len(pairs) + 1
    rows = near_kv[0].shape[0]
    dtype = queries.dtype
    far = pools * VMOST * BLK

    def here_of(step, tp_ref):
        owner = tp_ref[0] ^ jnp.where(step < quarter, flips[0], flips[1])
        return owner * quarter + step % quarter

    def whole(shape):
        return pl.BlockSpec(shape, lambda g, tp, ctx: (0,) * len(shape))

    table = pl.BlockSpec((1, heads, LANES), lambda g, tp, ctx: (here_of(g, tp), 0, 0))
    out_shapes = [(steps * BLK // 2, TILE)] * (2 * tiles)
    if with_rows:
        out_shapes.append((steps * BLK, width))
    return pl.pallas_call(
        functools.partial(attend_kernel, near, pools, with_rows, here_of),
        out_shape=[jax.ShapeDtypeStruct(shape, dtype) for shape in out_shapes],
        grid_spec=pltpu.PrefetchScalarGridSpec(
            num_scalar_prefetch=2,
            grid=(steps,),
            in_specs=[pl.BlockSpec((BLK, width), lambda g, tp, ctx: (here_of(g, tp), 0))]
            + [table, table]
            + [whole(x.shape) for x in [vertical, *near_kv, *pairs]]
            + [anywhere() for _ in range(1 + len(after))],
            out_specs=[whole(shape) for shape in out_shapes],
            scratch_shapes=[
                pltpu.VMEM((near * rows, HS), dtype),
                pltpu.VMEM((near * rows, HS), dtype),
                pltpu.VMEM((SPAN * BLK, LANES), dtype),
                pltpu.VMEM((far, HS), dtype),
                pltpu.VMEM((far, HS), dtype),
                pltpu.VMEM((far, LANES), dtype),
                pltpu.VMEM((steps * BLK, width), dtype),
                pltpu.VMEM((tiles, out_weight.shape[0], TILE), dtype),
                pltpu.SemaphoreType.DMA((tiles,)),
            ],
        ),
        compiler_params=params(60),
        cost_estimate=SHORT,
        name="attend",
    )(tp, ctx, queries, win, pool, vertical, *near_kv, *pairs, out_weight, *after)


def project_kernel(first, a_ref, w_hbm, *refs):
    weight, arrival = refs[-2:]
    tiles, _, tile = weight.shape
    outs = refs[-2 - 2 * tiles : -2]
    half = outs[0].shape[0]

    def fetch(t):
        return pltpu.make_async_copy(
            w_hbm.at[:, pl.ds((first + t) * tile, tile)], weight.at[t], arrival.at[t]
        )

    for t in range(tiles):
        fetch(t).start()
    for t in range(tiles):
        fetch(t).wait()
        product = jnp.dot(a_ref[...], weight[t], preferred_element_type=jnp.float32)
        product = product.astype(a_ref.dtype)
        outs[t][...] = product[:half]
        outs[tiles + t][...] = product[half:]


def project(attended, out_weight, first, tiles, after):
    rows, depth = attended.shape
    half = jax.ShapeDtypeStruct((rows // 2, TILE), attended.dtype)
    return pl.pallas_call(
        functools.partial(project_kernel, first),
        out_shape=[half] * (2 * tiles),
        in_specs=[vmem(), anywhere()] + [anywhere() for _ in after],
        out_specs=[vmem()] * (2 * tiles),
        scratch_shapes=[
            pltpu.VMEM((tiles, depth, TILE), attended.dtype),
            pltpu.SemaphoreType.DMA((tiles,)),
        ],
        compiler_params=params(60),
        cost_estimate=SHORT,
        name="project",
    )(attended, out_weight, *after)


def add_kernel(*refs):
    out_ref = refs[-1]
    tiles = len(refs) // 2
    for t in range(tiles):
        total = refs[t][...].astype(jnp.float32) + refs[tiles + t][...].astype(jnp.float32)
        out_ref[:, t * TILE : (t + 1) * TILE] = total.astype(out_ref.dtype)


def add(keep, got):
    rows = keep[0].shape[0]
    return pl.pallas_call(
        add_kernel,
        out_shape=jax.ShapeDtypeStruct((rows, len(keep) * TILE), keep[0].dtype),
        in_specs=[vmem()] * (2 * len(keep)),
        out_specs=vmem(),
        compiler_params=params(60),
        cost_estimate=SHORT,
        name="add",
    )(*keep, *got)


def finish_kernel(tiles, *refs):
    arrived_ref, out_ref = refs[2 * tiles], refs[-1]
    for t in range(tiles):
        at = slice(t * TILE, (t + 1) * TILE)
        total = refs[t][...].astype(jnp.float32) + refs[tiles + t][...].astype(jnp.float32)
        out_ref[:, at] = (total + arrived_ref[:, at].astype(jnp.float32)).astype(out_ref.dtype)


def finish(keep, got, arrived, place, width, out):
    rows, columns = arrived.shape
    before = [] if out is None else [out]
    return pl.pallas_call(
        functools.partial(finish_kernel, len(keep)),
        out_shape=jax.ShapeDtypeStruct((rows, width), arrived.dtype),
        grid=(1,),
        in_specs=[vmem()] * (2 * len(keep) + 1) + [anywhere() for _ in before],
        out_specs=pl.BlockSpec((rows, columns), lambda g: (0, place)),
        input_output_aliases={2 * len(keep) + 1: 0} if before else {},
        compiler_params=params(16),
        cost_estimate=SHORT,
        name="finish",
    )(*keep, *got, arrived, *before)


def shards(ctx_size, queries, keys, values, out_weight, vertical, slash):
    local_blocks = queries.shape[0] // BLK
    near = 1 + -(-(SPAN - 1) // local_blocks)
    ctx = jnp.reshape(lax.axis_index("ctx"), (1,)).astype(jnp.int32)
    tp = jnp.reshape(lax.axis_index("tp"), (1,)).astype(jnp.int32)

    def shifted(x, by):
        return lax.ppermute(x, "ctx", [(r, r + by) for r in range(ctx_size - by)])

    own, pair = pick(ctx, vertical, keys, values)
    near_kv = [shifted(own, s) for s in range(near - 1, 0, -1)] + [own]
    pairs = [shifted(pair, s) for s in range(near, ctx_size)]
    win, pool = masks(ctx, vertical, slash, local_blocks, near)

    def sibling(x):
        return lax.ppermute(x, "tp", [(j, j ^ 1) for j in range(4)])

    def across(x):
        return lax.ppermute(x, "tp", [(j, j ^ 2) for j in range(4)])

    def attention(flips, tiles, with_rows, after):
        return attend(
            flips, tp, ctx, queries, win, pool, vertical, near_kv, pairs, out_weight, tiles, with_rows, after
        )

    width = out_weight.shape[1]
    tiles = width // TILE
    head = ACROSS[0][1]
    assert ACROSS[0][0] == 0 and sum(count for _, count in ACROSS) == tiles
    *parts, attended = attention((3, 2), head, True, ())
    keep = parts[head:]
    got = [sibling(x) for x in parts[:head]]
    total = add(keep, got)
    arrived = [across(total)]
    rest = tiles - head
    parts = project(attended, out_weight, head, rest, (total,))
    keep += parts[rest:]
    got += [sibling(x) for x in parts[:rest]]
    for first, count in ACROSS[1:]:
        total = add(keep[first : first + count], got[first : first + count])
        arrived.append(across(total))
    parts = attention((1, 0), tiles, False, (total, arrived[0]))
    keep = parts[tiles:]
    got = [sibling(x) for x in parts[:tiles]]
    out = None
    for part, (first, count) in zip(arrived, ACROSS):
        assert first % count == 0
        at = slice(first, first + count)
        out = finish(keep[at], got[at], part, first // count, width, out)
    return out


def solution(mesh):
    assert mesh.shape["tp"] == 4
    return jax.shard_map(
        functools.partial(shards, mesh.shape["ctx"]),
        mesh=mesh,
        in_specs=(
            P("ctx", "tp"),
            P("ctx", "tp"),
            P("ctx", "tp"),
            P("tp", None),
            P("tp", None),
            P("tp", None),
        ),
        out_specs=P(("ctx", "tp"), None),
        check_vma=False,
    )
```

```python
import functools

import jax
import jax.numpy as jnp
from jax import lax
from jax.experimental import pallas as pl
from jax.experimental.pallas import tpu as pltpu
from jax.sharding import PartitionSpec as P

HS = 128
BLK = 64
SPAN = 16
VMOST = 2
NEAR = 3
LANES = 128
MASKED = -1e30
EXP_SCALE = 1.4426950408889634 / (HS**0.5)
TILE = 1024
PIECE = 2
ACROSS = 4
MIB = 1024 * 1024


SHORT = pl.CostEstimate(flops=0, bytes_accessed=0, transcendentals=0)


def vmem():
    return pl.BlockSpec(memory_space=pltpu.VMEM)


def smem():
    return pl.BlockSpec(memory_space=pltpu.SMEM)


def anywhere():
    return pl.BlockSpec(memory_space=pl.ANY)


def params(mib):
    return pltpu.CompilerParams(vmem_limit_bytes=mib * MIB)


def picked_blocks(vertical, shard, local_blocks):
    block = vertical - shard * local_blocks
    block = jnp.where((block >= 0) & (block < local_blocks), block, local_blocks)
    first = jnp.min(block)
    second = jnp.min(jnp.where(block > first, block, local_blocks))
    return [
        pl.ds(pl.multiple_of(jnp.minimum(x, local_blocks - 1) * BLK, BLK), BLK)
        for x in (first, second)
    ]


def pick_kernel(rank_ref, vert_ref, k_ref, v_ref, both_ref, pair_ref):
    both_ref[:, :HS] = k_ref[...]
    both_ref[:, HS:] = v_ref[...]
    blocks = picked_blocks(vert_ref[...], rank_ref[0], k_ref.shape[0] // BLK)
    for slot, rows in enumerate(blocks):
        pair_ref[slot * BLK : (slot + 1) * BLK, :] = both_ref[rows, :]


def pick(rank, vertical, keys, values):
    return pl.pallas_call(
        pick_kernel,
        out_shape=(
            jax.ShapeDtypeStruct((keys.shape[0], 2 * HS), keys.dtype),
            jax.ShapeDtypeStruct((VMOST * BLK, 2 * HS), keys.dtype),
        ),
        in_specs=[smem(), vmem(), vmem(), vmem()],
        out_specs=(vmem(), vmem()),
        compiler_params=params(60),
        name="pick",
    )(rank, vertical, keys, values)


def mask_kernel(local_blocks, slots, rank_ref, vert_ref, slash_ref, win_ref, pool_ref):
    heads, vert_count = vert_ref.shape
    slash_count = slash_ref.shape[1]
    rank = rank_ref[0]
    lane = lax.broadcasted_iota(jnp.int32, (heads, LANES), 1)
    vert = [vert_ref[:, s : s + 1] for s in range(vert_count)]
    zero = jnp.zeros((heads, LANES), jnp.float32)

    def member(columns, blocks):
        found = columns[0] == blocks
        for column in columns[1:]:
            found = found | (column == blocks)
        return found

    offset_ok = member([slash_ref[:, s : s + 1] for s in range(slash_count)], SPAN - 1 - lane)
    shard = jnp.full((heads, LANES), -1, jnp.int32)
    for slot, (back, back_odd) in enumerate(slots):
        shard = jnp.where(lane // VMOST == slot, rank - back - back_odd * (rank & 1), shard)
    first = jnp.full((1, LANES), local_blocks, jnp.int32)
    second = first
    for j in reversed(range(local_blocks)):
        here = member(vert, shard * local_blocks + j)
        here = jnp.max(jnp.where(here, 1, 0), axis=0, keepdims=True) == 1
        second = jnp.where(here, first, second)
        first = jnp.where(here, j, first)
    picked = jnp.where(lane % VMOST == 0, first, second)
    block = shard * local_blocks + picked
    pool_ok = (picked < local_blocks) & (shard >= 0) & member(vert, block)
    for i in range(local_blocks):
        row = rank * local_blocks + i
        seen = row - (SPAN - 1) + lane
        ok = (seen >= 0) & (offset_ok | member(vert, seen))
        win_ref[i] = jnp.where(ok | (lane >= SPAN), zero, MASKED)
        pool_ref[i] = jnp.where(pool_ok & (block < row - (SPAN - 1)), zero, MASKED)


def masks(rank, vertical, slash, local_blocks, slots):
    heads = vertical.shape[0]
    shape = jax.ShapeDtypeStruct((local_blocks, heads, LANES), jnp.float32)
    return pl.pallas_call(
        functools.partial(mask_kernel, local_blocks, slots),
        out_shape=(shape, shape),
        in_specs=[smem(), vmem(), vmem()],
        out_specs=(vmem(), vmem()),
        compiler_params=params(60),
        name="masks",
    )(rank, vertical, slash)


def attend_kernel(
    pools, tiles, here_of, tp_ref, ctx_ref, q_ref, win_ref, pool_ref, vert_ref, *refs
):
    own_kv, kv_2, kv_even, kv_back = refs[:4]
    pair_refs = refs[4 : 4 + pools - 2]
    w_hbm = refs[4 + pools - 2]
    k_win, v_win, e_win, k_pool, v_pool, e_pool, attended = refs[-9:-2]
    weight, arrival = refs[-2:]
    outs = refs[-12:-9] if tiles else refs[-10:-9]
    step = pl.program_id(0)
    heads = win_ref.shape[1]
    rows = own_kv.shape[0]

    def fetch(t):
        return pltpu.make_async_copy(
            w_hbm.at[:, pl.ds(t * TILE, TILE)], weight.at[t], arrival.at[t]
        )

    @pl.when(step == 0)
    def _():
        for t in range(tiles):
            fetch(t).start()
        odd = (ctx_ref[0] & 1) == 1

        def place(s, ref):
            k_win[s * rows : (s + 1) * rows, :] = ref[:, :HS]
            v_win[s * rows : (s + 1) * rows, :] = ref[:, HS:]

        place(0, kv_2)
        place(2, own_kv)

        @pl.when(odd)
        def _():
            place(1, kv_even)

        @pl.when(jnp.logical_not(odd))
        def _():
            place(1, kv_back)

        for s, (ref, back) in enumerate(((kv_2, 2), (kv_back, jnp.where(odd, 3, 1)))):
            blocks = picked_blocks(vert_ref[...], ctx_ref[0] - back, rows // BLK)
            for slot, block in enumerate(blocks):
                at = pl.ds((s * VMOST + slot) * BLK, BLK)
                k_pool[at, :] = ref[block, :HS]
                v_pool[at, :] = ref[block, HS:]
        for s in range(2, pools):
            at = slice(s * VMOST * BLK, (s + 1) * VMOST * BLK)
            k_pool[at, :] = pair_refs[s - 2][:, :HS]
            v_pool[at, :] = pair_refs[s - 2][:, HS:]
        key = lax.broadcasted_iota(jnp.int32, e_win.shape, 0)
        lane = lax.broadcasted_iota(jnp.int32, e_win.shape, 1)
        last = (key // BLK == SPAN - 1) & (key % BLK == lane - BLK)
        e_win[...] = jnp.where((key // BLK == lane) | last, 1.0, 0.0).astype(e_win.dtype)
        key = lax.broadcasted_iota(jnp.int32, e_pool.shape, 0)
        lane = lax.broadcasted_iota(jnp.int32, e_pool.shape, 1)
        e_pool[...] = jnp.where(key // BLK == lane, 1.0, 0.0).astype(e_pool.dtype)

    here = here_of(step, tp_ref)
    q = q_ref[...]
    q = jnp.concatenate([q[:, h * HS : (h + 1) * HS] for h in range(heads)], axis=0)
    row = lax.broadcasted_iota(jnp.int32, (BLK, LANES), 0)
    lane = lax.broadcasted_iota(jnp.int32, (BLK, LANES), 1)
    above = jnp.where(lane - BLK > row, MASKED, 0.0).astype(jnp.float32)
    win_mask = win_ref[0][:, None, :] + above[None]
    win_mask = win_mask.reshape(heads * BLK, LANES).astype(q.dtype)
    pool_mask = jnp.broadcast_to(pool_ref[0][:, None, :], (heads, BLK, LANES))
    pool_mask = pool_mask.reshape(heads * BLK, LANES).astype(q.dtype)

    start = pl.multiple_of((here + 1) * BLK, BLK)
    keys = jnp.concatenate([k_win[pl.ds(start, SPAN * BLK), :], e_win[...]], axis=1)
    contract = (((1,), (1,)), ((), ()))
    near_scores = lax.dot_general(
        jnp.concatenate([q, win_mask], axis=1), keys, contract, preferred_element_type=jnp.float32
    )
    far_keys = jnp.concatenate([k_pool[...], e_pool[...]], axis=1)
    far_scores = lax.dot_general(
        jnp.concatenate([q, pool_mask], axis=1),
        far_keys,
        contract,
        preferred_element_type=jnp.float32,
    )
    top = jnp.maximum(
        jnp.max(near_scores, axis=1, keepdims=True), jnp.max(far_scores, axis=1, keepdims=True)
    )
    near_probs = jnp.exp2((near_scores - top) * EXP_SCALE).astype(q.dtype)
    far_probs = jnp.exp2((far_scores - top) * EXP_SCALE).astype(q.dtype)
    near_values = jnp.concatenate(
        [v_win[pl.ds(start, SPAN * BLK), :], jnp.ones((SPAN * BLK, LANES), q.dtype)], axis=1
    )
    far_values = jnp.concatenate(
        [v_pool[...], jnp.ones((v_pool.shape[0], LANES), q.dtype)], axis=1
    )
    summed = jnp.dot(near_probs, near_values, preferred_element_type=jnp.float32)
    summed = summed + jnp.dot(far_probs, far_values, preferred_element_type=jnp.float32)
    out = (summed[:, :HS] / summed[:, HS:]).astype(q.dtype)
    out_rows = pl.ds(pl.multiple_of(step * BLK, BLK), BLK)
    for h in range(heads):
        attended[out_rows, h * HS : (h + 1) * HS] = out[h * BLK : (h + 1) * BLK]

    @pl.when(step == pl.num_programs(0) - 1)
    def _():
        outs[-1][...] = attended[...]
        half = attended.shape[0] // 2
        for t in range(tiles):
            fetch(t).wait()
            product = jnp.dot(attended[...], weight[t], preferred_element_type=jnp.float32)
            product = product.astype(q.dtype)
            outs[0][:, t * TILE : (t + 1) * TILE] = product[:half]
            outs[1][:, t * TILE : (t + 1) * TILE] = product[half:]


def attend(flips, tp, ctx, queries, win, pool, vertical, near_kv, pairs, out_weight, tiles, after):
    width = queries.shape[1]
    local_blocks, heads, _ = win.shape
    quarter = local_blocks // 4
    steps = len(flips) * quarter
    pools = len(pairs) + 2
    rows = near_kv[0].shape[0]
    dtype = queries.dtype
    far = pools * VMOST * BLK

    def here_of(step, tp_ref):
        owner = tp_ref[0] ^ jnp.where(step < quarter, flips[0], flips[1])
        return owner * quarter + step % quarter

    def whole(shape):
        return pl.BlockSpec(shape, lambda g, tp, ctx: (0,) * len(shape))

    table = pl.BlockSpec((1, heads, LANES), lambda g, tp, ctx: (here_of(g, tp), 0, 0))
    out_shapes = [(steps * BLK // 2, tiles * TILE)] * 2 if tiles else []
    out_shapes.append((steps * BLK, width))
    return pl.pallas_call(
        functools.partial(attend_kernel, pools, tiles, here_of),
        out_shape=[jax.ShapeDtypeStruct(shape, dtype) for shape in out_shapes],
        grid_spec=pltpu.PrefetchScalarGridSpec(
            num_scalar_prefetch=2,
            grid=(steps,),
            in_specs=[pl.BlockSpec((BLK, width), lambda g, tp, ctx: (here_of(g, tp), 0))]
            + [table, table]
            + [whole(x.shape) for x in [vertical, *near_kv, *pairs]]
            + [anywhere() for _ in range(1 + len(after))],
            out_specs=[whole(shape) for shape in out_shapes],
            scratch_shapes=[
                pltpu.VMEM((NEAR * rows, HS), dtype),
                pltpu.VMEM((NEAR * rows, HS), dtype),
                pltpu.VMEM((SPAN * BLK, LANES), dtype),
                pltpu.VMEM((far, HS), dtype),
                pltpu.VMEM((far, HS), dtype),
                pltpu.VMEM((far, LANES), dtype),
                pltpu.VMEM((steps * BLK, width), dtype),
                pltpu.VMEM((max(tiles, 1), out_weight.shape[0], TILE), dtype),
                pltpu.SemaphoreType.DMA((max(tiles, 1),)),
            ],
        ),
        compiler_params=params(60),
        cost_estimate=SHORT,
        name="attend",
    )(tp, ctx, queries, win, pool, vertical, *near_kv, *pairs, out_weight, *after)


def project_kernel(first, a_ref, w_hbm, *refs):
    weight, arrival = refs[-2:]
    tiles = weight.shape[0]
    pieces = tiles // PIECE
    outs = refs[-2 - 2 * pieces : -2]
    half = outs[0].shape[0]

    def fetch(t):
        return pltpu.make_async_copy(
            w_hbm.at[:, pl.ds((first + t) * TILE, TILE)], weight.at[t], arrival.at[t]
        )

    for t in range(tiles):
        fetch(t).start()
    for t in range(tiles):
        fetch(t).wait()
        product = jnp.dot(a_ref[...], weight[t], preferred_element_type=jnp.float32)
        product = product.astype(a_ref.dtype)
        at = slice(t % PIECE * TILE, (t % PIECE + 1) * TILE)
        outs[t // PIECE][:, at] = product[:half]
        outs[pieces + t // PIECE][:, at] = product[half:]


def project(attended, out_weight, first, tiles, after):
    rows, depth = attended.shape
    pieces = tiles // PIECE
    part = jax.ShapeDtypeStruct((rows // 2, PIECE * TILE), attended.dtype)
    outs = pl.pallas_call(
        functools.partial(project_kernel, first),
        out_shape=[part] * (2 * pieces),
        in_specs=[vmem(), anywhere()] + [anywhere() for _ in after],
        out_specs=[vmem()] * (2 * pieces),
        scratch_shapes=[
            pltpu.VMEM((tiles, depth, TILE), attended.dtype),
            pltpu.SemaphoreType.DMA((tiles,)),
        ],
        compiler_params=params(60),
        cost_estimate=SHORT,
        name="project",
    )(attended, out_weight, *after)
    return outs[:pieces], outs[pieces:]


def add_kernel(*refs):
    out_ref = refs[-1]
    tiles = len(refs) // 2
    for t in range(tiles):
        total = refs[t][...].astype(jnp.float32) + refs[tiles + t][...].astype(jnp.float32)
        out_ref[:, t * PIECE * TILE : (t + 1) * PIECE * TILE] = total.astype(out_ref.dtype)


def add(keep, got):
    rows = keep[0].shape[0]
    return pl.pallas_call(
        add_kernel,
        out_shape=jax.ShapeDtypeStruct((rows, len(keep) * PIECE * TILE), keep[0].dtype),
        in_specs=[vmem()] * (2 * len(keep)),
        out_specs=vmem(),
        compiler_params=params(60),
        cost_estimate=SHORT,
        name="add",
    )(*keep, *got)


def finish_kernel(tiles, *refs):
    arrived_ref, out_ref = refs[2 * tiles], refs[-1]
    for t in range(tiles):
        at = slice(t * PIECE * TILE, (t + 1) * PIECE * TILE)
        total = refs[t][...].astype(jnp.float32) + refs[tiles + t][...].astype(jnp.float32)
        out_ref[:, at] = (total + arrived_ref[:, at].astype(jnp.float32)).astype(out_ref.dtype)


def finish(keep, got, arrived, place, width, out):
    rows, columns = arrived.shape
    before = [] if out is None else [out]
    return pl.pallas_call(
        functools.partial(finish_kernel, len(keep)),
        out_shape=jax.ShapeDtypeStruct((rows, width), arrived.dtype),
        grid=(1,),
        in_specs=[vmem()] * (2 * len(keep) + 1) + [anywhere() for _ in before],
        out_specs=pl.BlockSpec((rows, columns), lambda g: (0, place)),
        input_output_aliases={2 * len(keep) + 1: 0} if before else {},
        compiler_params=params(16),
        cost_estimate=SHORT,
        name="finish",
    )(*keep, *got, arrived, *before)


def shards(ctx_size, queries, keys, values, out_weight, vertical, slash):
    local_blocks = queries.shape[0] // BLK
    assert ctx_size % 2 == 0 and (NEAR - 1) * local_blocks >= SPAN - 1
    ctx = jnp.reshape(lax.axis_index("ctx"), (1,)).astype(jnp.int32)
    tp = jnp.reshape(lax.axis_index("tp"), (1,)).astype(jnp.int32)

    def shifted(x, by):
        return lax.ppermute(x, "ctx", [(r, r + by) for r in range(ctx_size - by)])

    def swapped(x):
        return lax.ppermute(x, "ctx", [(r, r ^ 1) for r in range(ctx_size)])

    own, pair = pick(ctx, vertical, keys, values)
    kv_2 = shifted(own, 2)
    kv_even = lax.ppermute(own, "ctx", [(r, r + 1) for r in range(0, ctx_size, 2)])
    steps = range(4, ctx_size, 2)
    pairs = [shifted(pair, s) for s in steps]
    near_kv = [own, kv_2, kv_even, swapped(kv_2)]
    pairs += [swapped(x) for x in pairs]
    slots = [(2, 0), (1, 2)] + [(s, 0) for s in steps] + [(s - 1, 2) for s in steps]
    win, pool = masks(ctx, vertical, slash, local_blocks, slots)

    def sibling(x):
        return lax.ppermute(x, "tp", [(j, j ^ 1) for j in range(4)])

    def across(x):
        return lax.ppermute(x, "tp", [(j, j ^ 2) for j in range(4)])

    def attention(flips, tiles, after):
        return attend(
            flips, tp, ctx, queries, win, pool, vertical, near_kv, pairs, out_weight, tiles, after
        )

    width = out_weight.shape[1]
    tiles = width // TILE
    assert tiles == 2 * ACROSS
    send, keep, attended = attention((3, 2), ACROSS, ())
    total = keep.astype(jnp.float32) + sibling(send).astype(jnp.float32)
    total = total.astype(keep.dtype)
    arrived = [across(total)]
    send, keep = project(attended, out_weight, ACROSS, ACROSS, (total,))
    total = add(keep, [sibling(x) for x in send])
    arrived.append(across(total))
    (attended,) = attention((1, 0), 0, (total,))
    send, keep = project(attended, out_weight, 0, tiles, (arrived[0],))
    got = [sibling(x) for x in send]
    out = None
    for place, part in enumerate(arrived):
        at = slice(place * ACROSS // PIECE, (place + 1) * ACROSS // PIECE)
        out = finish(keep[at], got[at], part, place, width, out)
    return out


def solution(mesh):
    assert mesh.shape["tp"] == 4
    return jax.shard_map(
        functools.partial(shards, mesh.shape["ctx"]),
        mesh=mesh,
        in_specs=(
            P("ctx", "tp"),
            P("ctx", "tp"),
            P("ctx", "tp"),
            P("tp", None),
            P("tp", None),
            P("tp", None),
        ),
        out_specs=P(("ctx", "tp"), None),
        check_vma=False,
    )
```

```python
import functools

import jax
import jax.numpy as jnp
from jax import lax
from jax.experimental import pallas as pl
from jax.experimental.pallas import tpu as pltpu
from jax.sharding import PartitionSpec as P

HS = 128
BLK = 64
SPAN = 16
VMOST = 2
NEAR = 3
LANES = 128
MASKED = -1e30
EXP_SCALE = 1.4426950408889634 / (HS**0.5)
TILE = 1024
PIECE = 2
ACROSS = 4
MIB = 1024 * 1024


SHORT = pl.CostEstimate(flops=0, bytes_accessed=0, transcendentals=0)


def vmem():
    return pl.BlockSpec(memory_space=pltpu.VMEM)


def smem():
    return pl.BlockSpec(memory_space=pltpu.SMEM)


def anywhere():
    return pl.BlockSpec(memory_space=pl.ANY)


def params(mib):
    return pltpu.CompilerParams(vmem_limit_bytes=mib * MIB)


def picked_blocks(vertical, shard, local_blocks):
    block = vertical - shard * local_blocks
    block = jnp.where((block >= 0) & (block < local_blocks), block, local_blocks)
    first = jnp.min(block)
    second = jnp.min(jnp.where(block > first, block, local_blocks))
    return [
        pl.ds(pl.multiple_of(jnp.minimum(x, local_blocks - 1) * BLK, BLK), BLK)
        for x in (first, second)
    ]


def pick_kernel(rank_ref, vert_ref, k_ref, v_ref, both_ref, pair_ref):
    both_ref[:, :HS] = k_ref[...]
    both_ref[:, HS:] = v_ref[...]
    blocks = picked_blocks(vert_ref[...], rank_ref[0], k_ref.shape[0] // BLK)
    for slot, rows in enumerate(blocks):
        pair_ref[slot * BLK : (slot + 1) * BLK, :] = both_ref[rows, :]


def pick(rank, vertical, keys, values):
    return pl.pallas_call(
        pick_kernel,
        out_shape=(
            jax.ShapeDtypeStruct((keys.shape[0], 2 * HS), keys.dtype),
            jax.ShapeDtypeStruct((VMOST * BLK, 2 * HS), keys.dtype),
        ),
        in_specs=[smem(), vmem(), vmem(), vmem()],
        out_specs=(vmem(), vmem()),
        compiler_params=params(60),
        name="pick",
    )(rank, vertical, keys, values)


def mask_kernel(local_blocks, slots, rank_ref, vert_ref, slash_ref, win_ref, pool_ref):
    heads, vert_count = vert_ref.shape
    slash_count = slash_ref.shape[1]
    rank = rank_ref[0]
    lane = lax.broadcasted_iota(jnp.int32, (heads, LANES), 1)
    vert = [vert_ref[:, s : s + 1] for s in range(vert_count)]
    zero = jnp.zeros((heads, LANES), jnp.float32)

    def member(columns, blocks):
        found = columns[0] == blocks
        for column in columns[1:]:
            found = found | (column == blocks)
        return found

    offset_ok = member([slash_ref[:, s : s + 1] for s in range(slash_count)], SPAN - 1 - lane)
    shard = jnp.full((heads, LANES), -1, jnp.int32)
    for slot, back in enumerate(slots):
        shard = jnp.where(lane // VMOST == slot, rank - back, shard)
    first = jnp.full((1, LANES), local_blocks, jnp.int32)
    second = first
    for j in reversed(range(local_blocks)):
        here = member(vert, shard * local_blocks + j)
        here = jnp.max(jnp.where(here, 1, 0), axis=0, keepdims=True) == 1
        second = jnp.where(here, first, second)
        first = jnp.where(here, j, first)
    picked = jnp.where(lane % VMOST == 0, first, second)
    block = shard * local_blocks + picked
    pool_ok = (picked < local_blocks) & (shard >= 0) & member(vert, block)
    for i in range(local_blocks):
        row = rank * local_blocks + i
        seen = row - (SPAN - 1) + lane
        ok = (seen >= 0) & (offset_ok | member(vert, seen))
        win_ref[i] = jnp.where(ok | (lane >= SPAN), zero, MASKED)
        pool_ref[i] = jnp.where(pool_ok & (block < row - (SPAN - 1)), zero, MASKED)


def masks(rank, vertical, slash, local_blocks, slots):
    heads = vertical.shape[0]
    shape = jax.ShapeDtypeStruct((local_blocks, heads, LANES), jnp.float32)
    return pl.pallas_call(
        functools.partial(mask_kernel, local_blocks, slots),
        out_shape=(shape, shape),
        in_specs=[smem(), vmem(), vmem()],
        out_specs=(vmem(), vmem()),
        compiler_params=params(60),
        name="masks",
    )(rank, vertical, slash)


def attend_kernel(names, tiles, here_of, tp_ref, ctx_ref, *refs):
    ref = dict(zip(names, refs))
    near, far = "win" in ref, "pool" in ref
    q_ref = ref["q"]
    step = pl.program_id(0)
    heads = q_ref.shape[1] // HS
    dtype = q_ref.dtype

    def fetch(t):
        return pltpu.make_async_copy(
            ref["w"].at[:, pl.ds(t * TILE, TILE)], ref["weight"].at[t], ref["arrival"].at[t]
        )

    @pl.when(step == 0)
    def _():
        for t in range(tiles):
            fetch(t).start()
        rows = ref["kv_2"].shape[0]
        if near:
            for s, name in enumerate(("kv_2", "kv_1", "own")):
                ref["k_win"][s * rows : (s + 1) * rows, :] = ref[name][:, :HS]
                ref["v_win"][s * rows : (s + 1) * rows, :] = ref[name][:, HS:]
            e_win = ref["e_win"]
            key = lax.broadcasted_iota(jnp.int32, e_win.shape, 0)
            lane = lax.broadcasted_iota(jnp.int32, e_win.shape, 1)
            last = (key // BLK == SPAN - 1) & (key % BLK == lane - BLK)
            e_win[...] = jnp.where((key // BLK == lane) | last, 1.0, 0.0).astype(dtype)
        if far:
            blocks = picked_blocks(ref["vert"][...], ctx_ref[0] - (NEAR - 1), rows // BLK)
            for slot, block in enumerate(blocks):
                at = slice(slot * BLK, (slot + 1) * BLK)
                ref["k_pool"][at, :] = ref["kv_2"][block, :HS]
                ref["v_pool"][at, :] = ref["kv_2"][block, HS:]
            e_pool = ref["e_pool"]
            for s in range(1, e_pool.shape[0] // (VMOST * BLK)):
                at = slice(s * VMOST * BLK, (s + 1) * VMOST * BLK)
                ref["k_pool"][at, :] = ref["pair", s][:, :HS]
                ref["v_pool"][at, :] = ref["pair", s][:, HS:]
            key = lax.broadcasted_iota(jnp.int32, e_pool.shape, 0)
            lane = lax.broadcasted_iota(jnp.int32, e_pool.shape, 1)
            e_pool[...] = jnp.where(key // BLK == lane, 1.0, 0.0).astype(dtype)

    q = q_ref[...]
    q = jnp.concatenate([q[:, h * HS : (h + 1) * HS] for h in range(heads)], axis=0)

    def scores_of(mask, keys, lanes):
        mask = mask.reshape(heads * BLK, LANES).astype(dtype)
        return lax.dot_general(
            jnp.concatenate([q, mask], axis=1),
            jnp.concatenate([keys, lanes], axis=1),
            (((1,), (1,)), ((), ())),
            preferred_element_type=jnp.float32,
        )

    def weigh(scores, top, values):
        probs = jnp.exp2((scores - top) * EXP_SCALE).astype(dtype)
        values = jnp.concatenate([values, jnp.ones((values.shape[0], LANES), dtype)], axis=1)
        return jnp.dot(probs, values, preferred_element_type=jnp.float32)

    if near:
        row = lax.broadcasted_iota(jnp.int32, (BLK, LANES), 0)
        lane = lax.broadcasted_iota(jnp.int32, (BLK, LANES), 1)
        above = jnp.where(lane - BLK > row, MASKED, 0.0).astype(jnp.float32)
        start = pl.multiple_of((here_of(step, tp_ref) + 1) * BLK, BLK)
        window = pl.ds(start, SPAN * BLK)
        near_scores = scores_of(
            ref["win"][0][:, None, :] + above[None], ref["k_win"][window, :], ref["e_win"][...]
        )
        top = jnp.max(near_scores, axis=1, keepdims=True)
    if far:
        mask = jnp.broadcast_to(ref["pool"][0][:, None, :], (heads, BLK, LANES))
        far_scores = scores_of(mask, ref["k_pool"][...], ref["e_pool"][...])
        far_top = jnp.max(far_scores, axis=1, keepdims=True)
        if near:
            top = jnp.maximum(top, far_top)
        else:
            near_top = ref["top"][...]
            top = jnp.maximum(near_top[:, :1], far_top)
            shrink = jnp.exp2((near_top - top) * EXP_SCALE)
            summed = ref["sum"][...] * jnp.concatenate([shrink, shrink], axis=1)
    if near:
        summed = weigh(near_scores, top, ref["v_win"][window, :])
    if far:
        summed = summed + weigh(far_scores, top, ref["v_pool"][...])
    else:
        ref["sum_out"][...] = summed
        ref["top_out"][...] = jnp.broadcast_to(top, (heads * BLK, LANES))
        return

    out = (summed[:, :HS] / summed[:, HS:]).astype(dtype)
    attended = ref["attended"]
    out_rows = pl.ds(pl.multiple_of(step * BLK, BLK), BLK)
    for h in range(heads):
        attended[out_rows, h * HS : (h + 1) * HS] = out[h * BLK : (h + 1) * BLK]

    @pl.when(step == pl.num_programs(0) - 1)
    def _():
        ref["rows_out"][...] = attended[...]
        half = attended.shape[0] // 2
        for t in range(tiles):
            fetch(t).wait()
            product = jnp.dot(attended[...], ref["weight"][t], preferred_element_type=jnp.float32)
            product = product.astype(dtype)
            ref["send"][:, t * TILE : (t + 1) * TILE] = product[:half]
            ref["keep"][:, t * TILE : (t + 1) * TILE] = product[half:]


def attend(flips, tp, ctx, arrays, near, far, tiles, after):
    queries, win, dtype = arrays["q"], arrays["win"], arrays["q"].dtype
    width = queries.shape[1]
    local_blocks, heads, _ = win.shape
    quarter = local_blocks // 4
    steps = len(flips) * quarter
    rows = arrays["own"].shape[0]
    pairs = [name for name in arrays if isinstance(name, tuple)]
    far_rows = (len(pairs) + 1) * VMOST * BLK

    def here_of(step, tp_ref):
        owner = tp_ref[0] ^ jnp.where(step < quarter, flips[0], flips[1])
        return owner * quarter + step % quarter

    def whole(shape):
        return pl.BlockSpec(shape, lambda g, tp, ctx: (0,) * len(shape))

    def stepped(*block):
        return pl.BlockSpec(block, lambda g, tp, ctx: (g, 0))

    table = pl.BlockSpec((1, heads, LANES), lambda g, tp, ctx: (here_of(g, tp), 0, 0))
    inputs = {"q": pl.BlockSpec((BLK, width), lambda g, tp, ctx: (here_of(g, tp), 0))}
    inputs["kv_2"] = whole(arrays["kv_2"].shape)
    outputs, scratch = {}, {}
    if near:
        inputs["win"] = table
        inputs["kv_1"] = inputs["own"] = inputs["kv_2"]
        scratch["k_win"] = scratch["v_win"] = pltpu.VMEM((NEAR * rows, HS), dtype)
        scratch["e_win"] = pltpu.VMEM((SPAN * BLK, LANES), dtype)
    if far:
        inputs["pool"] = table
        inputs["vert"] = whole(arrays["vert"].shape)
        inputs.update((name, whole(arrays[name].shape)) for name in pairs)
        scratch["k_pool"] = scratch["v_pool"] = pltpu.VMEM((far_rows, HS), dtype)
        scratch["e_pool"] = pltpu.VMEM((far_rows, LANES), dtype)
        scratch["attended"] = pltpu.VMEM((steps * BLK, width), dtype)
        outputs["rows_out"] = (jax.ShapeDtypeStruct((steps * BLK, width), dtype), None)
        if not near:
            inputs["sum"] = stepped(heads * BLK, 2 * LANES)
            inputs["top"] = stepped(heads * BLK, LANES)
    else:
        shape = (steps * heads * BLK, 2 * LANES)
        outputs["sum_out"] = (jax.ShapeDtypeStruct(shape, jnp.float32), stepped(heads * BLK, 2 * LANES))
        shape = (steps * heads * BLK, LANES)
        outputs["top_out"] = (jax.ShapeDtypeStruct(shape, jnp.float32), stepped(heads * BLK, LANES))
    if tiles:
        inputs["w"] = anywhere()
        part = jax.ShapeDtypeStruct((steps * BLK // 2, tiles * TILE), dtype)
        outputs["send"] = outputs["keep"] = (part, None)
        scratch["weight"] = pltpu.VMEM((tiles, width, TILE), dtype)
        scratch["arrival"] = pltpu.SemaphoreType.DMA((tiles,))
    for place, x in enumerate(after):
        inputs["after", place] = anywhere()
        arrays = {**arrays, ("after", place): x}
    return pl.pallas_call(
        functools.partial(attend_kernel, [*inputs, *outputs, *scratch], tiles, here_of),
        out_shape=[shape for shape, _ in outputs.values()],
        grid_spec=pltpu.PrefetchScalarGridSpec(
            num_scalar_prefetch=2,
            grid=(steps,),
            in_specs=list(inputs.values()),
            out_specs=[spec or whole(shape.shape) for shape, spec in outputs.values()],
            scratch_shapes=list(scratch.values()),
        ),
        compiler_params=params(60),
        cost_estimate=SHORT,
        name="attend",
    )(tp, ctx, *[arrays[name] for name in inputs])


def project_kernel(first, a_ref, w_hbm, *refs):
    weight, arrival = refs[-2:]
    tiles = weight.shape[0]
    pieces = tiles // PIECE
    outs = refs[-2 - 2 * pieces : -2]
    half = outs[0].shape[0]

    def fetch(t):
        return pltpu.make_async_copy(
            w_hbm.at[:, pl.ds((first + t) * TILE, TILE)], weight.at[t], arrival.at[t]
        )

    for t in range(tiles):
        fetch(t).start()
    for t in range(tiles):
        fetch(t).wait()
        product = jnp.dot(a_ref[...], weight[t], preferred_element_type=jnp.float32)
        product = product.astype(a_ref.dtype)
        at = slice(t % PIECE * TILE, (t % PIECE + 1) * TILE)
        outs[t // PIECE][:, at] = product[:half]
        outs[pieces + t // PIECE][:, at] = product[half:]


def project(attended, out_weight, first, tiles, after):
    rows, depth = attended.shape
    pieces = tiles // PIECE
    part = jax.ShapeDtypeStruct((rows // 2, PIECE * TILE), attended.dtype)
    outs = pl.pallas_call(
        functools.partial(project_kernel, first),
        out_shape=[part] * (2 * pieces),
        in_specs=[vmem(), anywhere()] + [anywhere() for _ in after],
        out_specs=[vmem()] * (2 * pieces),
        scratch_shapes=[
            pltpu.VMEM((tiles, depth, TILE), attended.dtype),
            pltpu.SemaphoreType.DMA((tiles,)),
        ],
        compiler_params=params(60),
        cost_estimate=SHORT,
        name="project",
    )(attended, out_weight, *after)
    return outs[:pieces], outs[pieces:]


def add_kernel(*refs):
    out_ref = refs[-1]
    tiles = len(refs) // 2
    for t in range(tiles):
        total = refs[t][...].astype(jnp.float32) + refs[tiles + t][...].astype(jnp.float32)
        out_ref[:, t * PIECE * TILE : (t + 1) * PIECE * TILE] = total.astype(out_ref.dtype)


def add(keep, got):
    rows = keep[0].shape[0]
    return pl.pallas_call(
        add_kernel,
        out_shape=jax.ShapeDtypeStruct((rows, len(keep) * PIECE * TILE), keep[0].dtype),
        in_specs=[vmem()] * (2 * len(keep)),
        out_specs=vmem(),
        compiler_params=params(60),
        cost_estimate=SHORT,
        name="add",
    )(*keep, *got)


def finish_kernel(tiles, *refs):
    arrived_ref, out_ref = refs[2 * tiles], refs[-1]
    for t in range(tiles):
        at = slice(t * PIECE * TILE, (t + 1) * PIECE * TILE)
        total = refs[t][...].astype(jnp.float32) + refs[tiles + t][...].astype(jnp.float32)
        out_ref[:, at] = (total + arrived_ref[:, at].astype(jnp.float32)).astype(out_ref.dtype)


def finish(keep, got, arrived, place, width, out):
    rows, columns = arrived.shape
    before = [] if out is None else [out]
    return pl.pallas_call(
        functools.partial(finish_kernel, len(keep)),
        out_shape=jax.ShapeDtypeStruct((rows, width), arrived.dtype),
        grid=(1,),
        in_specs=[vmem()] * (2 * len(keep) + 1) + [anywhere() for _ in before],
        out_specs=pl.BlockSpec((rows, columns), lambda g: (0, place)),
        input_output_aliases={2 * len(keep) + 1: 0} if before else {},
        compiler_params=params(16),
        cost_estimate=SHORT,
        name="finish",
    )(*keep, *got, arrived, *before)


def shards(ctx_size, queries, keys, values, out_weight, vertical, slash):
    local_blocks = queries.shape[0] // BLK
    assert ctx_size % 2 == 0 and (NEAR - 1) * local_blocks >= SPAN - 1
    ctx = jnp.reshape(lax.axis_index("ctx"), (1,)).astype(jnp.int32)
    tp = jnp.reshape(lax.axis_index("tp"), (1,)).astype(jnp.int32)

    def shifted(x, by):
        return lax.ppermute(x, "ctx", [(r, r + by) for r in range(ctx_size - by)])

    own, pair = pick(ctx, vertical, keys, values)
    slots = range(NEAR - 1, ctx_size)
    win, pool = masks(ctx, vertical, slash, local_blocks, slots)
    arrays = {"q": queries, "own": own, "win": win, "pool": pool, "vert": vertical, "w": out_weight}
    arrays["kv_1"], arrays["kv_2"] = shifted(own, 1), shifted(own, 2)
    for slot, back in list(enumerate(slots))[1:]:
        arrays["pair", slot] = shifted(pair, back)

    def sibling(x):
        return lax.ppermute(x, "tp", [(j, j ^ 1) for j in range(4)])

    def across(x):
        return lax.ppermute(x, "tp", [(j, j ^ 2) for j in range(4)])

    width = out_weight.shape[1]
    tiles = width // TILE
    assert tiles == 2 * ACROSS
    arrays["sum"], arrays["top"] = attend((3, 2), tp, ctx, arrays, True, False, 0, ())
    attended, send, keep = attend((3, 2), tp, ctx, arrays, False, True, ACROSS, ())
    total = keep.astype(jnp.float32) + sibling(send).astype(jnp.float32)
    total = total.astype(keep.dtype)
    arrived = [across(total)]
    send, keep = project(attended, out_weight, ACROSS, ACROSS, (total,))
    total = add(keep, [sibling(x) for x in send])
    arrived.append(across(total))
    (attended,) = attend((1, 0), tp, ctx, arrays, True, True, 0, (total,))
    send, keep = project(attended, out_weight, 0, tiles, (arrived[0],))
    got = [sibling(x) for x in send]
    out = None
    for place, part in enumerate(arrived):
        at = slice(place * ACROSS // PIECE, (place + 1) * ACROSS // PIECE)
        out = finish(keep[at], got[at], part, place, width, out)
    return out


def solution(mesh):
    assert mesh.shape["tp"] == 4
    return jax.shard_map(
        functools.partial(shards, mesh.shape["ctx"]),
        mesh=mesh,
        in_specs=(
            P("ctx", "tp"),
            P("ctx", "tp"),
            P("ctx", "tp"),
            P("tp", None),
            P("tp", None),
            P("tp", None),
        ),
        out_specs=P(("ctx", "tp"), None),
        check_vma=False,
    )
```

```python
import functools

import jax
import jax.numpy as jnp
from jax import lax
from jax.experimental import pallas as pl
from jax.experimental.pallas import tpu as pltpu
from jax.sharding import PartitionSpec as P

HS = 128
BLK = 64
SPAN = 16
VMOST = 2
NEAR = 3
LANES = 128
MASKED = -1e30
EXP_SCALE = 1.4426950408889634 / (HS**0.5)
TILE = 1024
PIECE = 2
HEAD = 4
MIB = 1024 * 1024


SHORT = pl.CostEstimate(flops=0, bytes_accessed=0, transcendentals=0)


def vmem():
    return pl.BlockSpec(memory_space=pltpu.VMEM)


def smem():
    return pl.BlockSpec(memory_space=pltpu.SMEM)


def anywhere():
    return pl.BlockSpec(memory_space=pl.ANY)


def params(mib):
    return pltpu.CompilerParams(vmem_limit_bytes=mib * MIB)


def picked_blocks(vertical, shard, local_blocks):
    block = vertical - shard * local_blocks
    block = jnp.where((block >= 0) & (block < local_blocks), block, local_blocks)
    first = jnp.min(block)
    second = jnp.min(jnp.where(block > first, block, local_blocks))
    return [
        pl.ds(pl.multiple_of(jnp.minimum(x, local_blocks - 1) * BLK, BLK), BLK)
        for x in (first, second)
    ]


def pick_kernel(rank_ref, vert_ref, k_ref, v_ref, both_ref, pair_ref):
    both_ref[:, :HS] = k_ref[...]
    both_ref[:, HS:] = v_ref[...]
    blocks = picked_blocks(vert_ref[...], rank_ref[0], k_ref.shape[0] // BLK)
    for slot, rows in enumerate(blocks):
        pair_ref[slot * BLK : (slot + 1) * BLK, :] = both_ref[rows, :]


def pick(rank, vertical, keys, values):
    return pl.pallas_call(
        pick_kernel,
        out_shape=(
            jax.ShapeDtypeStruct((keys.shape[0], 2 * HS), keys.dtype),
            jax.ShapeDtypeStruct((VMOST * BLK, 2 * HS), keys.dtype),
        ),
        in_specs=[smem(), vmem(), vmem(), vmem()],
        out_specs=(vmem(), vmem()),
        compiler_params=params(60),
        name="pick",
    )(rank, vertical, keys, values)


def member(table, blocks):
    found = table[:, :1] == blocks
    for column in range(1, table.shape[1]):
        found = found | (table[:, column : column + 1] == blocks)
    return found


def pool_blocks(vertical, rank, slots, local_blocks):
    lane = lax.broadcasted_iota(jnp.int32, (vertical.shape[0], LANES), 1)
    shard = jnp.where(lane // VMOST < slots, rank - (NEAR - 1) - lane // VMOST, -1)
    first = jnp.full((1, LANES), local_blocks, jnp.int32)
    second = first
    for j in reversed(range(local_blocks)):
        here = member(vertical, shard * local_blocks + j)
        here = jnp.max(jnp.where(here, 1, 0), axis=0, keepdims=True) == 1
        second = jnp.where(here, first, second)
        first = jnp.where(here, j, first)
    picked = jnp.where(lane % VMOST == 0, first, second)
    return jnp.where((picked < local_blocks) & (shard >= 0), shard * local_blocks + picked, -1)


def attend_kernel(
    slots, tiles, flips, tp_ref, ctx_ref, q_ref, vert_ref, slash_ref, own, kv_1, kv_2, *refs
):
    pairs = refs[: slots - 1]
    w_hbm = refs[slots - 1]
    kv_win, e_win, kv_pool, e_pool, blocks_ref, attended, weight, arrival, landed = refs[-9:]
    outs = refs[-12:-9] if tiles else refs[-10:-9]
    step = pl.program_id(0)
    heads = vert_ref.shape[0]
    rows = own.shape[0]
    local_blocks = rows // BLK
    quarter = local_blocks // 4
    pair_rows = VMOST * BLK
    dtype = q_ref.dtype
    rank = ctx_ref[0]

    def fetch(t):
        return pltpu.make_async_copy(
            w_hbm.at[:, pl.ds(t * TILE, TILE)], weight.at[t], arrival.at[t]
        )

    @pl.when(step == 0)
    def _():
        copies = [
            pltpu.make_async_copy(x, kv_win.at[pl.ds(s * rows, rows), :], landed.at[s])
            for s, x in enumerate((kv_2, kv_1, own))
        ]
        copies += [
            pltpu.make_async_copy(
                x, kv_pool.at[pl.ds((s + 1) * pair_rows, pair_rows), :], landed.at[NEAR + s]
            )
            for s, x in enumerate(pairs)
        ]
        for copy in copies:
            copy.start()
        for t in range(tiles):
            fetch(t).start()
        key = lax.broadcasted_iota(jnp.int32, e_win.shape, 0)
        lane = lax.broadcasted_iota(jnp.int32, e_win.shape, 1)
        last = (key - (SPAN - 1) * BLK == lane - BLK) & (lane >= BLK)
        e_win[...] = jnp.where((key // BLK == lane) | last, 1.0, 0.0).astype(dtype)
        key = lax.broadcasted_iota(jnp.int32, e_pool.shape, 0)
        lane = lax.broadcasted_iota(jnp.int32, e_pool.shape, 1)
        e_pool[...] = jnp.where(key // BLK == lane, 1.0, 0.0).astype(dtype)
        blocks_ref[...] = pool_blocks(vert_ref[...], rank, slots, local_blocks)
        picked = picked_blocks(vert_ref[...], rank - (NEAR - 1), local_blocks)
        for copy in copies:
            copy.wait()
        for slot, block in enumerate(picked):
            kv_pool[slot * BLK : (slot + 1) * BLK, :] = kv_win[block, :]

    owner = tp_ref[0] ^ jnp.where(step == 0, flips[0], flips[1])
    lane = lax.broadcasted_iota(jnp.int32, (heads, LANES), 1)
    row = lax.broadcasted_iota(jnp.int32, (BLK, LANES), 0)
    above = lax.broadcasted_iota(jnp.int32, (BLK, LANES), 1) - BLK > row
    above = jnp.where(above, MASKED, 0.0).astype(jnp.float32)
    offset_ok = member(slash_ref[...], SPAN - 1 - lane)
    block = blocks_ref[...]
    pool_ok = member(vert_ref[...], block) & (block >= 0)
    contract = (((1,), (1,)), ((), ()))

    def with_ones(values):
        return jnp.concatenate([values, jnp.ones((values.shape[0], LANES), dtype)], axis=1)

    near, far_q, windows = [], [], []
    for u in range(quarter):
        here = owner * quarter + u
        q = q_ref[u * BLK : (u + 1) * BLK, :]
        q = jnp.concatenate([q[:, h * HS : (h + 1) * HS] for h in range(heads)], axis=0)
        first = rank * local_blocks + here - (SPAN - 1)
        seen = first + lane
        ok = (seen >= 0) & (offset_ok | member(vert_ref[...], seen))
        mask = jnp.where(ok | (lane >= SPAN), 0.0, MASKED).astype(jnp.float32)
        mask = (mask[:, None, :] + above[None]).reshape(heads * BLK, LANES).astype(dtype)
        far_mask = jnp.where(pool_ok & (block < first), 0.0, MASKED).astype(jnp.float32)
        far_mask = jnp.broadcast_to(far_mask[:, None, :], (heads, BLK, LANES))
        far_mask = far_mask.reshape(heads * BLK, LANES).astype(dtype)
        far_q.append(jnp.concatenate([q, far_mask], axis=1))
        window = pl.ds(pl.multiple_of((here + 1) * BLK, BLK), SPAN * BLK)
        windows.append(window)
        keys = jnp.concatenate([kv_win[window, :HS], e_win[...]], axis=1)
        near.append(
            lax.dot_general(
                jnp.concatenate([q, mask], axis=1),
                keys,
                contract,
                preferred_element_type=jnp.float32,
            )
        )
    far = lax.dot_general(
        jnp.concatenate(far_q, axis=0),
        jnp.concatenate([kv_pool[:, :HS], e_pool[...]], axis=1),
        contract,
        preferred_element_type=jnp.float32,
    )
    far_values = with_ones(kv_pool[:, HS:])
    for u in range(quarter):
        far_u = far[u * heads * BLK : (u + 1) * heads * BLK]
        top = jnp.maximum(
            jnp.max(near[u], axis=1, keepdims=True), jnp.max(far_u, axis=1, keepdims=True)
        )
        probs = jnp.exp2((near[u] - top) * EXP_SCALE).astype(dtype)
        values = with_ones(kv_win[windows[u], HS:])
        summed = jnp.dot(probs, values, preferred_element_type=jnp.float32)
        probs = jnp.exp2((far_u - top) * EXP_SCALE).astype(dtype)
        summed = summed + jnp.dot(probs, far_values, preferred_element_type=jnp.float32)
        out = (summed[:, :HS] / summed[:, HS:]).astype(dtype)
        at = pl.ds(pl.multiple_of((step * quarter + u) * BLK, BLK), BLK)
        for h in range(heads):
            attended[at, h * HS : (h + 1) * HS] = out[h * BLK : (h + 1) * BLK]

    @pl.when(step == pl.num_programs(0) - 1)
    def _():
        outs[0][...] = attended[...]
        half = attended.shape[0] // 2
        for t in range(tiles):
            fetch(t).wait()
            product = jnp.dot(attended[...], weight[t], preferred_element_type=jnp.float32)
            product = product.astype(dtype)
            outs[1][:, t * TILE : (t + 1) * TILE] = product[:half]
            outs[2][:, t * TILE : (t + 1) * TILE] = product[half:]


def attend(flips, tp, ctx, queries, vertical, slash, near_kv, pairs, out_weight, tiles, after):
    width = queries.shape[1]
    rows = near_kv[0].shape[0]
    quarter = rows // 4
    steps = len(flips)
    slots = len(pairs) + 1
    dtype = queries.dtype
    far = slots * VMOST * BLK

    def place(g, tp, ctx):
        return (tp[0] ^ jnp.where(g == 0, flips[0], flips[1]), 0)

    def whole(shape):
        return pl.BlockSpec(shape, lambda g, tp, ctx: (0,) * len(shape))

    out_shapes = [(steps * quarter, width)]
    if tiles:
        out_shapes += [(steps * quarter // 2, tiles * TILE)] * 2
    return pl.pallas_call(
        functools.partial(attend_kernel, slots, tiles, flips),
        out_shape=[jax.ShapeDtypeStruct(shape, dtype) for shape in out_shapes],
        grid_spec=pltpu.PrefetchScalarGridSpec(
            num_scalar_prefetch=2,
            grid=(steps,),
            in_specs=[pl.BlockSpec((quarter, width), place)]
            + [whole(vertical.shape), whole(slash.shape)]
            + [anywhere() for _ in [*near_kv, *pairs, out_weight, *after]],
            out_specs=[whole(shape) for shape in out_shapes],
            scratch_shapes=[
                pltpu.VMEM((NEAR * rows, 2 * HS), dtype),
                pltpu.VMEM((SPAN * BLK, LANES), dtype),
                pltpu.VMEM((far, 2 * HS), dtype),
                pltpu.VMEM((far, LANES), dtype),
                pltpu.VMEM((vertical.shape[0], LANES), jnp.int32),
                pltpu.VMEM((steps * quarter, width), dtype),
                pltpu.VMEM((max(tiles, 1), out_weight.shape[0], TILE), dtype),
                pltpu.SemaphoreType.DMA((max(tiles, 1),)),
                pltpu.SemaphoreType.DMA((NEAR + len(pairs),)),
            ],
        ),
        compiler_params=params(60),
        cost_estimate=SHORT,
        name="attend",
    )(tp, ctx, queries, vertical, slash, *near_kv, *pairs, out_weight, *after)


def project_kernel(first, a_ref, w_hbm, *refs):
    weight, arrival = refs[-2:]
    tiles = weight.shape[0]
    pieces = tiles // PIECE
    outs = refs[-2 - 2 * pieces : -2]
    half = outs[0].shape[0]

    def fetch(t):
        return pltpu.make_async_copy(
            w_hbm.at[:, pl.ds((first + t) * TILE, TILE)], weight.at[t], arrival.at[t]
        )

    for t in range(tiles):
        fetch(t).start()
    for t in range(tiles):
        fetch(t).wait()
        product = jnp.dot(a_ref[...], weight[t], preferred_element_type=jnp.float32)
        product = product.astype(a_ref.dtype)
        at = slice(t % PIECE * TILE, (t % PIECE + 1) * TILE)
        outs[t // PIECE][:, at] = product[:half]
        outs[pieces + t // PIECE][:, at] = product[half:]


def project(attended, out_weight, first, tiles, after):
    rows, depth = attended.shape
    pieces = tiles // PIECE
    part = jax.ShapeDtypeStruct((rows // 2, PIECE * TILE), attended.dtype)
    outs = pl.pallas_call(
        functools.partial(project_kernel, first),
        out_shape=[part] * (2 * pieces),
        in_specs=[vmem(), anywhere()] + [anywhere() for _ in after],
        out_specs=[vmem()] * (2 * pieces),
        scratch_shapes=[
            pltpu.VMEM((tiles, depth, TILE), attended.dtype),
            pltpu.SemaphoreType.DMA((tiles,)),
        ],
        compiler_params=params(60),
        cost_estimate=SHORT,
        name="project",
    )(attended, out_weight, *after)
    return outs[:pieces], outs[pieces:]


def add_kernel(*refs):
    out_ref = refs[-1]
    tiles = len(refs) // 2
    for t in range(tiles):
        total = refs[t][...].astype(jnp.float32) + refs[tiles + t][...].astype(jnp.float32)
        out_ref[:, t * PIECE * TILE : (t + 1) * PIECE * TILE] = total.astype(out_ref.dtype)


def add(keep, got):
    rows = keep[0].shape[0]
    return pl.pallas_call(
        add_kernel,
        out_shape=jax.ShapeDtypeStruct((rows, len(keep) * PIECE * TILE), keep[0].dtype),
        in_specs=[vmem()] * (2 * len(keep)),
        out_specs=vmem(),
        compiler_params=params(60),
        cost_estimate=SHORT,
        name="add",
    )(*keep, *got)


def finish_kernel(pieces, *refs):
    arrived_ref, out_ref = refs[2 * pieces], refs[-1]
    step = pl.program_id(0)
    for t in range(pieces * PIECE):

        @pl.when(step == t)
        def _():
            part = slice(t % PIECE * TILE, (t % PIECE + 1) * TILE)
            total = refs[t // PIECE][:, part].astype(jnp.float32)
            total = total + refs[pieces + t // PIECE][:, part].astype(jnp.float32)
            total = total + arrived_ref[:, t * TILE : (t + 1) * TILE].astype(jnp.float32)
            out_ref[...] = total.astype(out_ref.dtype)


def finish(keep, got, arrived, first, width, out):
    rows = arrived.shape[0]
    before = [] if out is None else [out]
    return pl.pallas_call(
        functools.partial(finish_kernel, len(keep)),
        out_shape=jax.ShapeDtypeStruct((rows, width), arrived.dtype),
        grid=(len(keep) * PIECE,),
        in_specs=[vmem()] * (2 * len(keep) + 1) + [anywhere() for _ in before],
        out_specs=pl.BlockSpec((rows, TILE), lambda g: (0, first + g)),
        input_output_aliases={2 * len(keep) + 1: 0} if before else {},
        compiler_params=params(16),
        cost_estimate=SHORT,
        name="finish",
    )(*keep, *got, arrived, *before)


def shards(ctx_size, queries, keys, values, out_weight, vertical, slash):
    local_blocks = queries.shape[0] // BLK
    assert ctx_size % 2 == 0 and (NEAR - 1) * local_blocks >= SPAN - 1
    ctx = jnp.reshape(lax.axis_index("ctx"), (1,)).astype(jnp.int32)
    tp = jnp.reshape(lax.axis_index("tp"), (1,)).astype(jnp.int32)

    def shifted(x, by):
        return lax.ppermute(x, "ctx", [(r, r + by) for r in range(ctx_size - by)])

    own, pair = pick(ctx, vertical, keys, values)
    near_kv = [own, shifted(own, 1), shifted(own, 2)]
    pairs = [shifted(pair, s) for s in range(NEAR, ctx_size)]

    def sibling(x):
        return lax.ppermute(x, "tp", [(j, j ^ 1) for j in range(4)])

    def across(x):
        return lax.ppermute(x, "tp", [(j, j ^ 2) for j in range(4)])

    def attention(flips, tiles, after):
        return attend(
            flips, tp, ctx, queries, vertical, slash, near_kv, pairs, out_weight, tiles, after
        )

    width = out_weight.shape[1]
    tiles = width // TILE
    attended, send, keep = attention((3, 2), HEAD, ())
    total = keep.astype(jnp.float32) + sibling(send).astype(jnp.float32)
    total = total.astype(keep.dtype)
    arrived = [across(total)]
    send, keep = project(attended, out_weight, HEAD, tiles - HEAD, (total,))
    total = add(keep, [sibling(x) for x in send])
    arrived.append(across(total))
    (attended,) = attention((1, 0), 0, (total,))
    send, keep = project(attended, out_weight, 0, tiles, (arrived[0],))
    got = [sibling(x) for x in send]
    cut = HEAD // PIECE
    out = finish(keep[:cut], got[:cut], arrived[0], 0, width, None)
    return finish(keep[cut:], got[cut:], arrived[1], HEAD, width, out)


def solution(mesh):
    assert mesh.shape["tp"] == 4
    return jax.shard_map(
        functools.partial(shards, mesh.shape["ctx"]),
        mesh=mesh,
        in_specs=(
            P("ctx", "tp"),
            P("ctx", "tp"),
            P("ctx", "tp"),
            P("tp", None),
            P("tp", None),
            P("tp", None),
        ),
        out_specs=P(("ctx", "tp"), None),
        check_vma=False,
    )
```

```python
import functools

import jax
import jax.numpy as jnp
from jax import lax
from jax.experimental import pallas as pl
from jax.experimental.pallas import tpu as pltpu
from jax.sharding import PartitionSpec as P

HS = 128
BLK = 64
SPAN = 16
VMOST = 2
NEAR = 3
LANES = 128
MASKED = -1e30
EXP_SCALE = 1.4426950408889634 / (HS**0.5)
TILE = 1024
PIECE = 2
HEAD = 4
MIB = 1024 * 1024


SHORT = pl.CostEstimate(flops=0, bytes_accessed=0, transcendentals=0)


def vmem():
    return pl.BlockSpec(memory_space=pltpu.VMEM)


def smem():
    return pl.BlockSpec(memory_space=pltpu.SMEM)


def anywhere():
    return pl.BlockSpec(memory_space=pl.ANY)


def params(mib):
    return pltpu.CompilerParams(vmem_limit_bytes=mib * MIB)


def picked_blocks(vertical, shard, local_blocks):
    block = vertical - shard * local_blocks
    block = jnp.where((block >= 0) & (block < local_blocks), block, local_blocks)
    first = jnp.min(block)
    second = jnp.min(jnp.where(block > first, block, local_blocks))
    return [
        pl.ds(pl.multiple_of(jnp.minimum(x, local_blocks - 1) * BLK, BLK), BLK)
        for x in (first, second)
    ]


def pick_kernel(rank_ref, vert_ref, k_ref, v_ref, both_ref, pair_ref):
    both_ref[:, :HS] = k_ref[...]
    both_ref[:, HS:] = v_ref[...]
    blocks = picked_blocks(vert_ref[...], rank_ref[0], k_ref.shape[0] // BLK)
    for slot, rows in enumerate(blocks):
        picked = both_ref[rows, :]
        for copy in range(pair_ref.shape[0]):
            pair_ref[copy, slot * BLK : (slot + 1) * BLK, :] = picked


def pick(rank, vertical, keys, values, copies):
    return pl.pallas_call(
        pick_kernel,
        out_shape=(
            jax.ShapeDtypeStruct((keys.shape[0], 2 * HS), keys.dtype),
            jax.ShapeDtypeStruct((copies, VMOST * BLK, 2 * HS), keys.dtype),
        ),
        in_specs=[smem(), vmem(), vmem(), vmem()],
        out_specs=(vmem(), vmem()),
        compiler_params=params(60),
        name="pick",
    )(rank, vertical, keys, values)


def member(table, blocks):
    found = table[:, :1] == blocks
    for column in range(1, table.shape[1]):
        found = found | (table[:, column : column + 1] == blocks)
    return found


def pool_blocks(vertical, rank, slots, local_blocks):
    lane = lax.broadcasted_iota(jnp.int32, (vertical.shape[0], LANES), 1)
    slot = lane // VMOST
    shard = jnp.where(slot < slots, 2 * slot + (rank & 1), 2 * (slot - slots) + 1 - (rank & 1))
    shard = jnp.where(slot < 2 * slots, shard, -1)
    first = jnp.full((1, LANES), local_blocks, jnp.int32)
    second = first
    for j in reversed(range(local_blocks)):
        here = member(vertical, shard * local_blocks + j)
        here = jnp.max(jnp.where(here, 1, 0), axis=0, keepdims=True) == 1
        second = jnp.where(here, first, second)
        first = jnp.where(here, j, first)
    picked = jnp.where(lane % VMOST == 0, first, second)
    return jnp.where((picked < local_blocks) & (shard >= 0), shard * local_blocks + picked, -1)


def attend_kernel(
    slots, tiles, flips, tp_ref, ctx_ref, q_ref, vert_ref, slash_ref, own, kv_1, kv_2, *refs
):
    pairs = refs[:2]
    w_hbm = refs[2]
    kv_win, e_win, kv_pool, e_pool, blocks_ref, attended, weight, arrival, landed = refs[-9:]
    outs = refs[-12:-9] if tiles else refs[-10:-9]
    step = pl.program_id(0)
    heads = vert_ref.shape[0]
    rows = own.shape[0]
    local_blocks = rows // BLK
    quarter = local_blocks // 4
    pair_rows = VMOST * BLK
    dtype = q_ref.dtype
    rank = ctx_ref[0]

    def fetch(t):
        return pltpu.make_async_copy(
            w_hbm.at[:, pl.ds(t * TILE, TILE)], weight.at[t], arrival.at[t]
        )

    @pl.when(step == 0)
    def _():
        copies = [
            pltpu.make_async_copy(x, kv_win.at[pl.ds(s * rows, rows), :], landed.at[s])
            for s, x in enumerate((kv_2, kv_1, own))
        ]
        copies += [
            pltpu.make_async_copy(
                x.at[s],
                kv_pool.at[pl.ds((p * slots + s) * pair_rows, pair_rows), :],
                landed.at[NEAR + p * slots + s],
            )
            for p, x in enumerate(pairs)
            for s in range(slots)
        ]
        for copy in copies:
            copy.start()
        for t in range(tiles):
            fetch(t).start()
        key = lax.broadcasted_iota(jnp.int32, e_win.shape, 0)
        lane = lax.broadcasted_iota(jnp.int32, e_win.shape, 1)
        last = (key - (SPAN - 1) * BLK == lane - BLK) & (lane >= BLK)
        e_win[...] = jnp.where((key // BLK == lane) | last, 1.0, 0.0).astype(dtype)
        key = lax.broadcasted_iota(jnp.int32, e_pool.shape, 0)
        lane = lax.broadcasted_iota(jnp.int32, e_pool.shape, 1)
        e_pool[...] = jnp.where(key // BLK == lane, 1.0, 0.0).astype(dtype)
        blocks_ref[...] = pool_blocks(vert_ref[...], rank, slots, local_blocks)
        for copy in copies:
            copy.wait()

    owner = tp_ref[0] ^ jnp.where(step == 0, flips[0], flips[1])
    lane = lax.broadcasted_iota(jnp.int32, (heads, LANES), 1)
    row = lax.broadcasted_iota(jnp.int32, (BLK, LANES), 0)
    above = lax.broadcasted_iota(jnp.int32, (BLK, LANES), 1) - BLK > row
    above = jnp.where(above, MASKED, 0.0).astype(jnp.float32)
    offset_ok = member(slash_ref[...], SPAN - 1 - lane)
    block = blocks_ref[...]
    pool_ok = member(vert_ref[...], block) & (block >= 0)
    contract = (((1,), (1,)), ((), ()))

    def with_ones(values):
        return jnp.concatenate([values, jnp.ones((values.shape[0], LANES), dtype)], axis=1)

    near, far_q, windows = [], [], []
    for u in range(quarter):
        here = owner * quarter + u
        q = q_ref[u * BLK : (u + 1) * BLK, :]
        q = jnp.concatenate([q[:, h * HS : (h + 1) * HS] for h in range(heads)], axis=0)
        first = rank * local_blocks + here - (SPAN - 1)
        seen = first + lane
        ok = (seen >= 0) & (offset_ok | member(vert_ref[...], seen))
        mask = jnp.where(ok | (lane >= SPAN), 0.0, MASKED).astype(jnp.float32)
        mask = (mask[:, None, :] + above[None]).reshape(heads * BLK, LANES).astype(dtype)
        far_mask = jnp.where(pool_ok & (block < first), 0.0, MASKED).astype(jnp.float32)
        far_mask = jnp.broadcast_to(far_mask[:, None, :], (heads, BLK, LANES))
        far_mask = far_mask.reshape(heads * BLK, LANES).astype(dtype)
        far_q.append(jnp.concatenate([q, far_mask], axis=1))
        window = pl.ds(pl.multiple_of((here + 1) * BLK, BLK), SPAN * BLK)
        windows.append(window)
        keys = jnp.concatenate([kv_win[window, :HS], e_win[...]], axis=1)
        near.append(
            lax.dot_general(
                jnp.concatenate([q, mask], axis=1),
                keys,
                contract,
                preferred_element_type=jnp.float32,
            )
        )
    far = lax.dot_general(
        jnp.concatenate(far_q, axis=0),
        jnp.concatenate([kv_pool[:, :HS], e_pool[...]], axis=1),
        contract,
        preferred_element_type=jnp.float32,
    )
    far_values = with_ones(kv_pool[:, HS:])
    for u in range(quarter):
        far_u = far[u * heads * BLK : (u + 1) * heads * BLK]
        top = jnp.maximum(
            jnp.max(near[u], axis=1, keepdims=True), jnp.max(far_u, axis=1, keepdims=True)
        )
        probs = jnp.exp2((near[u] - top) * EXP_SCALE).astype(dtype)
        values = with_ones(kv_win[windows[u], HS:])
        summed = jnp.dot(probs, values, preferred_element_type=jnp.float32)
        probs = jnp.exp2((far_u - top) * EXP_SCALE).astype(dtype)
        summed = summed + jnp.dot(probs, far_values, preferred_element_type=jnp.float32)
        out = (summed[:, :HS] / summed[:, HS:]).astype(dtype)
        at = pl.ds(pl.multiple_of((step * quarter + u) * BLK, BLK), BLK)
        for h in range(heads):
            attended[at, h * HS : (h + 1) * HS] = out[h * BLK : (h + 1) * BLK]

    @pl.when(step == pl.num_programs(0) - 1)
    def _():
        outs[0][...] = attended[...]
        half = attended.shape[0] // 2
        for t in range(tiles):
            fetch(t).wait()
            product = jnp.dot(attended[...], weight[t], preferred_element_type=jnp.float32)
            product = product.astype(dtype)
            outs[1][:, t * TILE : (t + 1) * TILE] = product[:half]
            outs[2][:, t * TILE : (t + 1) * TILE] = product[half:]


def attend(flips, tp, ctx, queries, vertical, slash, near_kv, pairs, out_weight, tiles, after):
    width = queries.shape[1]
    rows = near_kv[0].shape[0]
    quarter = rows // 4
    steps = len(flips)
    slots = pairs[0].shape[0] - 1
    dtype = queries.dtype
    far = 2 * slots * VMOST * BLK

    def place(g, tp, ctx):
        return (tp[0] ^ jnp.where(g == 0, flips[0], flips[1]), 0)

    def whole(shape):
        return pl.BlockSpec(shape, lambda g, tp, ctx: (0,) * len(shape))

    out_shapes = [(steps * quarter, width)]
    if tiles:
        out_shapes += [(steps * quarter // 2, tiles * TILE)] * 2
    return pl.pallas_call(
        functools.partial(attend_kernel, slots, tiles, flips),
        out_shape=[jax.ShapeDtypeStruct(shape, dtype) for shape in out_shapes],
        grid_spec=pltpu.PrefetchScalarGridSpec(
            num_scalar_prefetch=2,
            grid=(steps,),
            in_specs=[pl.BlockSpec((quarter, width), place)]
            + [whole(vertical.shape), whole(slash.shape)]
            + [anywhere() for _ in [*near_kv, *pairs, out_weight, *after]],
            out_specs=[whole(shape) for shape in out_shapes],
            scratch_shapes=[
                pltpu.VMEM((NEAR * rows, 2 * HS), dtype),
                pltpu.VMEM((SPAN * BLK, LANES), dtype),
                pltpu.VMEM((far, 2 * HS), dtype),
                pltpu.VMEM((far, LANES), dtype),
                pltpu.VMEM((vertical.shape[0], LANES), jnp.int32),
                pltpu.VMEM((steps * quarter, width), dtype),
                pltpu.VMEM((max(tiles, 1), out_weight.shape[0], TILE), dtype),
                pltpu.SemaphoreType.DMA((max(tiles, 1),)),
                pltpu.SemaphoreType.DMA((NEAR + 2 * slots,)),
            ],
        ),
        compiler_params=params(50),
        cost_estimate=SHORT,
        name="attend",
    )(tp, ctx, queries, vertical, slash, *near_kv, *pairs, out_weight, *after)


def project_kernel(first, a_ref, w_hbm, *refs):
    weight, arrival = refs[-2:]
    tiles = weight.shape[0]
    pieces = tiles // PIECE
    outs = refs[-2 - 2 * pieces : -2]
    half = outs[0].shape[0]

    def fetch(t):
        return pltpu.make_async_copy(
            w_hbm.at[:, pl.ds((first + t) * TILE, TILE)], weight.at[t], arrival.at[t]
        )

    for t in range(tiles):
        fetch(t).start()
    for t in range(tiles):
        fetch(t).wait()
        product = jnp.dot(a_ref[...], weight[t], preferred_element_type=jnp.float32)
        product = product.astype(a_ref.dtype)
        at = slice(t % PIECE * TILE, (t % PIECE + 1) * TILE)
        outs[t // PIECE][:, at] = product[:half]
        outs[pieces + t // PIECE][:, at] = product[half:]


def project(attended, out_weight, first, tiles, after):
    rows, depth = attended.shape
    pieces = tiles // PIECE
    part = jax.ShapeDtypeStruct((rows // 2, PIECE * TILE), attended.dtype)
    outs = pl.pallas_call(
        functools.partial(project_kernel, first),
        out_shape=[part] * (2 * pieces),
        in_specs=[vmem(), anywhere()] + [anywhere() for _ in after],
        out_specs=[vmem()] * (2 * pieces),
        scratch_shapes=[
            pltpu.VMEM((tiles, depth, TILE), attended.dtype),
            pltpu.SemaphoreType.DMA((tiles,)),
        ],
        compiler_params=params(50),
        cost_estimate=SHORT,
        name="project",
    )(attended, out_weight, *after)
    return outs[:pieces], outs[pieces:]


def add(keep, got):
    sums = [k.astype(jnp.float32) + g.astype(jnp.float32) for k, g in zip(keep, got)]
    return jnp.concatenate([x.astype(keep[0].dtype) for x in sums], axis=1)


def finish_kernel(pieces, *refs):
    arrived_ref, out_ref = refs[2 * pieces], refs[-1]
    step = pl.program_id(0)
    for t in range(pieces * PIECE):

        @pl.when(step == t)
        def _():
            part = slice(t % PIECE * TILE, (t % PIECE + 1) * TILE)
            total = refs[t // PIECE][:, part].astype(jnp.float32)
            total = total + refs[pieces + t // PIECE][:, part].astype(jnp.float32)
            total = total + arrived_ref[:, t * TILE : (t + 1) * TILE].astype(jnp.float32)
            out_ref[...] = total.astype(out_ref.dtype)


def finish(keep, got, arrived, first, width, out):
    rows = arrived.shape[0]
    before = [] if out is None else [out]
    return pl.pallas_call(
        functools.partial(finish_kernel, len(keep)),
        out_shape=jax.ShapeDtypeStruct((rows, width), arrived.dtype),
        grid=(len(keep) * PIECE,),
        in_specs=[vmem()] * (2 * len(keep) + 1) + [anywhere() for _ in before],
        out_specs=pl.BlockSpec((rows, TILE), lambda g: (0, first + g)),
        input_output_aliases={2 * len(keep) + 1: 0} if before else {},
        compiler_params=params(16),
        cost_estimate=SHORT,
        name="finish",
    )(*keep, *got, arrived, *before)


def shards(ctx_size, queries, keys, values, out_weight, vertical, slash):
    local_blocks = queries.shape[0] // BLK
    assert ctx_size % 2 == 0 and (NEAR - 1) * local_blocks >= SPAN - 1
    ctx = jnp.reshape(lax.axis_index("ctx"), (1,)).astype(jnp.int32)
    tp = jnp.reshape(lax.axis_index("tp"), (1,)).astype(jnp.int32)

    def shifted(x, by):
        return lax.ppermute(x, "ctx", [(r, r + by) for r in range(ctx_size - by)])

    own, pair = pick(ctx, vertical, keys, values, ctx_size // 2)
    near_kv = [own, shifted(own, 1), shifted(own, 2)]
    parities = [list(range(odd, ctx_size, 2)) for odd in (0, 1)]
    pairs = [lax.all_to_all(pair, "ctx", 0, 0, axis_index_groups=parities, tiled=True)]
    pairs.append(lax.ppermute(pairs[0], "ctx", [(r, r ^ 1) for r in range(ctx_size)]))

    def sibling(x):
        return lax.ppermute(x, "tp", [(j, j ^ 1) for j in range(4)])

    def across(x):
        return lax.ppermute(x, "tp", [(j, j ^ 2) for j in range(4)])

    def attention(flips, tiles, after):
        return attend(
            flips, tp, ctx, queries, vertical, slash, near_kv, pairs, out_weight, tiles, after
        )

    width = out_weight.shape[1]
    tiles = width // TILE
    attended, send, keep = attention((3, 2), HEAD, ())
    total = add([keep], [sibling(send)])
    arrived = [across(total)]
    send, keep = project(attended, out_weight, HEAD, tiles - HEAD, (total,))
    total = add(keep, [sibling(x) for x in send])
    arrived.append(across(total))
    (attended,) = attention((1, 0), 0, (total,))
    send, keep = project(attended, out_weight, 0, tiles, (arrived[0],))
    got = [sibling(x) for x in send]
    cut = HEAD // PIECE
    out = finish(keep[:cut], got[:cut], arrived[0], 0, width, None)
    return finish(keep[cut:], got[cut:], arrived[1], HEAD, width, out)


def solution(mesh):
    assert mesh.shape["tp"] == 4
    return jax.shard_map(
        functools.partial(shards, mesh.shape["ctx"]),
        mesh=mesh,
        in_specs=(
            P("ctx", "tp"),
            P("ctx", "tp"),
            P("ctx", "tp"),
            P("tp", None),
            P("tp", None),
            P("tp", None),
        ),
        out_specs=P(("ctx", "tp"), None),
        check_vma=False,
    )
```

```python
import functools

import jax
import jax.numpy as jnp
from jax import lax
from jax.experimental import pallas as pl
from jax.experimental.pallas import tpu as pltpu
from jax.sharding import PartitionSpec as P

HS = 128
BLK = 64
SPAN = 16
VMOST = 2
NEAR = 3
LANES = 128
NOWHERE = 1 << 20
MASKED = -1e30
EXP_SCALE = 1.4426950408889634 / (HS**0.5)
TILE = 1024
PIECE = 1
HEAD = 4
MIB = 1024 * 1024


SHORT = pl.CostEstimate(flops=0, bytes_accessed=0, transcendentals=0)


def vmem():
    return pl.BlockSpec(memory_space=pltpu.VMEM)


def smem():
    return pl.BlockSpec(memory_space=pltpu.SMEM)


def anywhere():
    return pl.BlockSpec(memory_space=pl.ANY)


def params(mib):
    return pltpu.CompilerParams(vmem_limit_bytes=mib * MIB)


def picked_blocks(vertical, shard, local_blocks):
    block = vertical - shard * local_blocks
    block = jnp.where((block >= 0) & (block < local_blocks), block, local_blocks)
    first = jnp.min(block)
    second = jnp.min(jnp.where(block > first, block, local_blocks))
    return [
        pl.ds(pl.multiple_of(jnp.minimum(x, local_blocks - 1) * BLK, BLK), BLK)
        for x in (first, second)
    ]


def pick_kernel(rank_ref, vert_ref, k_ref, v_ref, both_ref, pair_ref):
    both_ref[:, :HS] = k_ref[...]
    both_ref[:, HS:] = v_ref[...]
    blocks = picked_blocks(vert_ref[...], rank_ref[0], k_ref.shape[0] // BLK)
    for slot, rows in enumerate(blocks):
        pair_ref[slot * BLK : (slot + 1) * BLK, :] = both_ref[rows, :]


def pick(rank, vertical, keys, values):
    return pl.pallas_call(
        pick_kernel,
        out_shape=(
            jax.ShapeDtypeStruct((keys.shape[0], 2 * HS), keys.dtype),
            jax.ShapeDtypeStruct((VMOST * BLK, 2 * HS), keys.dtype),
        ),
        in_specs=[smem(), vmem(), vmem(), vmem()],
        out_specs=(vmem(), vmem()),
        compiler_params=params(60),
        name="pick",
    )(rank, vertical, keys, values)


def member(table, blocks):
    found = table[:, :1] == blocks
    for column in range(1, table.shape[1]):
        found = found | (table[:, column : column + 1] == blocks)
    return found


def pool_blocks(vertical, rank, slots, local_blocks):
    lane = lax.broadcasted_iota(jnp.int32, (vertical.shape[0], LANES), 1)
    shard = jnp.full(lane.shape, -1, jnp.int32)
    for slot, (even, odd) in enumerate(slots):
        back = jnp.where(rank & 1 == 1, odd, even)
        shard = jnp.where(lane // VMOST == slot, rank - back, shard)
    first = jnp.full((1, LANES), local_blocks, jnp.int32)
    second = first
    for j in reversed(range(local_blocks)):
        here = member(vertical, shard * local_blocks + j)
        here = jnp.max(jnp.where(here, 1, 0), axis=0, keepdims=True) == 1
        second = jnp.where(here, first, second)
        first = jnp.where(here, j, first)
    picked = jnp.where(lane % VMOST == 0, first, second)
    return jnp.where((picked < local_blocks) & (shard >= 0), shard * local_blocks + picked, -1)


def attend_kernel(
    slots, tiles, flips, tp_ref, ctx_ref, q_ref, vert_ref, slash_ref, own, kv_1, kv_2, *refs
):
    pairs = refs[: len(slots) - 1]
    w_hbm = refs[len(slots) - 1]
    kv_win, e_win, kv_pool, e_pool, blocks_ref, attended, weight, arrival, landed = refs[-9:]
    outs = refs[-12:-9] if tiles else refs[-10:-9]
    step = pl.program_id(0)
    heads = vert_ref.shape[0]
    rows = own.shape[0]
    local_blocks = rows // BLK
    quarter = local_blocks // 4
    pair_rows = VMOST * BLK
    dtype = q_ref.dtype
    rank = ctx_ref[0]

    def fetch(t):
        return pltpu.make_async_copy(
            w_hbm.at[:, pl.ds(t * TILE, TILE)], weight.at[t], arrival.at[t]
        )

    @pl.when(step == 0)
    def _():
        copies = [
            pltpu.make_async_copy(x, kv_win.at[pl.ds(s * rows, rows), :], landed.at[s])
            for s, x in enumerate((kv_2, kv_1, own))
        ]
        copies += [
            pltpu.make_async_copy(
                x, kv_pool.at[pl.ds((s + 1) * pair_rows, pair_rows), :], landed.at[NEAR + s]
            )
            for s, x in enumerate(pairs)
        ]
        for copy in copies:
            copy.start()
        for t in range(tiles):
            fetch(t).start()
        key = lax.broadcasted_iota(jnp.int32, e_win.shape, 0)
        lane = lax.broadcasted_iota(jnp.int32, e_win.shape, 1)
        last = (key - (SPAN - 1) * BLK == lane - BLK) & (lane >= BLK)
        e_win[...] = jnp.where((key // BLK == lane) | last, 1.0, 0.0).astype(dtype)
        key = lax.broadcasted_iota(jnp.int32, e_pool.shape, 0)
        lane = lax.broadcasted_iota(jnp.int32, e_pool.shape, 1)
        e_pool[...] = jnp.where(key // BLK == lane, 1.0, 0.0).astype(dtype)
        blocks_ref[...] = pool_blocks(vert_ref[...], rank, slots, local_blocks)
        picked = picked_blocks(vert_ref[...], rank - (NEAR - 1), local_blocks)
        for copy in copies:
            copy.wait()
        for slot, block in enumerate(picked):
            kv_pool[slot * BLK : (slot + 1) * BLK, :] = kv_win[block, :]

    owner = tp_ref[0] ^ jnp.where(step == 0, flips[0], flips[1])
    lane = lax.broadcasted_iota(jnp.int32, (heads, LANES), 1)
    row = lax.broadcasted_iota(jnp.int32, (BLK, LANES), 0)
    above = lax.broadcasted_iota(jnp.int32, (BLK, LANES), 1) - BLK > row
    above = jnp.where(above, MASKED, 0.0).astype(jnp.float32)
    offset_ok = member(slash_ref[...], SPAN - 1 - lane)
    block = blocks_ref[...]
    pool_ok = member(vert_ref[...], block) & (block >= 0)
    contract = (((1,), (1,)), ((), ()))

    def with_ones(values):
        return jnp.concatenate([values, jnp.ones((values.shape[0], LANES), dtype)], axis=1)

    near, far_q, windows = [], [], []
    for u in range(quarter):
        here = owner * quarter + u
        q = q_ref[u * BLK : (u + 1) * BLK, :]
        q = jnp.concatenate([q[:, h * HS : (h + 1) * HS] for h in range(heads)], axis=0)
        first = rank * local_blocks + here - (SPAN - 1)
        seen = first + lane
        ok = (seen >= 0) & (offset_ok | member(vert_ref[...], seen))
        mask = jnp.where(ok | (lane >= SPAN), 0.0, MASKED).astype(jnp.float32)
        mask = (mask[:, None, :] + above[None]).reshape(heads * BLK, LANES).astype(dtype)
        far_mask = jnp.where(pool_ok & (block < first), 0.0, MASKED).astype(jnp.float32)
        far_mask = jnp.broadcast_to(far_mask[:, None, :], (heads, BLK, LANES))
        far_mask = far_mask.reshape(heads * BLK, LANES).astype(dtype)
        far_q.append(jnp.concatenate([q, far_mask], axis=1))
        window = pl.ds(pl.multiple_of((here + 1) * BLK, BLK), SPAN * BLK)
        windows.append(window)
        keys = jnp.concatenate([kv_win[window, :HS], e_win[...]], axis=1)
        near.append(
            lax.dot_general(
                jnp.concatenate([q, mask], axis=1),
                keys,
                contract,
                preferred_element_type=jnp.float32,
            )
        )
    far = lax.dot_general(
        jnp.concatenate(far_q, axis=0),
        jnp.concatenate([kv_pool[:, :HS], e_pool[...]], axis=1),
        contract,
        preferred_element_type=jnp.float32,
    )
    far_values = with_ones(kv_pool[:, HS:])
    for u in range(quarter):
        far_u = far[u * heads * BLK : (u + 1) * heads * BLK]
        top = jnp.maximum(
            jnp.max(near[u], axis=1, keepdims=True), jnp.max(far_u, axis=1, keepdims=True)
        )
        probs = jnp.exp2((near[u] - top) * EXP_SCALE).astype(dtype)
        values = with_ones(kv_win[windows[u], HS:])
        summed = jnp.dot(probs, values, preferred_element_type=jnp.float32)
        probs = jnp.exp2((far_u - top) * EXP_SCALE).astype(dtype)
        summed = summed + jnp.dot(probs, far_values, preferred_element_type=jnp.float32)
        out = (summed[:, :HS] / summed[:, HS:]).astype(dtype)
        at = pl.ds(pl.multiple_of((step * quarter + u) * BLK, BLK), BLK)
        for h in range(heads):
            attended[at, h * HS : (h + 1) * HS] = out[h * BLK : (h + 1) * BLK]

    @pl.when(step == pl.num_programs(0) - 1)
    def _():
        outs[0][...] = attended[...]
        half = attended.shape[0] // 2
        for t in range(tiles):
            fetch(t).wait()
            product = jnp.dot(attended[...], weight[t], preferred_element_type=jnp.float32)
            product = product.astype(dtype)
            outs[1][:, t * TILE : (t + 1) * TILE] = product[:half]
            outs[2][:, t * TILE : (t + 1) * TILE] = product[half:]


def attend(flips, tp, ctx, queries, vertical, slash, near_kv, pairs, slots, out_weight, tiles, after):
    width = queries.shape[1]
    rows = near_kv[0].shape[0]
    quarter = rows // 4
    steps = len(flips)
    dtype = queries.dtype
    far = len(slots) * VMOST * BLK

    def place(g, tp, ctx):
        return (tp[0] ^ jnp.where(g == 0, flips[0], flips[1]), 0)

    def whole(shape):
        return pl.BlockSpec(shape, lambda g, tp, ctx: (0,) * len(shape))

    out_shapes = [(steps * quarter, width)]
    if tiles:
        out_shapes += [(steps * quarter // 2, tiles * TILE)] * 2
    return pl.pallas_call(
        functools.partial(attend_kernel, slots, tiles, flips),
        out_shape=[jax.ShapeDtypeStruct(shape, dtype) for shape in out_shapes],
        grid_spec=pltpu.PrefetchScalarGridSpec(
            num_scalar_prefetch=2,
            grid=(steps,),
            in_specs=[pl.BlockSpec((quarter, width), place)]
            + [whole(vertical.shape), whole(slash.shape)]
            + [anywhere() for _ in [*near_kv, *pairs, out_weight, *after]],
            out_specs=[whole(shape) for shape in out_shapes],
            scratch_shapes=[
                pltpu.VMEM((NEAR * rows, 2 * HS), dtype),
                pltpu.VMEM((SPAN * BLK, LANES), dtype),
                pltpu.VMEM((far, 2 * HS), dtype),
                pltpu.VMEM((far, LANES), dtype),
                pltpu.VMEM((vertical.shape[0], LANES), jnp.int32),
                pltpu.VMEM((steps * quarter, width), dtype),
                pltpu.VMEM((max(tiles, 1), out_weight.shape[0], TILE), dtype),
                pltpu.SemaphoreType.DMA((max(tiles, 1),)),
                pltpu.SemaphoreType.DMA((NEAR + len(pairs),)),
            ],
        ),
        compiler_params=params(50),
        cost_estimate=SHORT,
        name="attend",
    )(tp, ctx, queries, vertical, slash, *near_kv, *pairs, out_weight, *after)


def project_kernel(first, a_ref, w_hbm, *refs):
    weight, arrival = refs[-2:]
    tiles = weight.shape[0]
    pieces = tiles // PIECE
    outs = refs[-2 - 2 * pieces : -2]
    half = outs[0].shape[0]

    def fetch(t):
        return pltpu.make_async_copy(
            w_hbm.at[:, pl.ds((first + t) * TILE, TILE)], weight.at[t], arrival.at[t]
        )

    for t in range(tiles):
        fetch(t).start()
    for t in range(tiles):
        fetch(t).wait()
        product = jnp.dot(a_ref[...], weight[t], preferred_element_type=jnp.float32)
        product = product.astype(a_ref.dtype)
        at = slice(t % PIECE * TILE, (t % PIECE + 1) * TILE)
        outs[t // PIECE][:, at] = product[:half]
        outs[pieces + t // PIECE][:, at] = product[half:]


def project(attended, out_weight, first, tiles, after):
    rows, depth = attended.shape
    pieces = tiles // PIECE
    part = jax.ShapeDtypeStruct((rows // 2, PIECE * TILE), attended.dtype)
    outs = pl.pallas_call(
        functools.partial(project_kernel, first),
        out_shape=[part] * (2 * pieces),
        in_specs=[vmem(), anywhere()] + [anywhere() for _ in after],
        out_specs=[vmem()] * (2 * pieces),
        scratch_shapes=[
            pltpu.VMEM((tiles, depth, TILE), attended.dtype),
            pltpu.SemaphoreType.DMA((tiles,)),
        ],
        compiler_params=params(50),
        cost_estimate=SHORT,
        name="project",
    )(attended, out_weight, *after)
    return outs[:pieces], outs[pieces:]


def add_kernel(*refs):
    out_ref = refs[-1]
    pieces = len(refs) // 2
    for t in range(pieces):
        total = refs[t][...].astype(jnp.float32) + refs[pieces + t][...].astype(jnp.float32)
        columns = total.shape[1]
        out_ref[:, t * columns : (t + 1) * columns] = total.astype(out_ref.dtype)


def add(keep, got):
    rows, columns = keep[0].shape
    return pl.pallas_call(
        add_kernel,
        out_shape=jax.ShapeDtypeStruct((rows, len(keep) * columns), keep[0].dtype),
        in_specs=[vmem()] * (2 * len(keep)),
        out_specs=vmem(),
        compiler_params=params(16),
        cost_estimate=SHORT,
        name="add",
    )(*keep, *got)


def finish_kernel(pieces, first, *refs):
    arrived_ref = refs[2 * pieces]
    out_ref, tiles_ref, sent = refs[-3:]
    copies = []
    for t in range(pieces * PIECE):
        part = slice(t % PIECE * TILE, (t % PIECE + 1) * TILE)
        total = refs[t // PIECE][:, part].astype(jnp.float32)
        total = total + refs[pieces + t // PIECE][:, part].astype(jnp.float32)
        total = total + arrived_ref[:, t * TILE : (t + 1) * TILE].astype(jnp.float32)
        tiles_ref[t] = total.astype(out_ref.dtype)
        columns = pl.ds((first + t) * TILE, TILE)
        copies.append(pltpu.make_async_copy(tiles_ref.at[t], out_ref.at[:, columns], sent.at[t]))
        copies[-1].start()
    for copy in copies:
        copy.wait()


def finish(keep, got, arrived, first, width, out):
    rows = arrived.shape[0]
    tiles = len(keep) * PIECE
    before = [] if out is None else [out]
    return pl.pallas_call(
        functools.partial(finish_kernel, len(keep), first),
        out_shape=jax.ShapeDtypeStruct((rows, width), arrived.dtype),
        in_specs=[vmem()] * (2 * len(keep) + 1) + [anywhere() for _ in before],
        out_specs=anywhere(),
        input_output_aliases={2 * len(keep) + 1: 0} if before else {},
        scratch_shapes=[
            pltpu.VMEM((tiles, rows, TILE), arrived.dtype),
            pltpu.SemaphoreType.DMA((tiles,)),
        ],
        compiler_params=params(16),
        cost_estimate=SHORT,
        name="finish",
    )(*keep, *got, arrived, *before)


def shards(ctx_size, queries, keys, values, out_weight, vertical, slash):
    local_blocks = queries.shape[0] // BLK
    assert ctx_size % 2 == 0 and (NEAR - 1) * local_blocks >= SPAN - 1
    ctx = jnp.reshape(lax.axis_index("ctx"), (1,)).astype(jnp.int32)
    tp = jnp.reshape(lax.axis_index("tp"), (1,)).astype(jnp.int32)

    def shifted(x, by):
        return lax.ppermute(x, "ctx", [(r, r + by) for r in range(ctx_size - by)])

    def swapped(x):
        return lax.ppermute(x, "ctx", [(r, r ^ 1) for r in range(ctx_size)])

    own, pair = pick(ctx, vertical, keys, values)
    near_kv = [own, shifted(own, 1), shifted(own, 2)]
    backs = range(4, ctx_size, 2)
    pairs = [shifted(pair, s) for s in backs]
    third = lax.ppermute(pair, "ctx", [(r, r + 3) for r in range(0, ctx_size - 3, 2)])
    pairs += [third] + [swapped(x) for x in pairs]
    slots = [(2, 2)] + [(s, s) for s in backs] + [(NOWHERE, 3)] + [(s - 1, s + 1) for s in backs]

    def sibling(x):
        return lax.ppermute(x, "tp", [(j, j ^ 1) for j in range(4)])

    def across(x):
        return lax.ppermute(x, "tp", [(j, j ^ 2) for j in range(4)])

    def attention(flips, tiles, after):
        return attend(
            flips, tp, ctx, queries, vertical, slash, near_kv, pairs, slots, out_weight, tiles, after
        )

    width = out_weight.shape[1]
    tiles = width // TILE
    attended, send, keep = attention((3, 2), HEAD, ())
    total = (keep.astype(jnp.float32) + sibling(send).astype(jnp.float32)).astype(keep.dtype)
    arrived = [across(total)]
    send, keep = project(attended, out_weight, HEAD, tiles - HEAD, (total,))
    total = add(keep, [sibling(x) for x in send])
    arrived.append(across(total))
    (attended,) = attention((1, 0), 0, (total,))
    send, keep = project(attended, out_weight, 0, tiles, (arrived[0],))
    got = [sibling(x) for x in send]
    cut = HEAD // PIECE
    out = finish(keep[:cut], got[:cut], arrived[0], 0, width, None)
    return finish(keep[cut:], got[cut:], arrived[1], HEAD, width, out)


def solution(mesh):
    assert mesh.shape["tp"] == 4
    return jax.shard_map(
        functools.partial(shards, mesh.shape["ctx"]),
        mesh=mesh,
        in_specs=(
            P("ctx", "tp"),
            P("ctx", "tp"),
            P("ctx", "tp"),
            P("tp", None),
            P("tp", None),
            P("tp", None),
        ),
        out_specs=P(("ctx", "tp"), None),
        check_vma=False,
    )
```

```python
import functools

import jax
import jax.numpy as jnp
from jax import lax
from jax.experimental import pallas as pl
from jax.experimental.pallas import tpu as pltpu
from jax.sharding import PartitionSpec as P

HS = 128
BLK = 64
SPAN = 16
VMOST = 2
NEAR = 3
LANES = 128
NOWHERE = 1 << 20
MASKED = -1e30
EXP_SCALE = 1.4426950408889634 / (HS**0.5)
TILE = 1024
HEAD = 4
REST = (1, 1, 1, 1)
MIB = 1024 * 1024


SHORT = pl.CostEstimate(flops=0, bytes_accessed=0, transcendentals=0)


def vmem():
    return pl.BlockSpec(memory_space=pltpu.VMEM)


def smem():
    return pl.BlockSpec(memory_space=pltpu.SMEM)


def anywhere():
    return pl.BlockSpec(memory_space=pl.ANY)


def params(mib):
    return pltpu.CompilerParams(vmem_limit_bytes=mib * MIB)


def picked_blocks(vertical, shard, local_blocks):
    block = vertical - shard * local_blocks
    block = jnp.where((block >= 0) & (block < local_blocks), block, local_blocks)
    first = jnp.min(block)
    second = jnp.min(jnp.where(block > first, block, local_blocks))
    return [
        pl.ds(pl.multiple_of(jnp.minimum(x, local_blocks - 1) * BLK, BLK), BLK)
        for x in (first, second)
    ]


def pick_kernel(rank_ref, vert_ref, k_ref, v_ref, both_ref, pair_ref):
    both_ref[:, :HS] = k_ref[...]
    both_ref[:, HS:] = v_ref[...]
    blocks = picked_blocks(vert_ref[...], rank_ref[0], k_ref.shape[0] // BLK)
    for slot, rows in enumerate(blocks):
        pair_ref[slot * BLK : (slot + 1) * BLK, :] = both_ref[rows, :]


def pick(rank, vertical, keys, values):
    return pl.pallas_call(
        pick_kernel,
        out_shape=(
            jax.ShapeDtypeStruct((keys.shape[0], 2 * HS), keys.dtype),
            jax.ShapeDtypeStruct((VMOST * BLK, 2 * HS), keys.dtype),
        ),
        in_specs=[smem(), vmem(), vmem(), vmem()],
        out_specs=(vmem(), vmem()),
        compiler_params=params(60),
        name="pick",
    )(rank, vertical, keys, values)


def hold(x, others):
    return pl.pallas_call(
        lambda *refs: None,
        out_shape=jax.ShapeDtypeStruct(x.shape, x.dtype),
        in_specs=[anywhere() for _ in [x, *others]],
        out_specs=anywhere(),
        input_output_aliases={0: 0},
        compiler_params=params(1),
        cost_estimate=SHORT,
        name="hold",
    )(x, *others)


def member(table, blocks):
    found = table[:, :1] == blocks
    for column in range(1, table.shape[1]):
        found = found | (table[:, column : column + 1] == blocks)
    return found


def pool_blocks(vertical, rank, slots, local_blocks):
    lane = lax.broadcasted_iota(jnp.int32, (vertical.shape[0], LANES), 1)
    shard = jnp.full(lane.shape, -1, jnp.int32)
    for slot, (even, odd) in enumerate(slots):
        back = jnp.where(rank & 1 == 1, odd, even)
        shard = jnp.where(lane // VMOST == slot, rank - back, shard)
    first = jnp.full((1, LANES), local_blocks, jnp.int32)
    second = first
    for j in reversed(range(local_blocks)):
        here = member(vertical, shard * local_blocks + j)
        here = jnp.max(jnp.where(here, 1, 0), axis=0, keepdims=True) == 1
        second = jnp.where(here, first, second)
        first = jnp.where(here, j, first)
    picked = jnp.where(lane % VMOST == 0, first, second)
    return jnp.where((picked < local_blocks) & (shard >= 0), shard * local_blocks + picked, -1)


def tables_kernel(slots, rank_ref, vert_ref, slash_ref, own_ref, table_ref, copy_ref):
    copy_ref[...] = own_ref[...]
    local_blocks = own_ref.shape[0] // BLK
    table_ref[0, :, : vert_ref.shape[1]] = vert_ref[...]
    table_ref[1, :, : slash_ref.shape[1]] = slash_ref[...]
    table_ref[2] = pool_blocks(vert_ref[...], rank_ref[0], slots, local_blocks)


def tables(rank, vertical, slash, own, slots):
    shape = (3, vertical.shape[0], LANES)
    return pl.pallas_call(
        functools.partial(tables_kernel, slots),
        out_shape=(
            jax.ShapeDtypeStruct(shape, jnp.int32),
            jax.ShapeDtypeStruct(own.shape, own.dtype),
        ),
        in_specs=[smem(), vmem(), vmem(), vmem()],
        out_specs=(vmem(), vmem()),
        compiler_params=params(4),
        cost_estimate=SHORT,
        name="tables",
    )(rank, vertical, slash, own)


def attend_kernel(
    slots, tiles, sizes, flips, tp_ref, ctx_ref, q_ref, table_ref, own, kv_1, kv_2, *refs
):
    pairs = refs[: len(slots) - 1]
    w_hbm = refs[len(slots) - 1]
    kv_win, e_win, kv_pool, e_pool, attended, weight, arrival, landed = refs[-8:]
    outs = refs[-11:-8] if tiles else refs[-9:-8]
    step = pl.program_id(0)
    heads = table_ref.shape[1]
    rows = own.shape[0]
    local_blocks = rows // BLK
    quarter = local_blocks // 4
    pair_rows = VMOST * BLK
    dtype = q_ref.dtype
    rank = ctx_ref[0]
    vert = table_ref[0][:, : sizes[0]]
    slash = table_ref[1][:, : sizes[1]]
    block = table_ref[2]

    def fetch(t):
        return pltpu.make_async_copy(
            w_hbm.at[:, pl.ds(t * TILE, TILE)], weight.at[t], arrival.at[t]
        )

    @pl.when(step == 0)
    def _():
        copies = [
            pltpu.make_async_copy(x, kv_win.at[pl.ds(s * rows, rows), :], landed.at[s])
            for s, x in enumerate((kv_2, kv_1, own))
        ]
        copies += [
            pltpu.make_async_copy(
                x, kv_pool.at[pl.ds((s + 1) * pair_rows, pair_rows), :], landed.at[NEAR + s]
            )
            for s, x in enumerate(pairs)
        ]
        for copy in copies:
            copy.start()
        for t in range(tiles):
            fetch(t).start()
        key = lax.broadcasted_iota(jnp.int32, e_win.shape, 0)
        lane = lax.broadcasted_iota(jnp.int32, e_win.shape, 1)
        last = (key - (SPAN - 1) * BLK == lane - BLK) & (lane >= BLK)
        e_win[...] = jnp.where((key // BLK == lane) | last, 1.0, 0.0).astype(dtype)
        key = lax.broadcasted_iota(jnp.int32, e_pool.shape, 0)
        lane = lax.broadcasted_iota(jnp.int32, e_pool.shape, 1)
        e_pool[...] = jnp.where(key // BLK == lane, 1.0, 0.0).astype(dtype)
        picked = picked_blocks(vert, rank - (NEAR - 1), local_blocks)
        for copy in copies:
            copy.wait()
        for slot, block in enumerate(picked):
            kv_pool[slot * BLK : (slot + 1) * BLK, :] = kv_win[block, :]

    owner = tp_ref[0] ^ jnp.where(step == 0, flips[0], flips[1])
    lane = lax.broadcasted_iota(jnp.int32, (heads, LANES), 1)
    row = lax.broadcasted_iota(jnp.int32, (BLK, LANES), 0)
    above = lax.broadcasted_iota(jnp.int32, (BLK, LANES), 1) - BLK > row
    above = jnp.where(above, MASKED, 0.0).astype(jnp.float32)
    offset_ok = member(slash, SPAN - 1 - lane)
    pool_ok = member(vert, block) & (block >= 0)
    contract = (((1,), (1,)), ((), ()))

    def with_ones(values):
        return jnp.concatenate([values, jnp.ones((values.shape[0], LANES), dtype)], axis=1)

    near, far_q, windows = [], [], []
    for u in range(quarter):
        here = owner * quarter + u
        q = q_ref[u * BLK : (u + 1) * BLK, :]
        q = jnp.concatenate([q[:, h * HS : (h + 1) * HS] for h in range(heads)], axis=0)
        first = rank * local_blocks + here - (SPAN - 1)
        seen = first + lane
        ok = (seen >= 0) & (offset_ok | member(vert, seen))
        mask = jnp.where(ok | (lane >= SPAN), 0.0, MASKED).astype(jnp.float32)
        mask = (mask[:, None, :] + above[None]).reshape(heads * BLK, LANES).astype(dtype)
        far_mask = jnp.where(pool_ok & (block < first), 0.0, MASKED).astype(jnp.float32)
        far_mask = jnp.broadcast_to(far_mask[:, None, :], (heads, BLK, LANES))
        far_mask = far_mask.reshape(heads * BLK, LANES).astype(dtype)
        far_q.append(jnp.concatenate([q, far_mask], axis=1))
        window = pl.ds(pl.multiple_of((here + 1) * BLK, BLK), SPAN * BLK)
        windows.append(window)
        keys = jnp.concatenate([kv_win[window, :HS], e_win[...]], axis=1)
        near.append(
            lax.dot_general(
                jnp.concatenate([q, mask], axis=1),
                keys,
                contract,
                preferred_element_type=jnp.float32,
            )
        )
    far = lax.dot_general(
        jnp.concatenate(far_q, axis=0),
        jnp.concatenate([kv_pool[:, :HS], e_pool[...]], axis=1),
        contract,
        preferred_element_type=jnp.float32,
    )
    far_values = with_ones(kv_pool[:, HS:])
    for u in range(quarter):
        far_u = far[u * heads * BLK : (u + 1) * heads * BLK]
        top = jnp.maximum(
            jnp.max(near[u], axis=1, keepdims=True), jnp.max(far_u, axis=1, keepdims=True)
        )
        probs = jnp.exp2((near[u] - top) * EXP_SCALE).astype(dtype)
        values = with_ones(kv_win[windows[u], HS:])
        summed = jnp.dot(probs, values, preferred_element_type=jnp.float32)
        probs = jnp.exp2((far_u - top) * EXP_SCALE).astype(dtype)
        summed = summed + jnp.dot(probs, far_values, preferred_element_type=jnp.float32)
        out = (summed[:, :HS] / summed[:, HS:]).astype(dtype)
        at = pl.ds(pl.multiple_of((step * quarter + u) * BLK, BLK), BLK)
        for h in range(heads):
            attended[at, h * HS : (h + 1) * HS] = out[h * BLK : (h + 1) * BLK]

    @pl.when(step == pl.num_programs(0) - 1)
    def _():
        outs[0][...] = attended[...]
        half = attended.shape[0] // 2
        for t in range(tiles):
            fetch(t).wait()
            product = jnp.dot(attended[...], weight[t], preferred_element_type=jnp.float32)
            product = product.astype(dtype)
            outs[1][:, t * TILE : (t + 1) * TILE] = product[:half]
            outs[2][:, t * TILE : (t + 1) * TILE] = product[half:]


def attend(flips, tp, ctx, queries, table, near_kv, pairs, slots, sizes, out_weight, tiles, after):
    width = queries.shape[1]
    rows = near_kv[0].shape[0]
    quarter = rows // 4
    steps = len(flips)
    dtype = queries.dtype
    far = len(slots) * VMOST * BLK

    def place(g, tp, ctx):
        return (tp[0] ^ jnp.where(g == 0, flips[0], flips[1]), 0)

    def whole(shape):
        return pl.BlockSpec(shape, lambda g, tp, ctx: (0,) * len(shape))

    out_shapes = [(steps * quarter, width)]
    if tiles:
        out_shapes += [(steps * quarter // 2, tiles * TILE)] * 2
    return pl.pallas_call(
        functools.partial(attend_kernel, slots, tiles, sizes, flips),
        out_shape=[jax.ShapeDtypeStruct(shape, dtype) for shape in out_shapes],
        grid_spec=pltpu.PrefetchScalarGridSpec(
            num_scalar_prefetch=2,
            grid=(steps,),
            in_specs=[pl.BlockSpec((quarter, width), place)]
            + [whole(table.shape)]
            + [anywhere() for _ in [*near_kv, *pairs, out_weight, *after]],
            out_specs=[whole(shape) for shape in out_shapes],
            scratch_shapes=[
                pltpu.VMEM((NEAR * rows, 2 * HS), dtype),
                pltpu.VMEM((SPAN * BLK, LANES), dtype),
                pltpu.VMEM((far, 2 * HS), dtype),
                pltpu.VMEM((far, LANES), dtype),
                pltpu.VMEM((steps * quarter, width), dtype),
                pltpu.VMEM((max(tiles, 1), out_weight.shape[0], TILE), dtype),
                pltpu.SemaphoreType.DMA((max(tiles, 1),)),
                pltpu.SemaphoreType.DMA((NEAR + len(pairs),)),
            ],
        ),
        compiler_params=params(50),
        cost_estimate=SHORT,
        name="attend",
    )(tp, ctx, queries, table, *near_kv, *pairs, out_weight, *after)


def project_kernel(first, sizes, a_ref, w_hbm, *refs):
    weight, arrival = refs[-2:]
    outs = refs[-2 - 2 * len(sizes) : -2]
    half = outs[0].shape[0]

    def fetch(t):
        return pltpu.make_async_copy(
            w_hbm.at[:, pl.ds((first + t) * TILE, TILE)], weight.at[t], arrival.at[t]
        )

    for t in range(sum(sizes)):
        fetch(t).start()
    t = 0
    for piece, size in enumerate(sizes):
        for place in range(size):
            fetch(t).wait()
            product = jnp.dot(a_ref[...], weight[t], preferred_element_type=jnp.float32)
            product = product.astype(a_ref.dtype)
            at = slice(place * TILE, (place + 1) * TILE)
            outs[piece][:, at] = product[:half]
            outs[len(sizes) + piece][:, at] = product[half:]
            t += 1


def project(attended, out_weight, first, sizes, after):
    rows, depth = attended.shape
    parts = [
        jax.ShapeDtypeStruct((rows // 2, size * TILE), attended.dtype) for size in sizes
    ]
    outs = pl.pallas_call(
        functools.partial(project_kernel, first, sizes),
        out_shape=parts + parts,
        in_specs=[vmem(), anywhere()] + [anywhere() for _ in after],
        out_specs=[vmem()] * (2 * len(sizes)),
        scratch_shapes=[
            pltpu.VMEM((sum(sizes), depth, TILE), attended.dtype),
            pltpu.SemaphoreType.DMA((sum(sizes),)),
        ],
        compiler_params=params(50),
        cost_estimate=SHORT,
        name="project",
    )(attended, out_weight, *after)
    return outs[: len(sizes)], outs[len(sizes) :]


def add_kernel(*refs):
    out_ref = refs[-1]
    pieces = len(refs) // 2
    first = 0
    for t in range(pieces):
        total = refs[t][...].astype(jnp.float32) + refs[pieces + t][...].astype(jnp.float32)
        last = first + total.shape[1]
        out_ref[:, first:last] = total.astype(out_ref.dtype)
        first = last


def add(keep, got):
    rows, columns = keep[0].shape[0], sum(x.shape[1] for x in keep)
    return pl.pallas_call(
        add_kernel,
        out_shape=jax.ShapeDtypeStruct((rows, columns), keep[0].dtype),
        in_specs=[vmem()] * (2 * len(keep)),
        out_specs=vmem(),
        compiler_params=params(16),
        cost_estimate=SHORT,
        name="add",
    )(*keep, *got)


def finish_kernel(pieces, first, *refs):
    arrived_ref = refs[2 * pieces]
    out_ref, tiles_ref, sent = refs[-3:]
    copies = []
    for t in range(pieces):
        total = refs[t][...].astype(jnp.float32) + refs[pieces + t][...].astype(jnp.float32)
        total = total + arrived_ref[:, t * TILE : (t + 1) * TILE].astype(jnp.float32)
        tiles_ref[t] = total.astype(out_ref.dtype)
        columns = pl.ds((first + t) * TILE, TILE)
        copies.append(pltpu.make_async_copy(tiles_ref.at[t], out_ref.at[:, columns], sent.at[t]))
        copies[-1].start()
    for copy in copies:
        copy.wait()


def finish(keep, got, arrived, first, width, out):
    rows = arrived.shape[0]
    tiles = len(keep)
    before = [] if out is None else [out]
    return pl.pallas_call(
        functools.partial(finish_kernel, len(keep), first),
        out_shape=jax.ShapeDtypeStruct((rows, width), arrived.dtype),
        in_specs=[vmem()] * (2 * len(keep) + 1) + [anywhere() for _ in before],
        out_specs=anywhere(),
        input_output_aliases={2 * len(keep) + 1: 0} if before else {},
        scratch_shapes=[
            pltpu.VMEM((tiles, rows, TILE), arrived.dtype),
            pltpu.SemaphoreType.DMA((tiles,)),
        ],
        compiler_params=params(16),
        cost_estimate=SHORT,
        name="finish",
    )(*keep, *got, arrived, *before)


def shards(ctx_size, queries, keys, values, out_weight, vertical, slash):
    local_blocks = queries.shape[0] // BLK
    assert ctx_size % 2 == 0 and (NEAR - 1) * local_blocks >= SPAN - 1
    ctx = jnp.reshape(lax.axis_index("ctx"), (1,)).astype(jnp.int32)
    tp = jnp.reshape(lax.axis_index("tp"), (1,)).astype(jnp.int32)

    def shifted(x, by):
        return lax.ppermute(x, "ctx", [(r, r + by) for r in range(ctx_size - by)])

    def swapped(x):
        return lax.ppermute(x, "ctx", [(r, r ^ 1) for r in range(ctx_size)])

    own, pair = pick(ctx, vertical, keys, values)
    backs = range(4, ctx_size, 2)
    pairs = [shifted(pair, s) for s in backs]
    third = lax.ppermute(pair, "ctx", [(r, r + 3) for r in range(0, ctx_size - 3, 2)])
    slots = [(2, 2)] + [(s, s) for s in backs] + [(NOWHERE, 3)] + [(s - 1, s + 1) for s in backs]
    table, own_copy = tables(ctx, vertical, slash, own, slots)
    own = hold(own, [*pairs, third, table])
    near_kv = [own_copy, shifted(own, 1), shifted(own, 2)]
    pairs += [third] + [swapped(x) for x in pairs]

    def sibling(x):
        return lax.ppermute(x, "tp", [(j, j ^ 1) for j in range(4)])

    def across(x):
        return lax.ppermute(x, "tp", [(j, j ^ 2) for j in range(4)])

    def attention(flips, tiles, after):
        sizes = (vertical.shape[1], slash.shape[1])
        return attend(
            flips, tp, ctx, queries, table, near_kv, pairs, slots, sizes, out_weight, tiles, after
        )

    width = out_weight.shape[1]
    tiles = width // TILE
    assert HEAD + sum(REST) == tiles
    attended, send, keep = attention((3, 2), HEAD, ())
    total = (keep.astype(jnp.float32) + sibling(send).astype(jnp.float32)).astype(keep.dtype)
    arrived = [across(total)]
    send, keep = project(attended, out_weight, HEAD, REST, (total,))
    total = add(keep, [sibling(x) for x in send])
    arrived.append(across(total))
    (attended,) = attention((1, 0), 0, (total,))
    send, keep = project(attended, out_weight, 0, (1,) * tiles, (arrived[0],))
    got = [sibling(x) for x in send]
    out = finish(keep[:HEAD], got[:HEAD], arrived[0], 0, width, None)
    return finish(keep[HEAD:], got[HEAD:], arrived[1], HEAD, width, out)


def solution(mesh):
    assert mesh.shape["tp"] == 4
    return jax.shard_map(
        functools.partial(shards, mesh.shape["ctx"]),
        mesh=mesh,
        in_specs=(
            P("ctx", "tp"),
            P("ctx", "tp"),
            P("ctx", "tp"),
            P("tp", None),
            P("tp", None),
            P("tp", None),
        ),
        out_specs=P(("ctx", "tp"), None),
        check_vma=False,
    )
```

```python
import functools

import jax
import jax.numpy as jnp
from jax import lax
from jax.experimental import pallas as pl
from jax.experimental.pallas import tpu as pltpu
from jax.sharding import PartitionSpec as P

HS = 128
BLK = 64
SPAN = 16
VMOST = 2
NEAR = 3
LANES = 128
MASKED = -1e30
EXP_SCALE = 1.4426950408889634 / (HS**0.5)
TILE = 1024
ACROSS = (3, 4, 1)
MIB = 1024 * 1024


SHORT = pl.CostEstimate(flops=0, bytes_accessed=0, transcendentals=0)


def vmem():
    return pl.BlockSpec(memory_space=pltpu.VMEM)


def smem():
    return pl.BlockSpec(memory_space=pltpu.SMEM)


def anywhere():
    return pl.BlockSpec(memory_space=pl.ANY)


def params(mib):
    return pltpu.CompilerParams(vmem_limit_bytes=mib * MIB)


def picked_blocks(vertical, shard, local_blocks):
    block = vertical - shard * local_blocks
    block = jnp.where((block >= 0) & (block < local_blocks), block, local_blocks)
    first = jnp.min(block)
    second = jnp.min(jnp.where(block > first, block, local_blocks))
    return [
        pl.ds(pl.multiple_of(jnp.minimum(x, local_blocks - 1) * BLK, BLK), BLK)
        for x in (first, second)
    ]


def pick_kernel(rank_ref, vert_ref, k_ref, v_ref, both_ref, pair_ref):
    both_ref[:, :HS] = k_ref[...]
    both_ref[:, HS:] = v_ref[...]
    blocks = picked_blocks(vert_ref[...], rank_ref[0], k_ref.shape[0] // BLK)
    for slot, rows in enumerate(blocks):
        picked = both_ref[rows, :]
        for copy in range(pair_ref.shape[0]):
            pair_ref[copy, slot * BLK : (slot + 1) * BLK, :] = picked


def pick(rank, vertical, keys, values, copies):
    return pl.pallas_call(
        pick_kernel,
        out_shape=(
            jax.ShapeDtypeStruct((keys.shape[0], 2 * HS), keys.dtype),
            jax.ShapeDtypeStruct((copies, VMOST * BLK, 2 * HS), keys.dtype),
        ),
        in_specs=[smem(), vmem(), vmem(), vmem()],
        out_specs=(vmem(), vmem()),
        compiler_params=params(60),
        name="pick",
    )(rank, vertical, keys, values)


def member(table, blocks):
    found = table[:, :1] == blocks
    for column in range(1, table.shape[1]):
        found = found | (table[:, column : column + 1] == blocks)
    return found


def pool_blocks(vertical, rank, slots, local_blocks):
    lane = lax.broadcasted_iota(jnp.int32, (vertical.shape[0], LANES), 1)
    slot = lane // VMOST
    shard = jnp.where(slot < slots, 2 * slot + (rank & 1), 2 * (slot - slots) + 1 - (rank & 1))
    shard = jnp.where(slot < 2 * slots, shard, -1)
    first = jnp.full((1, LANES), local_blocks, jnp.int32)
    second = first
    for j in reversed(range(local_blocks)):
        here = member(vertical, shard * local_blocks + j)
        here = jnp.max(jnp.where(here, 1, 0), axis=0, keepdims=True) == 1
        second = jnp.where(here, first, second)
        first = jnp.where(here, j, first)
    picked = jnp.where(lane % VMOST == 0, first, second)
    return jnp.where((picked < local_blocks) & (shard >= 0), shard * local_blocks + picked, -1)


def tables_kernel(slots, rank_ref, vert_ref, slash_ref, own_ref, table_ref, copy_ref):
    copy_ref[...] = own_ref[...]
    local_blocks = own_ref.shape[0] // BLK
    table_ref[0, :, : vert_ref.shape[1]] = vert_ref[...]
    table_ref[1, :, : slash_ref.shape[1]] = slash_ref[...]
    table_ref[2] = pool_blocks(vert_ref[...], rank_ref[0], slots, local_blocks)


def tables(rank, vertical, slash, own, slots):
    shape = (3, vertical.shape[0], LANES)
    return pl.pallas_call(
        functools.partial(tables_kernel, slots),
        out_shape=(
            jax.ShapeDtypeStruct(shape, jnp.int32),
            jax.ShapeDtypeStruct(own.shape, own.dtype),
        ),
        in_specs=[smem(), vmem(), vmem(), vmem()],
        out_specs=(vmem(), vmem()),
        compiler_params=params(4),
        cost_estimate=SHORT,
        name="tables",
    )(rank, vertical, slash, own)


def attend_kernel(
    slots, tiles, sizes, flips, tp_ref, ctx_ref, q_ref, table_ref, own, kv_1, kv_2, *refs
):
    pairs = refs[:2]
    w_hbm = refs[2]
    kv_win, e_win, kv_pool, e_pool, attended, weight, arrival, landed = refs[-8:]
    outs = refs[-11:-8] if tiles else refs[-9:-8]
    step = pl.program_id(0)
    heads = table_ref.shape[1]
    rows = own.shape[0]
    local_blocks = rows // BLK
    quarter = local_blocks // 4
    far_rows = e_pool.shape[0]
    dtype = q_ref.dtype
    rank = ctx_ref[0]
    vert = table_ref[0][:, : sizes[0]]
    slash = table_ref[1][:, : sizes[1]]
    block = table_ref[2]

    def fetch(t):
        return pltpu.make_async_copy(
            w_hbm.at[:, pl.ds(t * TILE, TILE)], weight.at[t], arrival.at[t]
        )

    @pl.when(step == 0)
    def _():
        copies = [
            pltpu.make_async_copy(x, kv_win.at[pl.ds(s * rows, rows), :], landed.at[s])
            for s, x in enumerate((kv_2, kv_1, own))
        ]
        copies += [
            pltpu.make_async_copy(
                x.at[pl.ds(0, slots)], kv_pool.at[pl.ds(p * slots, slots)], landed.at[NEAR + p]
            )
            for p, x in enumerate(pairs)
        ]
        for copy in copies:
            copy.start()
        for t in range(tiles):
            fetch(t).start()
        key = lax.broadcasted_iota(jnp.int32, e_win.shape, 0)
        lane = lax.broadcasted_iota(jnp.int32, e_win.shape, 1)
        last = (key - (SPAN - 1) * BLK == lane - BLK) & (lane >= BLK)
        e_win[...] = jnp.where((key // BLK == lane) | last, 1.0, 0.0).astype(dtype)
        key = lax.broadcasted_iota(jnp.int32, e_pool.shape, 0)
        lane = lax.broadcasted_iota(jnp.int32, e_pool.shape, 1)
        e_pool[...] = jnp.where(key // BLK == lane, 1.0, 0.0).astype(dtype)
        for copy in copies:
            copy.wait()

    owner = tp_ref[0] ^ jnp.where(step == 0, flips[0], flips[1])
    lane = lax.broadcasted_iota(jnp.int32, (heads, LANES), 1)
    row = lax.broadcasted_iota(jnp.int32, (BLK, LANES), 0)
    above = lax.broadcasted_iota(jnp.int32, (BLK, LANES), 1) - BLK > row
    above = jnp.where(above, MASKED, 0.0).astype(jnp.float32)
    offset_ok = member(slash, SPAN - 1 - lane)
    pool_ok = member(vert, block) & (block >= 0)
    contract = (((1,), (1,)), ((), ()))

    def with_ones(values):
        return jnp.concatenate([values, jnp.ones((values.shape[0], LANES), dtype)], axis=1)

    near, far_q, windows = [], [], []
    for u in range(quarter):
        here = owner * quarter + u
        q = q_ref[u * BLK : (u + 1) * BLK, :]
        q = jnp.concatenate([q[:, h * HS : (h + 1) * HS] for h in range(heads)], axis=0)
        first = rank * local_blocks + here - (SPAN - 1)
        seen = first + lane
        ok = (seen >= 0) & (offset_ok | member(vert, seen))
        mask = jnp.where(ok | (lane >= SPAN), 0.0, MASKED).astype(jnp.float32)
        mask = (mask[:, None, :] + above[None]).reshape(heads * BLK, LANES).astype(dtype)
        far_mask = jnp.where(pool_ok & (block < first), 0.0, MASKED).astype(jnp.float32)
        far_mask = jnp.broadcast_to(far_mask[:, None, :], (heads, BLK, LANES))
        far_mask = far_mask.reshape(heads * BLK, LANES).astype(dtype)
        far_q.append(jnp.concatenate([q, far_mask], axis=1))
        window = pl.ds(pl.multiple_of((here + 1) * BLK, BLK), SPAN * BLK)
        windows.append(window)
        keys = jnp.concatenate([kv_win[window, :HS], e_win[...]], axis=1)
        near.append(
            lax.dot_general(
                jnp.concatenate([q, mask], axis=1),
                keys,
                contract,
                preferred_element_type=jnp.float32,
            )
        )
    far = lax.dot_general(
        jnp.concatenate(far_q, axis=0),
        jnp.concatenate([kv_pool[:, :, :HS].reshape(far_rows, HS), e_pool[...]], axis=1),
        contract,
        preferred_element_type=jnp.float32,
    )
    far_values = with_ones(kv_pool[:, :, HS:].reshape(far_rows, HS))
    for u in range(quarter):
        far_u = far[u * heads * BLK : (u + 1) * heads * BLK]
        top = jnp.maximum(
            jnp.max(near[u], axis=1, keepdims=True), jnp.max(far_u, axis=1, keepdims=True)
        )
        probs = jnp.exp2((near[u] - top) * EXP_SCALE).astype(dtype)
        values = with_ones(kv_win[windows[u], HS:])
        summed = jnp.dot(probs, values, preferred_element_type=jnp.float32)
        probs = jnp.exp2((far_u - top) * EXP_SCALE).astype(dtype)
        summed = summed + jnp.dot(probs, far_values, preferred_element_type=jnp.float32)
        out = (summed[:, :HS] / summed[:, HS:]).astype(dtype)
        at = pl.ds(pl.multiple_of((step * quarter + u) * BLK, BLK), BLK)
        for h in range(heads):
            attended[at, h * HS : (h + 1) * HS] = out[h * BLK : (h + 1) * BLK]

    @pl.when(step == pl.num_programs(0) - 1)
    def _():
        outs[0][...] = attended[...]
        half = attended.shape[0] // 2
        for t in range(tiles):
            fetch(t).wait()
            product = jnp.dot(attended[...], weight[t], preferred_element_type=jnp.float32)
            product = product.astype(dtype)
            outs[1][:, t * TILE : (t + 1) * TILE] = product[:half]
            outs[2][:, t * TILE : (t + 1) * TILE] = product[half:]


def attend(flips, tp, ctx, queries, table, near_kv, pairs, sizes, out_weight, tiles, after):
    width = queries.shape[1]
    rows = near_kv[0].shape[0]
    quarter = rows // 4
    steps = len(flips)
    slots = pairs[1].shape[0]
    dtype = queries.dtype
    far = 2 * slots * VMOST * BLK

    def place(g, tp, ctx):
        return (tp[0] ^ jnp.where(g == 0, flips[0], flips[1]), 0)

    def whole(shape):
        return pl.BlockSpec(shape, lambda g, tp, ctx: (0,) * len(shape))

    out_shapes = [(steps * quarter, width)]
    if tiles:
        out_shapes += [(steps * quarter // 2, tiles * TILE)] * 2
    return pl.pallas_call(
        functools.partial(attend_kernel, slots, tiles, sizes, flips),
        out_shape=[jax.ShapeDtypeStruct(shape, dtype) for shape in out_shapes],
        grid_spec=pltpu.PrefetchScalarGridSpec(
            num_scalar_prefetch=2,
            grid=(steps,),
            in_specs=[pl.BlockSpec((quarter, width), place)]
            + [whole(table.shape)]
            + [anywhere() for _ in [*near_kv, *pairs, out_weight, *after]],
            out_specs=[whole(shape) for shape in out_shapes],
            scratch_shapes=[
                pltpu.VMEM((NEAR * rows, 2 * HS), dtype),
                pltpu.VMEM((SPAN * BLK, LANES), dtype),
                pltpu.VMEM((2 * slots, VMOST * BLK, 2 * HS), dtype),
                pltpu.VMEM((far, LANES), dtype),
                pltpu.VMEM((steps * quarter, width), dtype),
                pltpu.VMEM((max(tiles, 1), out_weight.shape[0], TILE), dtype),
                pltpu.SemaphoreType.DMA((max(tiles, 1),)),
                pltpu.SemaphoreType.DMA((NEAR + 2,)),
            ],
        ),
        compiler_params=params(50),
        cost_estimate=SHORT,
        name="attend",
    )(tp, ctx, queries, table, *near_kv, *pairs, out_weight, *after)


def project_kernel(first, a_ref, w_hbm, *refs):
    weight, arrival = refs[-2:]
    tiles = weight.shape[0]
    outs = refs[-2 - 2 * tiles : -2]
    half = outs[0].shape[0]

    def fetch(t):
        return pltpu.make_async_copy(
            w_hbm.at[:, pl.ds((first + t) * TILE, TILE)], weight.at[t], arrival.at[t]
        )

    for t in range(tiles):
        fetch(t).start()
    for t in range(tiles):
        fetch(t).wait()
        product = jnp.dot(a_ref[...], weight[t], preferred_element_type=jnp.float32)
        product = product.astype(a_ref.dtype)
        outs[t][...] = product[:half]
        outs[tiles + t][...] = product[half:]


def project(attended, out_weight, first, tiles, after):
    rows, depth = attended.shape
    part = jax.ShapeDtypeStruct((rows // 2, TILE), attended.dtype)
    outs = pl.pallas_call(
        functools.partial(project_kernel, first),
        out_shape=[part] * (2 * tiles),
        in_specs=[vmem(), anywhere()] + [anywhere() for _ in after],
        out_specs=[vmem()] * (2 * tiles),
        scratch_shapes=[
            pltpu.VMEM((tiles, depth, TILE), attended.dtype),
            pltpu.SemaphoreType.DMA((tiles,)),
        ],
        compiler_params=params(50),
        cost_estimate=SHORT,
        name="project",
    )(attended, out_weight, *after)
    return outs[:tiles], outs[tiles:]


def add_kernel(*refs):
    out_ref = refs[-1]
    pieces = len(refs) // 2
    first = 0
    for t in range(pieces):
        total = refs[t][...].astype(jnp.float32) + refs[pieces + t][...].astype(jnp.float32)
        last = first + total.shape[1]
        out_ref[:, first:last] = total.astype(out_ref.dtype)
        first = last


def add(keep, got):
    rows, columns = keep[0].shape[0], sum(x.shape[1] for x in keep)
    return pl.pallas_call(
        add_kernel,
        out_shape=jax.ShapeDtypeStruct((rows, columns), keep[0].dtype),
        in_specs=[vmem()] * (2 * len(keep)),
        out_specs=vmem(),
        compiler_params=params(16),
        cost_estimate=SHORT,
        name="add",
    )(*keep, *got)


def finish_kernel(pieces, first, *refs):
    arrived_ref = refs[2 * pieces]
    out_ref, tiles_ref, sent = refs[-3:]
    copies = []
    for t in range(pieces):
        total = refs[t][...].astype(jnp.float32) + refs[pieces + t][...].astype(jnp.float32)
        total = total + arrived_ref[:, t * TILE : (t + 1) * TILE].astype(jnp.float32)
        tiles_ref[t] = total.astype(out_ref.dtype)
        columns = pl.ds((first + t) * TILE, TILE)
        copies.append(pltpu.make_async_copy(tiles_ref.at[t], out_ref.at[:, columns], sent.at[t]))
        copies[-1].start()
    for copy in copies:
        copy.wait()


def finish(keep, got, arrived, first, width, out):
    rows = arrived.shape[0]
    tiles = len(keep)
    before = [] if out is None else [out]
    return pl.pallas_call(
        functools.partial(finish_kernel, len(keep), first),
        out_shape=jax.ShapeDtypeStruct((rows, width), arrived.dtype),
        in_specs=[vmem()] * (2 * len(keep) + 1) + [anywhere() for _ in before],
        out_specs=anywhere(),
        input_output_aliases={2 * len(keep) + 1: 0} if before else {},
        scratch_shapes=[
            pltpu.VMEM((tiles, rows, TILE), arrived.dtype),
            pltpu.SemaphoreType.DMA((tiles,)),
        ],
        compiler_params=params(16),
        cost_estimate=SHORT,
        name="finish",
    )(*keep, *got, arrived, *before)


def shards(ctx_size, queries, keys, values, out_weight, vertical, slash):
    local_blocks = queries.shape[0] // BLK
    assert ctx_size % 2 == 0 and (NEAR - 1) * local_blocks >= SPAN - 1
    ctx = jnp.reshape(lax.axis_index("ctx"), (1,)).astype(jnp.int32)
    tp = jnp.reshape(lax.axis_index("tp"), (1,)).astype(jnp.int32)

    def shifted(x, by):
        return lax.ppermute(x, "ctx", [(r, r + by) for r in range(ctx_size - by)])

    half = ctx_size // 2
    own, pair = pick(ctx, vertical, keys, values, half)
    parities = [list(range(odd, ctx_size, 2)) for odd in (0, 1)]
    pairs = [lax.all_to_all(pair, "ctx", 0, 0, axis_index_groups=parities, tiled=True)]
    needed = pairs[0][: half - 1]
    pairs.append(lax.ppermute(needed, "ctx", [(r, r ^ 1) for r in range(ctx_size)]))
    table, own_copy = tables(ctx, vertical, slash, own, half - 1)
    near_kv = [own_copy, shifted(own, 1), shifted(own, 2)]

    def sibling(x):
        return lax.ppermute(x, "tp", [(j, j ^ 1) for j in range(4)])

    def across(x):
        return lax.ppermute(x, "tp", [(j, j ^ 2) for j in range(4)])

    def attention(flips, tiles, after):
        sizes = (vertical.shape[1], slash.shape[1])
        return attend(
            flips, tp, ctx, queries, table, near_kv, pairs, sizes, out_weight, tiles, after
        )

    width = out_weight.shape[1]
    tiles = width // TILE
    assert sum(ACROSS) == tiles
    starts = [sum(ACROSS[:n]) for n in range(len(ACROSS))]

    def send_chunk(chunk, after):
        send, keep = project(attended, out_weight, starts[chunk], ACROSS[chunk], after)
        return add(keep, [sibling(x) for x in send])

    attended, send, keep = attention((3, 2), ACROSS[0], ())
    total = (keep.astype(jnp.float32) + sibling(send).astype(jnp.float32)).astype(keep.dtype)
    arrived = [across(total)]
    total = send_chunk(1, (total,))
    arrived.append(across(total))
    (own_attended,) = attention((1, 0), 0, (total,))
    total = send_chunk(2, (own_attended,))
    arrived.append(across(total))
    send, keep = project(own_attended, out_weight, 0, tiles, (total, arrived[0]))
    got = [sibling(x) for x in send]
    out = None
    for part, first, count in zip(arrived, starts, ACROSS):
        at = slice(first, first + count)
        out = finish(keep[at], got[at], part, first, width, out)
    return out


def solution(mesh):
    assert mesh.shape["tp"] == 4
    return jax.shard_map(
        functools.partial(shards, mesh.shape["ctx"]),
        mesh=mesh,
        in_specs=(
            P("ctx", "tp"),
            P("ctx", "tp"),
            P("ctx", "tp"),
            P("tp", None),
            P("tp", None),
            P("tp", None),
        ),
        out_specs=P(("ctx", "tp"), None),
        check_vma=False,
    )
```

```python
import functools

import jax
import jax.numpy as jnp
from jax import lax
from jax.experimental import pallas as pl
from jax.experimental.pallas import tpu as pltpu
from jax.sharding import PartitionSpec as P

HS = 128
BLK = 64
SPAN = 16
VMOST = 2
NEAR = 3
LANES = 128
MASKED = -1e30
EXP_SCALE = 1.4426950408889634 / (HS**0.5)
TILE = 1024
HEAD = 2
MIB = 1024 * 1024


SHORT = pl.CostEstimate(flops=0, bytes_accessed=0, transcendentals=0)


def vmem():
    return pl.BlockSpec(memory_space=pltpu.VMEM)


def smem():
    return pl.BlockSpec(memory_space=pltpu.SMEM)


def anywhere():
    return pl.BlockSpec(memory_space=pl.ANY)


def params(mib):
    return pltpu.CompilerParams(vmem_limit_bytes=mib * MIB)


def picked_blocks(vertical, shard, local_blocks):
    block = vertical - shard * local_blocks
    block = jnp.where((block >= 0) & (block < local_blocks), block, local_blocks)
    first = jnp.min(block)
    second = jnp.min(jnp.where(block > first, block, local_blocks))
    return [
        pl.ds(pl.multiple_of(jnp.minimum(x, local_blocks - 1) * BLK, BLK), BLK)
        for x in (first, second)
    ]


def pick_kernel(rank_ref, vert_ref, k_ref, v_ref, both_ref, pair_ref):
    both_ref[:, :HS] = k_ref[...]
    both_ref[:, HS:] = v_ref[...]
    blocks = picked_blocks(vert_ref[...], rank_ref[0], k_ref.shape[0] // BLK)
    for slot, rows in enumerate(blocks):
        picked = both_ref[rows, :]
        for copy in range(pair_ref.shape[0]):
            pair_ref[copy, slot * BLK : (slot + 1) * BLK, :] = picked


def pick(rank, vertical, keys, values, copies):
    return pl.pallas_call(
        pick_kernel,
        out_shape=(
            jax.ShapeDtypeStruct((keys.shape[0], 2 * HS), keys.dtype),
            jax.ShapeDtypeStruct((copies, VMOST * BLK, 2 * HS), keys.dtype),
        ),
        in_specs=[smem(), vmem(), vmem(), vmem()],
        out_specs=(vmem(), vmem()),
        compiler_params=params(60),
        name="pick",
    )(rank, vertical, keys, values)


def member(table, blocks):
    found = table[:, :1] == blocks
    for column in range(1, table.shape[1]):
        found = found | (table[:, column : column + 1] == blocks)
    return found


def pool_blocks(vertical, rank, slots, local_blocks):
    lane = lax.broadcasted_iota(jnp.int32, (vertical.shape[0], LANES), 1)
    slot = lane // VMOST
    shard = jnp.where(slot < slots, 2 * slot + (rank & 1), 2 * (slot - slots) + 1 - (rank & 1))
    shard = jnp.where(slot < 2 * slots, shard, -1)
    first = jnp.full((1, LANES), local_blocks, jnp.int32)
    second = first
    for j in reversed(range(local_blocks)):
        here = member(vertical, shard * local_blocks + j)
        here = jnp.max(jnp.where(here, 1, 0), axis=0, keepdims=True) == 1
        second = jnp.where(here, first, second)
        first = jnp.where(here, j, first)
    picked = jnp.where(lane % VMOST == 0, first, second)
    return jnp.where((picked < local_blocks) & (shard >= 0), shard * local_blocks + picked, -1)


def tables_kernel(slots, rank_ref, vert_ref, slash_ref, own_ref, table_ref, copy_ref):
    copy_ref[...] = own_ref[...]
    local_blocks = own_ref.shape[0] // BLK
    table_ref[0, :, : vert_ref.shape[1]] = vert_ref[...]
    table_ref[1, :, : slash_ref.shape[1]] = slash_ref[...]
    table_ref[2] = pool_blocks(vert_ref[...], rank_ref[0], slots, local_blocks)


def tables(rank, vertical, slash, own, slots):
    shape = (3, vertical.shape[0], LANES)
    return pl.pallas_call(
        functools.partial(tables_kernel, slots),
        out_shape=(
            jax.ShapeDtypeStruct(shape, jnp.int32),
            jax.ShapeDtypeStruct(own.shape, own.dtype),
        ),
        in_specs=[smem(), vmem(), vmem(), vmem()],
        out_specs=(vmem(), vmem()),
        compiler_params=params(4),
        cost_estimate=SHORT,
        name="tables",
    )(rank, vertical, slash, own)


def attend_kernel(
    slots, tiles, sizes, place, tp_ref, ctx_ref, q_0, q_1, table_ref, own, kv_1, kv_2, *refs
):
    pairs = refs[:2]
    w_hbm = refs[2]
    kv_win, e_win, kv_pool, e_pool, attended, weight, arrival, landed = refs[-8:]
    outs = refs[-11:-8] if tiles else refs[-9:-8]
    step = pl.program_id(0)
    heads = table_ref.shape[1]
    rows = own.shape[0]
    local_blocks = rows // BLK
    far_rows = e_pool.shape[0]
    dtype = q_0.dtype
    rank = ctx_ref[0]
    vert = table_ref[0][:, : sizes[0]]
    slash = table_ref[1][:, : sizes[1]]
    block = table_ref[2]

    def fetch(t):
        return pltpu.make_async_copy(
            w_hbm.at[:, pl.ds(t * TILE, TILE)], weight.at[t], arrival.at[t]
        )

    @pl.when(step == 0)
    def _():
        copies = [
            pltpu.make_async_copy(x, kv_win.at[pl.ds(s * rows, rows), :], landed.at[s])
            for s, x in enumerate((kv_2, kv_1, own))
        ]
        copies += [
            pltpu.make_async_copy(
                x.at[pl.ds(0, slots)], kv_pool.at[pl.ds(p * slots, slots)], landed.at[NEAR + p]
            )
            for p, x in enumerate(pairs)
        ]
        for copy in copies:
            copy.start()
        for t in range(tiles):
            fetch(t).start()
        key = lax.broadcasted_iota(jnp.int32, e_win.shape, 0)
        lane = lax.broadcasted_iota(jnp.int32, e_win.shape, 1)
        last = (key - (SPAN - 1) * BLK == lane - BLK) & (lane >= BLK)
        e_win[...] = jnp.where((key // BLK == lane) | last, 1.0, 0.0).astype(dtype)
        key = lax.broadcasted_iota(jnp.int32, e_pool.shape, 0)
        lane = lax.broadcasted_iota(jnp.int32, e_pool.shape, 1)
        e_pool[...] = jnp.where(key // BLK == lane, 1.0, 0.0).astype(dtype)
        for copy in copies:
            copy.wait()

    lane = lax.broadcasted_iota(jnp.int32, (heads, LANES), 1)
    row = lax.broadcasted_iota(jnp.int32, (BLK, LANES), 0)
    above = lax.broadcasted_iota(jnp.int32, (BLK, LANES), 1) - BLK > row
    above = jnp.where(above, MASKED, 0.0).astype(jnp.float32)
    offset_ok = member(slash, SPAN - 1 - lane)
    pool_ok = member(vert, block) & (block >= 0)
    contract = (((1,), (1,)), ((), ()))

    def with_ones(values):
        return jnp.concatenate([values, jnp.ones((values.shape[0], LANES), dtype)], axis=1)

    near, far_q, windows = [], [], []
    for u, q_ref in enumerate((q_0, q_1)):
        here = place(u, step, tp_ref)
        q = q_ref[...]
        q = jnp.concatenate([q[:, h * HS : (h + 1) * HS] for h in range(heads)], axis=0)
        first = rank * local_blocks + here - (SPAN - 1)
        seen = first + lane
        ok = (seen >= 0) & (offset_ok | member(vert, seen))
        mask = jnp.where(ok | (lane >= SPAN), 0.0, MASKED).astype(jnp.float32)
        mask = (mask[:, None, :] + above[None]).reshape(heads * BLK, LANES).astype(dtype)
        far_mask = jnp.where(pool_ok & (block < first), 0.0, MASKED).astype(jnp.float32)
        far_mask = jnp.broadcast_to(far_mask[:, None, :], (heads, BLK, LANES))
        far_mask = far_mask.reshape(heads * BLK, LANES).astype(dtype)
        far_q.append(jnp.concatenate([q, far_mask], axis=1))
        window = pl.ds(pl.multiple_of((here + 1) * BLK, BLK), SPAN * BLK)
        windows.append(window)
        keys = jnp.concatenate([kv_win[window, :HS], e_win[...]], axis=1)
        near.append(
            lax.dot_general(
                jnp.concatenate([q, mask], axis=1),
                keys,
                contract,
                preferred_element_type=jnp.float32,
            )
        )
    far = lax.dot_general(
        jnp.concatenate(far_q, axis=0),
        jnp.concatenate([kv_pool[:, :, :HS].reshape(far_rows, HS), e_pool[...]], axis=1),
        contract,
        preferred_element_type=jnp.float32,
    )
    far_values = with_ones(kv_pool[:, :, HS:].reshape(far_rows, HS))
    for u in range(2):
        far_u = far[u * heads * BLK : (u + 1) * heads * BLK]
        top = jnp.maximum(
            jnp.max(near[u], axis=1, keepdims=True), jnp.max(far_u, axis=1, keepdims=True)
        )
        probs = jnp.exp2((near[u] - top) * EXP_SCALE).astype(dtype)
        values = with_ones(kv_win[windows[u], HS:])
        summed = jnp.dot(probs, values, preferred_element_type=jnp.float32)
        probs = jnp.exp2((far_u - top) * EXP_SCALE).astype(dtype)
        summed = summed + jnp.dot(probs, far_values, preferred_element_type=jnp.float32)
        out = (summed[:, :HS] / summed[:, HS:]).astype(dtype)
        at = pl.ds(pl.multiple_of((step * 2 + u) * BLK, BLK), BLK)
        for h in range(heads):
            attended[at, h * HS : (h + 1) * HS] = out[h * BLK : (h + 1) * BLK]

    @pl.when(step == pl.num_programs(0) - 1)
    def _():
        outs[0][...] = attended[...]
        half = attended.shape[0] // 2
        for t in range(tiles):
            fetch(t).wait()
            product = jnp.dot(attended[...], weight[t], preferred_element_type=jnp.float32)
            product = product.astype(dtype)
            outs[1][:, t * TILE : (t + 1) * TILE] = product[:half]
            outs[2][:, t * TILE : (t + 1) * TILE] = product[half:]


def attend(blocks, tp, ctx, queries, table, near_kv, pairs, sizes, out_weight, tiles, after):
    width = queries.shape[1]
    rows = near_kv[0].shape[0]
    quarter = rows // BLK // 4
    steps = len(blocks)
    slots = pairs[1].shape[0]
    dtype = queries.dtype
    far = 2 * slots * VMOST * BLK

    def place(u, g, tp):
        flip, block = blocks[-1][u]
        for step in range(steps - 1):
            flip = jnp.where(g == step, blocks[step][u][0], flip)
            block = jnp.where(g == step, blocks[step][u][1], block)
        return (tp[0] ^ flip) * quarter + block

    def whole(shape):
        return pl.BlockSpec(shape, lambda g, tp, ctx: (0,) * len(shape))

    out_shapes = [(steps * 2 * BLK, width)]
    if tiles:
        out_shapes += [(steps * BLK, tiles * TILE)] * 2
    return pl.pallas_call(
        functools.partial(attend_kernel, slots, tiles, sizes, place),
        out_shape=[jax.ShapeDtypeStruct(shape, dtype) for shape in out_shapes],
        grid_spec=pltpu.PrefetchScalarGridSpec(
            num_scalar_prefetch=2,
            grid=(steps,),
            in_specs=[
                pl.BlockSpec((BLK, width), lambda g, tp, ctx: (place(0, g, tp), 0)),
                pl.BlockSpec((BLK, width), lambda g, tp, ctx: (place(1, g, tp), 0)),
            ]
            + [whole(table.shape)]
            + [anywhere() for _ in [*near_kv, *pairs, out_weight, *after]],
            out_specs=[whole(shape) for shape in out_shapes],
            scratch_shapes=[
                pltpu.VMEM((NEAR * rows, 2 * HS), dtype),
                pltpu.VMEM((SPAN * BLK, LANES), dtype),
                pltpu.VMEM((2 * slots, VMOST * BLK, 2 * HS), dtype),
                pltpu.VMEM((far, LANES), dtype),
                pltpu.VMEM((steps * 2 * BLK, width), dtype),
                pltpu.VMEM((max(tiles, 1), out_weight.shape[0], TILE), dtype),
                pltpu.SemaphoreType.DMA((max(tiles, 1),)),
                pltpu.SemaphoreType.DMA((NEAR + 2,)),
            ],
        ),
        compiler_params=params(50),
        cost_estimate=SHORT,
        name="attend",
    )(tp, ctx, queries, queries, table, *near_kv, *pairs, out_weight, *after)


def project_kernel(first, a_ref, w_hbm, *refs):
    weight, arrival = refs[-2:]
    tiles, _, tile = weight.shape
    outs = refs[-2 - 2 * tiles : -2]
    half = outs[0].shape[0]

    def fetch(t):
        return pltpu.make_async_copy(
            w_hbm.at[:, pl.ds(first + t * tile, tile)], weight.at[t], arrival.at[t]
        )

    for t in range(tiles):
        fetch(t).start()
    for t in range(tiles):
        fetch(t).wait()
        product = jnp.dot(a_ref[...], weight[t], preferred_element_type=jnp.float32)
        product = product.astype(a_ref.dtype)
        outs[t][...] = product[:half]
        outs[tiles + t][...] = product[half:]


def project(attended, out_weight, first, tiles, after):
    rows, depth = attended.shape
    tile = (out_weight.shape[1] - first) // tiles
    part = jax.ShapeDtypeStruct((rows // 2, tile), attended.dtype)
    outs = pl.pallas_call(
        functools.partial(project_kernel, first),
        out_shape=[part] * (2 * tiles),
        in_specs=[vmem(), anywhere()] + [anywhere() for _ in after],
        out_specs=[vmem()] * (2 * tiles),
        scratch_shapes=[
            pltpu.VMEM((tiles, depth, tile), attended.dtype),
            pltpu.SemaphoreType.DMA((tiles,)),
        ],
        compiler_params=params(50),
        cost_estimate=SHORT,
        name="project",
    )(attended, out_weight, *after)
    return outs[:tiles], outs[tiles:]


def add_kernel(*refs):
    out_ref = refs[-1]
    pieces = len(refs) // 2
    first = 0
    for t in range(pieces):
        total = refs[t][...].astype(jnp.float32) + refs[pieces + t][...].astype(jnp.float32)
        last = first + total.shape[1]
        out_ref[:, first:last] = total.astype(out_ref.dtype)
        first = last


def add(keep, got):
    rows, columns = keep[0].shape[0], sum(x.shape[1] for x in keep)
    return pl.pallas_call(
        add_kernel,
        out_shape=jax.ShapeDtypeStruct((rows, columns), keep[0].dtype),
        in_specs=[vmem()] * (2 * len(keep)),
        out_specs=vmem(),
        compiler_params=params(16),
        cost_estimate=SHORT,
        name="add",
    )(*keep, *got)


def finish_kernel(tiles, first, top, *refs):
    arrived_ref = refs[2 * tiles]
    out_ref, tiles_ref, sent = refs[-3:]
    rows = pl.ds(top, arrived_ref.shape[0])
    copies = []
    for t in range(tiles):
        total = refs[t][rows, :].astype(jnp.float32) + refs[tiles + t][rows, :].astype(jnp.float32)
        total = total + arrived_ref[:, t * TILE : (t + 1) * TILE].astype(jnp.float32)
        tiles_ref[t] = total.astype(out_ref.dtype)
        columns = pl.ds((first + t) * TILE, TILE)
        copies.append(
            pltpu.make_async_copy(tiles_ref.at[t], out_ref.at[rows, columns], sent.at[t])
        )
        copies[-1].start()
    for copy in copies:
        copy.wait()


def finish(keep, got, arrived, first, top, shape, out):
    tiles = len(keep)
    before = [] if out is None else [out]
    return pl.pallas_call(
        functools.partial(finish_kernel, tiles, first, top),
        out_shape=jax.ShapeDtypeStruct(shape, arrived.dtype),
        in_specs=[vmem()] * (2 * tiles + 1) + [anywhere() for _ in before],
        out_specs=anywhere(),
        input_output_aliases={2 * tiles + 1: 0} if before else {},
        scratch_shapes=[
            pltpu.VMEM((tiles, arrived.shape[0], TILE), arrived.dtype),
            pltpu.SemaphoreType.DMA((tiles,)),
        ],
        compiler_params=params(16),
        cost_estimate=SHORT,
        name="finish",
    )(*keep, *got, arrived, *before)


def shards(ctx_size, queries, keys, values, out_weight, vertical, slash):
    local_blocks = queries.shape[0] // BLK
    assert ctx_size % 2 == 0 and (NEAR - 1) * local_blocks >= SPAN - 1
    ctx = jnp.reshape(lax.axis_index("ctx"), (1,)).astype(jnp.int32)
    tp = jnp.reshape(lax.axis_index("tp"), (1,)).astype(jnp.int32)

    def shifted(x, by):
        return lax.ppermute(x, "ctx", [(r, r + by) for r in range(ctx_size - by)])

    half = ctx_size // 2
    own, pair = pick(ctx, vertical, keys, values, half)
    parities = [list(range(odd, ctx_size, 2)) for odd in (0, 1)]
    pairs = [lax.all_to_all(pair, "ctx", 0, 0, axis_index_groups=parities, tiled=True)]
    needed = pairs[0][: half - 1]
    pairs.append(lax.ppermute(needed, "ctx", [(r, r ^ 1) for r in range(ctx_size)]))
    table, own_copy = tables(ctx, vertical, slash, own, half - 1)
    near_kv = [own_copy, shifted(own, 1), shifted(own, 2)]

    def sibling(x):
        return lax.ppermute(x, "tp", [(j, j ^ 1) for j in range(4)])

    def across(x):
        return lax.ppermute(x, "tp", [(j, j ^ 2) for j in range(4)])

    def attention(blocks, tiles, after):
        sizes = (vertical.shape[1], slash.shape[1])
        return attend(
            blocks, tp, ctx, queries, table, near_kv, pairs, sizes, out_weight, tiles, after
        )

    def exchanged(send, keep):
        return add(keep, [sibling(x) for x in send])

    width = out_weight.shape[1]
    tiles = width // TILE
    assert local_blocks == 8
    attended, send, keep = attention((((3, 0), (2, 0)),), HEAD, ())
    total = (keep.astype(jnp.float32) + sibling(send).astype(jnp.float32)).astype(keep.dtype)
    arrived = [across(total)]
    total = exchanged(*project(attended, out_weight, HEAD * TILE, 4, (total,)))
    arrived.append(across(total))
    (attended,) = attention((((3, 1), (2, 1)),), 0, (total,))
    total = exchanged(*project(attended, out_weight, 0, 4, (arrived[0],)))
    arrived.append(across(total))
    (attended,) = attention((((1, 0), (1, 1)), ((0, 0), (0, 1))), 0, (total, arrived[1]))
    send, keep = project(attended, out_weight, 0, tiles, ())
    got = [sibling(x) for x in send]
    shape = (queries.shape[0] // 4, width)
    out = finish(keep[:HEAD], got[:HEAD], arrived[0], 0, 0, shape, None)
    out = finish(keep[HEAD:], got[HEAD:], arrived[1], HEAD, 0, shape, out)
    return finish(keep, got, arrived[2], 0, BLK, shape, out)


def solution(mesh):
    assert mesh.shape["tp"] == 4
    return jax.shard_map(
        functools.partial(shards, mesh.shape["ctx"]),
        mesh=mesh,
        in_specs=(
            P("ctx", "tp"),
            P("ctx", "tp"),
            P("ctx", "tp"),
            P("tp", None),
            P("tp", None),
            P("tp", None),
        ),
        out_specs=P(("ctx", "tp"), None),
        check_vma=False,
    )
```

```python
import functools

import jax
import jax.numpy as jnp
from jax import lax
from jax.experimental import pallas as pl
from jax.experimental.pallas import tpu as pltpu
from jax.sharding import PartitionSpec as P

HS = 128
BLK = 64
SPAN = 16
VMOST = 2
NEAR = 3
LANES = 128
MASKED = -1e30
EXP_SCALE = 1.4426950408889634 / (HS**0.5)
TILE = 1024
HEAD = 2
MIB = 1024 * 1024


SHORT = pl.CostEstimate(flops=0, bytes_accessed=0, transcendentals=0)


def vmem():
    return pl.BlockSpec(memory_space=pltpu.VMEM)


def smem():
    return pl.BlockSpec(memory_space=pltpu.SMEM)


def anywhere():
    return pl.BlockSpec(memory_space=pl.ANY)


def params(mib):
    return pltpu.CompilerParams(vmem_limit_bytes=mib * MIB)


def picked_blocks(vertical, shard, local_blocks):
    block = vertical - shard * local_blocks
    block = jnp.where((block >= 0) & (block < local_blocks), block, local_blocks)
    first = jnp.min(block)
    second = jnp.min(jnp.where(block > first, block, local_blocks))
    return [
        pl.ds(pl.multiple_of(jnp.minimum(x, local_blocks - 1) * BLK, BLK), BLK)
        for x in (first, second)
    ]


def pick_kernel(rank_ref, vert_ref, k_ref, v_ref, both_ref, pair_ref):
    both_ref[:, :HS] = k_ref[...]
    both_ref[:, HS:] = v_ref[...]
    blocks = picked_blocks(vert_ref[...], rank_ref[0], k_ref.shape[0] // BLK)
    for slot, rows in enumerate(blocks):
        picked = both_ref[rows, :]
        for copy in range(pair_ref.shape[0]):
            pair_ref[copy, slot * BLK : (slot + 1) * BLK, :] = picked


def pick(rank, vertical, keys, values, copies):
    return pl.pallas_call(
        pick_kernel,
        out_shape=(
            jax.ShapeDtypeStruct((keys.shape[0], 2 * HS), keys.dtype),
            jax.ShapeDtypeStruct((copies, VMOST * BLK, 2 * HS), keys.dtype),
        ),
        in_specs=[smem(), vmem(), vmem(), vmem()],
        out_specs=(vmem(), vmem()),
        compiler_params=params(60),
        name="pick",
    )(rank, vertical, keys, values)


def member(table, blocks):
    found = table[:, :1] == blocks
    for column in range(1, table.shape[1]):
        found = found | (table[:, column : column + 1] == blocks)
    return found


def pool_blocks(vertical, rank, slots, local_blocks):
    lane = lax.broadcasted_iota(jnp.int32, (vertical.shape[0], LANES), 1)
    slot = lane // VMOST
    shard = jnp.where(slot < slots, 2 * slot + (rank & 1), 2 * (slot - slots) + 1 - (rank & 1))
    shard = jnp.where(slot < 2 * slots, shard, -1)
    first = jnp.full((1, LANES), local_blocks, jnp.int32)
    second = first
    for j in reversed(range(local_blocks)):
        here = member(vertical, shard * local_blocks + j)
        here = jnp.max(jnp.where(here, 1, 0), axis=0, keepdims=True) == 1
        second = jnp.where(here, first, second)
        first = jnp.where(here, j, first)
    picked = jnp.where(lane % VMOST == 0, first, second)
    return jnp.where((picked < local_blocks) & (shard >= 0), shard * local_blocks + picked, -1)


def tables_kernel(slots, rank_ref, vert_ref, slash_ref, own_ref, table_ref, copy_ref):
    copy_ref[...] = own_ref[...]
    local_blocks = own_ref.shape[0] // BLK
    table_ref[0, :, : vert_ref.shape[1]] = vert_ref[...]
    table_ref[1, :, : slash_ref.shape[1]] = slash_ref[...]
    table_ref[2] = pool_blocks(vert_ref[...], rank_ref[0], slots, local_blocks)


def tables(rank, vertical, slash, own, slots):
    shape = (3, vertical.shape[0], LANES)
    return pl.pallas_call(
        functools.partial(tables_kernel, slots),
        out_shape=(
            jax.ShapeDtypeStruct(shape, jnp.int32),
            jax.ShapeDtypeStruct(own.shape, own.dtype),
        ),
        in_specs=[smem(), vmem(), vmem(), vmem()],
        out_specs=(vmem(), vmem()),
        compiler_params=params(4),
        cost_estimate=SHORT,
        name="tables",
    )(rank, vertical, slash, own)


def attend_kernel(
    slots, tiles, sizes, place, tp_ref, ctx_ref, q_0, q_1, table_ref, own, kv_2, kv_1, *refs
):
    pairs = refs[:2]
    w_hbm = refs[2]
    kv_win, e_win, kv_pool, e_pool, attended, weight, arrival, landed = refs[-8:]
    outs = refs[-11:-8] if tiles else refs[-9:-8]
    step = pl.program_id(0)
    heads = table_ref.shape[1]
    rows = own.shape[0]
    local_blocks = rows // BLK
    far_rows = e_pool.shape[0]
    dtype = q_0.dtype
    rank = ctx_ref[0]
    vert = table_ref[0][:, : sizes[0]]
    slash = table_ref[1][:, : sizes[1]]
    block = table_ref[2]

    def fetch(t):
        return pltpu.make_async_copy(
            w_hbm.at[:, pl.ds(t * TILE, TILE)], weight.at[t], arrival.at[t]
        )

    @pl.when(step == 0)
    def _():
        copies = [
            pltpu.make_async_copy(x, kv_win.at[pl.ds(s * rows, rows), :], landed.at[s])
            for s, x in enumerate((kv_2, kv_1, own))
        ]
        copies += [
            pltpu.make_async_copy(
                x.at[pl.ds(0, slots)], kv_pool.at[pl.ds(p * slots, slots)], landed.at[NEAR + p]
            )
            for p, x in enumerate(pairs)
        ]
        for copy in copies:
            copy.start()
        for t in range(tiles):
            fetch(t).start()
        key = lax.broadcasted_iota(jnp.int32, e_win.shape, 0)
        lane = lax.broadcasted_iota(jnp.int32, e_win.shape, 1)
        last = (key - (SPAN - 1) * BLK == lane - BLK) & (lane >= BLK)
        e_win[...] = jnp.where((key // BLK == lane) | last, 1.0, 0.0).astype(dtype)
        key = lax.broadcasted_iota(jnp.int32, e_pool.shape, 0)
        lane = lax.broadcasted_iota(jnp.int32, e_pool.shape, 1)
        e_pool[...] = jnp.where(key // BLK == lane, 1.0, 0.0).astype(dtype)
        for copy in copies:
            copy.wait()

    lane = lax.broadcasted_iota(jnp.int32, (heads, LANES), 1)
    row = lax.broadcasted_iota(jnp.int32, (BLK, LANES), 0)
    above = lax.broadcasted_iota(jnp.int32, (BLK, LANES), 1) - BLK > row
    above = jnp.where(above, MASKED, 0.0).astype(jnp.float32)
    offset_ok = member(slash, SPAN - 1 - lane)
    pool_ok = member(vert, block) & (block >= 0)
    contract = (((1,), (1,)), ((), ()))

    def with_ones(values):
        return jnp.concatenate([values, jnp.ones((values.shape[0], LANES), dtype)], axis=1)

    near, far_q, windows = [], [], []
    for u, q_ref in enumerate((q_0, q_1)):
        here = place(u, step, tp_ref)
        q = q_ref[...]
        q = jnp.concatenate([q[:, h * HS : (h + 1) * HS] for h in range(heads)], axis=0)
        first = rank * local_blocks + here - (SPAN - 1)
        seen = first + lane
        ok = (seen >= 0) & (offset_ok | member(vert, seen))
        mask = jnp.where(ok | (lane >= SPAN), 0.0, MASKED).astype(jnp.float32)
        mask = (mask[:, None, :] + above[None]).reshape(heads * BLK, LANES).astype(dtype)
        far_mask = jnp.where(pool_ok & (block < first), 0.0, MASKED).astype(jnp.float32)
        far_mask = jnp.broadcast_to(far_mask[:, None, :], (heads, BLK, LANES))
        far_mask = far_mask.reshape(heads * BLK, LANES).astype(dtype)
        far_q.append(jnp.concatenate([q, far_mask], axis=1))
        window = pl.ds(pl.multiple_of((here + 1) * BLK, BLK), SPAN * BLK)
        windows.append(window)
        keys = jnp.concatenate([kv_win[window, :HS], e_win[...]], axis=1)
        near.append(
            lax.dot_general(
                jnp.concatenate([q, mask], axis=1),
                keys,
                contract,
                preferred_element_type=jnp.float32,
            )
        )
    far = lax.dot_general(
        jnp.concatenate(far_q, axis=0),
        jnp.concatenate([kv_pool[:, :, :HS].reshape(far_rows, HS), e_pool[...]], axis=1),
        contract,
        preferred_element_type=jnp.float32,
    )
    far_values = with_ones(kv_pool[:, :, HS:].reshape(far_rows, HS))
    for u in range(2):
        far_u = far[u * heads * BLK : (u + 1) * heads * BLK]
        top = jnp.maximum(
            jnp.max(near[u], axis=1, keepdims=True), jnp.max(far_u, axis=1, keepdims=True)
        )
        probs = jnp.exp2((near[u] - top) * EXP_SCALE).astype(dtype)
        values = with_ones(kv_win[windows[u], HS:])
        summed = jnp.dot(probs, values, preferred_element_type=jnp.float32)
        probs = jnp.exp2((far_u - top) * EXP_SCALE).astype(dtype)
        summed = summed + jnp.dot(probs, far_values, preferred_element_type=jnp.float32)
        out = (summed[:, :HS] / summed[:, HS:]).astype(dtype)
        at = pl.ds(pl.multiple_of((step * 2 + u) * BLK, BLK), BLK)
        for h in range(heads):
            attended[at, h * HS : (h + 1) * HS] = out[h * BLK : (h + 1) * BLK]

    @pl.when(step == pl.num_programs(0) - 1)
    def _():
        outs[0][...] = attended[...]
        half = attended.shape[0] // 2
        for t in range(tiles):
            fetch(t).wait()
            product = jnp.dot(attended[...], weight[t], preferred_element_type=jnp.float32)
            product = product.astype(dtype)
            outs[1][:, t * TILE : (t + 1) * TILE] = product[:half]
            outs[2][:, t * TILE : (t + 1) * TILE] = product[half:]


def attend(blocks, tp, ctx, queries, table, near_kv, pairs, sizes, out_weight, tiles, after):
    width = queries.shape[1]
    rows = near_kv[0].shape[0]
    quarter = rows // BLK // 4
    steps = len(blocks)
    slots = pairs[1].shape[0]
    dtype = queries.dtype
    far = 2 * slots * VMOST * BLK

    def place(u, g, tp):
        flip, block = blocks[-1][u]
        for step in range(steps - 1):
            flip = jnp.where(g == step, blocks[step][u][0], flip)
            block = jnp.where(g == step, blocks[step][u][1], block)
        return (tp[0] ^ flip) * quarter + block

    def whole(shape):
        return pl.BlockSpec(shape, lambda g, tp, ctx: (0,) * len(shape))

    out_shapes = [(steps * 2 * BLK, width)]
    if tiles:
        out_shapes += [(steps * BLK, tiles * TILE)] * 2
    return pl.pallas_call(
        functools.partial(attend_kernel, slots, tiles, sizes, place),
        out_shape=[jax.ShapeDtypeStruct(shape, dtype) for shape in out_shapes],
        grid_spec=pltpu.PrefetchScalarGridSpec(
            num_scalar_prefetch=2,
            grid=(steps,),
            in_specs=[
                pl.BlockSpec((BLK, width), lambda g, tp, ctx: (place(0, g, tp), 0)),
                pl.BlockSpec((BLK, width), lambda g, tp, ctx: (place(1, g, tp), 0)),
            ]
            + [whole(table.shape)]
            + [anywhere() for _ in [*near_kv, *pairs, out_weight, *after]],
            out_specs=[whole(shape) for shape in out_shapes],
            scratch_shapes=[
                pltpu.VMEM((NEAR * rows, 2 * HS), dtype),
                pltpu.VMEM((SPAN * BLK, LANES), dtype),
                pltpu.VMEM((2 * slots, VMOST * BLK, 2 * HS), dtype),
                pltpu.VMEM((far, LANES), dtype),
                pltpu.VMEM((steps * 2 * BLK, width), dtype),
                pltpu.VMEM((max(tiles, 1), out_weight.shape[0], TILE), dtype),
                pltpu.SemaphoreType.DMA((max(tiles, 1),)),
                pltpu.SemaphoreType.DMA((NEAR + 2,)),
            ],
        ),
        compiler_params=params(50),
        cost_estimate=SHORT,
        name="attend",
    )(tp, ctx, queries, queries, table, *near_kv, *pairs, out_weight, *after)


def project_kernel(first, a_ref, w_hbm, *refs):
    weight, arrival = refs[-2:]
    tiles, _, tile = weight.shape
    outs = refs[-2 - 2 * tiles : -2]
    half = outs[0].shape[0]

    def fetch(t):
        return pltpu.make_async_copy(
            w_hbm.at[:, pl.ds(first + t * tile, tile)], weight.at[t], arrival.at[t]
        )

    for t in range(tiles):
        fetch(t).start()
    for t in range(tiles):
        fetch(t).wait()
        product = jnp.dot(a_ref[...], weight[t], preferred_element_type=jnp.float32)
        product = product.astype(a_ref.dtype)
        outs[t][...] = product[:half]
        outs[tiles + t][...] = product[half:]


def project(attended, out_weight, first, tiles, after):
    rows, depth = attended.shape
    tile = (out_weight.shape[1] - first) // tiles
    part = jax.ShapeDtypeStruct((rows // 2, tile), attended.dtype)
    outs = pl.pallas_call(
        functools.partial(project_kernel, first),
        out_shape=[part] * (2 * tiles),
        in_specs=[vmem(), anywhere()] + [anywhere() for _ in after],
        out_specs=[vmem()] * (2 * tiles),
        scratch_shapes=[
            pltpu.VMEM((tiles, depth, tile), attended.dtype),
            pltpu.SemaphoreType.DMA((tiles,)),
        ],
        compiler_params=params(50),
        cost_estimate=SHORT,
        name="project",
    )(attended, out_weight, *after)
    return outs[:tiles], outs[tiles:]


def add_kernel(*refs):
    out_ref = refs[-1]
    pieces = len(refs) // 2
    first = 0
    for t in range(pieces):
        total = refs[t][...].astype(jnp.float32) + refs[pieces + t][...].astype(jnp.float32)
        last = first + total.shape[1]
        out_ref[:, first:last] = total.astype(out_ref.dtype)
        first = last


def add(keep, got):
    rows, columns = keep[0].shape[0], sum(x.shape[1] for x in keep)
    return pl.pallas_call(
        add_kernel,
        out_shape=jax.ShapeDtypeStruct((rows, columns), keep[0].dtype),
        in_specs=[vmem()] * (2 * len(keep)),
        out_specs=vmem(),
        compiler_params=params(16),
        cost_estimate=SHORT,
        name="add",
    )(*keep, *got)


def finish_kernel(tiles, first, top, *refs):
    arrived_ref = refs[2 * tiles]
    out_ref, tiles_ref, sent = refs[-3:]
    rows = pl.ds(top, arrived_ref.shape[0])
    copies = []
    for t in range(tiles):
        total = refs[t][rows, :].astype(jnp.float32) + refs[tiles + t][rows, :].astype(jnp.float32)
        total = total + arrived_ref[:, t * TILE : (t + 1) * TILE].astype(jnp.float32)
        tiles_ref[t] = total.astype(out_ref.dtype)
        columns = pl.ds((first + t) * TILE, TILE)
        copies.append(
            pltpu.make_async_copy(tiles_ref.at[t], out_ref.at[rows, columns], sent.at[t])
        )
        copies[-1].start()
    for copy in copies:
        copy.wait()


def finish(keep, got, arrived, first, top, shape, out):
    tiles = len(keep)
    before = [] if out is None else [out]
    return pl.pallas_call(
        functools.partial(finish_kernel, tiles, first, top),
        out_shape=jax.ShapeDtypeStruct(shape, arrived.dtype),
        in_specs=[vmem()] * (2 * tiles + 1) + [anywhere() for _ in before],
        out_specs=anywhere(),
        input_output_aliases={2 * tiles + 1: 0} if before else {},
        scratch_shapes=[
            pltpu.VMEM((tiles, arrived.shape[0], TILE), arrived.dtype),
            pltpu.SemaphoreType.DMA((tiles,)),
        ],
        compiler_params=params(16),
        cost_estimate=SHORT,
        name="finish",
    )(*keep, *got, arrived, *before)


def shards(ctx_size, queries, keys, values, out_weight, vertical, slash):
    local_blocks = queries.shape[0] // BLK
    assert ctx_size % 2 == 0 and (NEAR - 1) * local_blocks >= SPAN - 1
    ctx = jnp.reshape(lax.axis_index("ctx"), (1,)).astype(jnp.int32)
    tp = jnp.reshape(lax.axis_index("tp"), (1,)).astype(jnp.int32)

    def shifted(x, by):
        return lax.ppermute(x, "ctx", [(r, r + by) for r in range(ctx_size - by)])

    half = ctx_size // 2
    own, pair = pick(ctx, vertical, keys, values, half)
    parities = [list(range(odd, ctx_size, 2)) for odd in (0, 1)]
    pairs = [lax.all_to_all(pair, "ctx", 0, 0, axis_index_groups=parities, tiled=True)]
    needed = pairs[0][: half - 1]
    pairs.append(lax.ppermute(needed, "ctx", [(r, r ^ 1) for r in range(ctx_size)]))
    table, own_copy = tables(ctx, vertical, slash, own, half - 1)
    near_kv = [own_copy, shifted(own, 2), shifted(own, 1)]

    def sibling(x):
        return lax.ppermute(x, "tp", [(j, j ^ 1) for j in range(4)])

    def across(x):
        return lax.ppermute(x, "tp", [(j, j ^ 2) for j in range(4)])

    def attention(blocks, tiles, after):
        sizes = (vertical.shape[1], slash.shape[1])
        return attend(
            blocks, tp, ctx, queries, table, near_kv, pairs, sizes, out_weight, tiles, after
        )

    def exchanged(send, keep):
        return add(keep, [sibling(x) for x in send])

    width = out_weight.shape[1]
    tiles = width // TILE
    assert local_blocks == 8
    attended, send, keep = attention((((3, 0), (2, 0)),), HEAD, ())
    total = (keep.astype(jnp.float32) + sibling(send).astype(jnp.float32)).astype(keep.dtype)
    arrived = [across(total)]
    total = exchanged(*project(attended, out_weight, HEAD * TILE, 4, (total,)))
    arrived.append(across(total))
    (attended,) = attention((((3, 1), (2, 1)),), 0, (total,))
    total = exchanged(*project(attended, out_weight, 0, 4, (arrived[0],)))
    arrived.append(across(total))
    (attended,) = attention((((1, 0), (1, 1)), ((0, 0), (0, 1))), 0, (total, arrived[1]))
    send, keep = project(attended, out_weight, 0, tiles, ())
    got = [sibling(x) for x in send]
    shape = (queries.shape[0] // 4, width)
    out = finish(keep[:HEAD], got[:HEAD], arrived[0], 0, 0, shape, None)
    out = finish(keep[HEAD:], got[HEAD:], arrived[1], HEAD, 0, shape, out)
    return finish(keep, got, arrived[2], 0, BLK, shape, out)


def solution(mesh):
    assert mesh.shape["tp"] == 4
    return jax.shard_map(
        functools.partial(shards, mesh.shape["ctx"]),
        mesh=mesh,
        in_specs=(
            P("ctx", "tp"),
            P("ctx", "tp"),
            P("ctx", "tp"),
            P("tp", None),
            P("tp", None),
            P("tp", None),
        ),
        out_specs=P(("ctx", "tp"), None),
        check_vma=False,
    )
```

```python
import functools

import jax
import jax.numpy as jnp
from jax import lax
from jax.experimental import pallas as pl
from jax.experimental.pallas import tpu as pltpu
from jax.sharding import PartitionSpec as P

HS = 128
BLK = 64
SPAN = 16
VMOST = 2
NEAR = 3
LANES = 128
MASKED = -1e30
EXP_SCALE = 1.4426950408889634 / (HS**0.5)
TILE = 1024
HEAD = 2
MIB = 1024 * 1024


SHORT = pl.CostEstimate(flops=0, bytes_accessed=0, transcendentals=0)


def vmem():
    return pl.BlockSpec(memory_space=pltpu.VMEM)


def smem():
    return pl.BlockSpec(memory_space=pltpu.SMEM)


def anywhere():
    return pl.BlockSpec(memory_space=pl.ANY)


def params(mib):
    return pltpu.CompilerParams(vmem_limit_bytes=mib * MIB)


def picked_blocks(vertical, shard, local_blocks):
    block = vertical - shard * local_blocks
    block = jnp.where((block >= 0) & (block < local_blocks), block, local_blocks)
    first = jnp.min(block)
    second = jnp.min(jnp.where(block > first, block, local_blocks))
    return [
        pl.ds(pl.multiple_of(jnp.minimum(x, local_blocks - 1) * BLK, BLK), BLK)
        for x in (first, second)
    ]


def pick_kernel(rank_ref, vert_ref, k_ref, v_ref, both_ref, low_ref, high_ref, pair_ref):
    both_ref[:, :HS] = k_ref[...]
    both_ref[:, HS:] = v_ref[...]
    half = low_ref.shape[0]
    low_ref[...] = both_ref[:half, :]
    high_ref[...] = both_ref[half:, :]
    blocks = picked_blocks(vert_ref[...], rank_ref[0], k_ref.shape[0] // BLK)
    for slot, rows in enumerate(blocks):
        picked = both_ref[rows, :]
        for copy in range(pair_ref.shape[0]):
            pair_ref[copy, slot * BLK : (slot + 1) * BLK, :] = picked


def pick(rank, vertical, keys, values, copies):
    return pl.pallas_call(
        pick_kernel,
        out_shape=(
            jax.ShapeDtypeStruct((keys.shape[0], 2 * HS), keys.dtype),
            jax.ShapeDtypeStruct((keys.shape[0] // 2, 2 * HS), keys.dtype),
            jax.ShapeDtypeStruct((keys.shape[0] // 2, 2 * HS), keys.dtype),
            jax.ShapeDtypeStruct((copies, VMOST * BLK, 2 * HS), keys.dtype),
        ),
        in_specs=[smem(), vmem(), vmem(), vmem()],
        out_specs=(vmem(),) * 4,
        compiler_params=params(60),
        name="pick",
    )(rank, vertical, keys, values)


def member(table, blocks):
    found = table[:, :1] == blocks
    for column in range(1, table.shape[1]):
        found = found | (table[:, column : column + 1] == blocks)
    return found


def pool_blocks(vertical, rank, slots, local_blocks):
    lane = lax.broadcasted_iota(jnp.int32, (vertical.shape[0], LANES), 1)
    slot = lane // VMOST
    shard = jnp.where(slot < slots, 2 * slot + (rank & 1), 2 * (slot - slots) + 1 - (rank & 1))
    shard = jnp.where(slot < 2 * slots, shard, -1)
    first = jnp.full((1, LANES), local_blocks, jnp.int32)
    second = first
    for j in reversed(range(local_blocks)):
        here = member(vertical, shard * local_blocks + j)
        here = jnp.max(jnp.where(here, 1, 0), axis=0, keepdims=True) == 1
        second = jnp.where(here, first, second)
        first = jnp.where(here, j, first)
    picked = jnp.where(lane % VMOST == 0, first, second)
    return jnp.where((picked < local_blocks) & (shard >= 0), shard * local_blocks + picked, -1)


def tables_kernel(slots, rank_ref, vert_ref, slash_ref, own_ref, table_ref, copy_ref):
    copy_ref[...] = own_ref[...]
    local_blocks = own_ref.shape[0] // BLK
    table_ref[0, :, : vert_ref.shape[1]] = vert_ref[...]
    table_ref[1, :, : slash_ref.shape[1]] = slash_ref[...]
    table_ref[2] = pool_blocks(vert_ref[...], rank_ref[0], slots, local_blocks)


def tables(rank, vertical, slash, own, slots):
    shape = (3, vertical.shape[0], LANES)
    return pl.pallas_call(
        functools.partial(tables_kernel, slots),
        out_shape=(
            jax.ShapeDtypeStruct(shape, jnp.int32),
            jax.ShapeDtypeStruct(own.shape, own.dtype),
        ),
        in_specs=[smem(), vmem(), vmem(), vmem()],
        out_specs=(vmem(), vmem()),
        compiler_params=params(4),
        cost_estimate=SHORT,
        name="tables",
    )(rank, vertical, slash, own)


def attend_kernel(
    slots, tiles, sizes, place, tp_ref, ctx_ref, q_0, q_1, table_ref, own, kv_2, *refs
):
    kv_1, kv_1_odd, kv_1_even = refs[:3]
    pairs = refs[3:5]
    w_hbm = refs[5]
    kv_win, e_win, kv_pool, e_pool, attended, weight, arrival, landed = refs[-8:]
    outs = refs[-11:-8] if tiles else refs[-9:-8]
    step = pl.program_id(0)
    heads = table_ref.shape[1]
    rows = own.shape[0]
    local_blocks = rows // BLK
    far_rows = e_pool.shape[0]
    dtype = q_0.dtype
    rank = ctx_ref[0]
    vert = table_ref[0][:, : sizes[0]]
    slash = table_ref[1][:, : sizes[1]]
    block = table_ref[2]

    def fetch(t):
        return pltpu.make_async_copy(
            w_hbm.at[:, pl.ds(t * TILE, TILE)], weight.at[t], arrival.at[t]
        )

    @pl.when(step == 0)
    def _():
        half = kv_1.shape[0]
        places = ((kv_2, 0), (kv_1, rows), (own, 2 * rows))
        copies = [
            pltpu.make_async_copy(x, kv_win.at[pl.ds(at, x.shape[0]), :], landed.at[s])
            for s, (x, at) in enumerate(places)
        ]
        second = kv_win.at[pl.ds(rows + half, half), :]
        odd = (rank & 1) == 1

        @pl.when(odd)
        def _():
            pltpu.make_async_copy(kv_1_odd, second, landed.at[NEAR + 2]).start()

        @pl.when(jnp.logical_not(odd))
        def _():
            pltpu.make_async_copy(kv_1_even, second, landed.at[NEAR + 2]).start()

        copies.append(pltpu.make_async_copy(kv_1_odd, second, landed.at[NEAR + 2]))
        copies += [
            pltpu.make_async_copy(
                x.at[pl.ds(0, slots)], kv_pool.at[pl.ds(p * slots, slots)], landed.at[NEAR + p]
            )
            for p, x in enumerate(pairs)
        ]
        for copy in copies:
            if copy is not copies[NEAR]:
                copy.start()
        for t in range(tiles):
            fetch(t).start()
        key = lax.broadcasted_iota(jnp.int32, e_win.shape, 0)
        lane = lax.broadcasted_iota(jnp.int32, e_win.shape, 1)
        last = (key - (SPAN - 1) * BLK == lane - BLK) & (lane >= BLK)
        e_win[...] = jnp.where((key // BLK == lane) | last, 1.0, 0.0).astype(dtype)
        key = lax.broadcasted_iota(jnp.int32, e_pool.shape, 0)
        lane = lax.broadcasted_iota(jnp.int32, e_pool.shape, 1)
        e_pool[...] = jnp.where(key // BLK == lane, 1.0, 0.0).astype(dtype)
        for copy in copies:
            copy.wait()

    lane = lax.broadcasted_iota(jnp.int32, (heads, LANES), 1)
    row = lax.broadcasted_iota(jnp.int32, (BLK, LANES), 0)
    above = lax.broadcasted_iota(jnp.int32, (BLK, LANES), 1) - BLK > row
    above = jnp.where(above, MASKED, 0.0).astype(jnp.float32)
    offset_ok = member(slash, SPAN - 1 - lane)
    pool_ok = member(vert, block) & (block >= 0)
    contract = (((1,), (1,)), ((), ()))

    def with_ones(values):
        return jnp.concatenate([values, jnp.ones((values.shape[0], LANES), dtype)], axis=1)

    near, far_q, windows = [], [], []
    for u, q_ref in enumerate((q_0, q_1)):
        here = place(u, step, tp_ref)
        q = q_ref[...]
        q = jnp.concatenate([q[:, h * HS : (h + 1) * HS] for h in range(heads)], axis=0)
        first = rank * local_blocks + here - (SPAN - 1)
        seen = first + lane
        ok = (seen >= 0) & (offset_ok | member(vert, seen))
        mask = jnp.where(ok | (lane >= SPAN), 0.0, MASKED).astype(jnp.float32)
        mask = (mask[:, None, :] + above[None]).reshape(heads * BLK, LANES).astype(dtype)
        far_mask = jnp.where(pool_ok & (block < first), 0.0, MASKED).astype(jnp.float32)
        far_mask = jnp.broadcast_to(far_mask[:, None, :], (heads, BLK, LANES))
        far_mask = far_mask.reshape(heads * BLK, LANES).astype(dtype)
        far_q.append(jnp.concatenate([q, far_mask], axis=1))
        window = pl.ds(pl.multiple_of((here + 1) * BLK, BLK), SPAN * BLK)
        windows.append(window)
        keys = jnp.concatenate([kv_win[window, :HS], e_win[...]], axis=1)
        near.append(
            lax.dot_general(
                jnp.concatenate([q, mask], axis=1),
                keys,
                contract,
                preferred_element_type=jnp.float32,
            )
        )
    far = lax.dot_general(
        jnp.concatenate(far_q, axis=0),
        jnp.concatenate([kv_pool[:, :, :HS].reshape(far_rows, HS), e_pool[...]], axis=1),
        contract,
        preferred_element_type=jnp.float32,
    )
    far_values = with_ones(kv_pool[:, :, HS:].reshape(far_rows, HS))
    for u in range(2):
        far_u = far[u * heads * BLK : (u + 1) * heads * BLK]
        top = jnp.maximum(
            jnp.max(near[u], axis=1, keepdims=True), jnp.max(far_u, axis=1, keepdims=True)
        )
        probs = jnp.exp2((near[u] - top) * EXP_SCALE).astype(dtype)
        values = with_ones(kv_win[windows[u], HS:])
        summed = jnp.dot(probs, values, preferred_element_type=jnp.float32)
        probs = jnp.exp2((far_u - top) * EXP_SCALE).astype(dtype)
        summed = summed + jnp.dot(probs, far_values, preferred_element_type=jnp.float32)
        out = (summed[:, :HS] / summed[:, HS:]).astype(dtype)
        at = pl.ds(pl.multiple_of((step * 2 + u) * BLK, BLK), BLK)
        for h in range(heads):
            attended[at, h * HS : (h + 1) * HS] = out[h * BLK : (h + 1) * BLK]

    @pl.when(step == pl.num_programs(0) - 1)
    def _():
        outs[0][...] = attended[...]
        half = attended.shape[0] // 2
        for t in range(tiles):
            fetch(t).wait()
            product = jnp.dot(attended[...], weight[t], preferred_element_type=jnp.float32)
            product = product.astype(dtype)
            outs[1][:, t * TILE : (t + 1) * TILE] = product[:half]
            outs[2][:, t * TILE : (t + 1) * TILE] = product[half:]


def attend(blocks, tp, ctx, queries, table, near_kv, pairs, sizes, out_weight, tiles, after):
    width = queries.shape[1]
    rows = near_kv[0].shape[0]
    quarter = rows // BLK // 4
    steps = len(blocks)
    slots = pairs[1].shape[0]
    dtype = queries.dtype
    far = 2 * slots * VMOST * BLK

    def place(u, g, tp):
        flip, block = blocks[-1][u]
        for step in range(steps - 1):
            flip = jnp.where(g == step, blocks[step][u][0], flip)
            block = jnp.where(g == step, blocks[step][u][1], block)
        return (tp[0] ^ flip) * quarter + block

    def whole(shape):
        return pl.BlockSpec(shape, lambda g, tp, ctx: (0,) * len(shape))

    out_shapes = [(steps * 2 * BLK, width)]
    if tiles:
        out_shapes += [(steps * BLK, tiles * TILE)] * 2
    return pl.pallas_call(
        functools.partial(attend_kernel, slots, tiles, sizes, place),
        out_shape=[jax.ShapeDtypeStruct(shape, dtype) for shape in out_shapes],
        grid_spec=pltpu.PrefetchScalarGridSpec(
            num_scalar_prefetch=2,
            grid=(steps,),
            in_specs=[
                pl.BlockSpec((BLK, width), lambda g, tp, ctx: (place(0, g, tp), 0)),
                pl.BlockSpec((BLK, width), lambda g, tp, ctx: (place(1, g, tp), 0)),
            ]
            + [whole(table.shape)]
            + [anywhere() for _ in [*near_kv, *pairs, out_weight, *after]],
            out_specs=[whole(shape) for shape in out_shapes],
            scratch_shapes=[
                pltpu.VMEM((NEAR * rows, 2 * HS), dtype),
                pltpu.VMEM((SPAN * BLK, LANES), dtype),
                pltpu.VMEM((2 * slots, VMOST * BLK, 2 * HS), dtype),
                pltpu.VMEM((far, LANES), dtype),
                pltpu.VMEM((steps * 2 * BLK, width), dtype),
                pltpu.VMEM((max(tiles, 1), out_weight.shape[0], TILE), dtype),
                pltpu.SemaphoreType.DMA((max(tiles, 1),)),
                pltpu.SemaphoreType.DMA((NEAR + 3,)),
            ],
        ),
        compiler_params=params(50),
        cost_estimate=SHORT,
        name="attend",
    )(tp, ctx, queries, queries, table, *near_kv, *pairs, out_weight, *after)


def project_kernel(first, a_ref, w_hbm, *refs):
    weight, arrival = refs[-2:]
    tiles, _, tile = weight.shape
    outs = refs[-2 - 2 * tiles : -2]
    half = outs[0].shape[0]

    def fetch(t):
        return pltpu.make_async_copy(
            w_hbm.at[:, pl.ds(first + t * tile, tile)], weight.at[t], arrival.at[t]
        )

    for t in range(tiles):
        fetch(t).start()
    for t in range(tiles):
        fetch(t).wait()
        product = jnp.dot(a_ref[...], weight[t], preferred_element_type=jnp.float32)
        product = product.astype(a_ref.dtype)
        outs[t][...] = product[:half]
        outs[tiles + t][...] = product[half:]


def project(attended, out_weight, first, tiles, after):
    rows, depth = attended.shape
    tile = (out_weight.shape[1] - first) // tiles
    part = jax.ShapeDtypeStruct((rows // 2, tile), attended.dtype)
    outs = pl.pallas_call(
        functools.partial(project_kernel, first),
        out_shape=[part] * (2 * tiles),
        in_specs=[vmem(), anywhere()] + [anywhere() for _ in after],
        out_specs=[vmem()] * (2 * tiles),
        scratch_shapes=[
            pltpu.VMEM((tiles, depth, tile), attended.dtype),
            pltpu.SemaphoreType.DMA((tiles,)),
        ],
        compiler_params=params(50),
        cost_estimate=SHORT,
        name="project",
    )(attended, out_weight, *after)
    return outs[:tiles], outs[tiles:]


def add_kernel(*refs):
    out_ref = refs[-1]
    pieces = len(refs) // 2
    first = 0
    for t in range(pieces):
        total = refs[t][...].astype(jnp.float32) + refs[pieces + t][...].astype(jnp.float32)
        last = first + total.shape[1]
        out_ref[:, first:last] = total.astype(out_ref.dtype)
        first = last


def add(keep, got):
    rows, columns = keep[0].shape[0], sum(x.shape[1] for x in keep)
    return pl.pallas_call(
        add_kernel,
        out_shape=jax.ShapeDtypeStruct((rows, columns), keep[0].dtype),
        in_specs=[vmem()] * (2 * len(keep)),
        out_specs=vmem(),
        compiler_params=params(16),
        cost_estimate=SHORT,
        name="add",
    )(*keep, *got)


def finish_kernel(tiles, first, top, *refs):
    arrived_ref = refs[2 * tiles]
    out_ref, tiles_ref, sent = refs[-3:]
    rows = pl.ds(top, arrived_ref.shape[0])
    copies = []
    for t in range(tiles):
        total = refs[t][rows, :].astype(jnp.float32) + refs[tiles + t][rows, :].astype(jnp.float32)
        total = total + arrived_ref[:, t * TILE : (t + 1) * TILE].astype(jnp.float32)
        tiles_ref[t] = total.astype(out_ref.dtype)
        columns = pl.ds((first + t) * TILE, TILE)
        copies.append(
            pltpu.make_async_copy(tiles_ref.at[t], out_ref.at[rows, columns], sent.at[t])
        )
        copies[-1].start()
    for copy in copies:
        copy.wait()


def finish(keep, got, arrived, first, top, shape, out):
    tiles = len(keep)
    before = [] if out is None else [out]
    return pl.pallas_call(
        functools.partial(finish_kernel, tiles, first, top),
        out_shape=jax.ShapeDtypeStruct(shape, arrived.dtype),
        in_specs=[vmem()] * (2 * tiles + 1) + [anywhere() for _ in before],
        out_specs=anywhere(),
        input_output_aliases={2 * tiles + 1: 0} if before else {},
        scratch_shapes=[
            pltpu.VMEM((tiles, arrived.shape[0], TILE), arrived.dtype),
            pltpu.SemaphoreType.DMA((tiles,)),
        ],
        compiler_params=params(16),
        cost_estimate=SHORT,
        name="finish",
    )(*keep, *got, arrived, *before)


def shards(ctx_size, queries, keys, values, out_weight, vertical, slash):
    local_blocks = queries.shape[0] // BLK
    assert ctx_size % 2 == 0 and (NEAR - 1) * local_blocks >= SPAN - 1
    ctx = jnp.reshape(lax.axis_index("ctx"), (1,)).astype(jnp.int32)
    tp = jnp.reshape(lax.axis_index("tp"), (1,)).astype(jnp.int32)

    def shifted(x, by):
        return lax.ppermute(x, "ctx", [(r, r + by) for r in range(ctx_size - by)])

    half = ctx_size // 2
    own, low, high, pair = pick(ctx, vertical, keys, values, half)
    parities = [list(range(odd, ctx_size, 2)) for odd in (0, 1)]
    pairs = [lax.all_to_all(pair, "ctx", 0, 0, axis_index_groups=parities, tiled=True)]
    needed = pairs[0][: half - 1]
    pairs.append(lax.ppermute(needed, "ctx", [(r, r ^ 1) for r in range(ctx_size)]))
    table, own_copy = tables(ctx, vertical, slash, own, half - 1)
    kv_1_odd = lax.ppermute(high, "ctx", [(r, r ^ 1) for r in range(ctx_size)])
    kv_1_even = lax.ppermute(kv_1_odd, "ctx", [(r, r + 2) for r in range(0, ctx_size - 2, 2)])
    near_kv = [own_copy, shifted(own, 2), shifted(low, 1), kv_1_odd, kv_1_even]

    def sibling(x):
        return lax.ppermute(x, "tp", [(j, j ^ 1) for j in range(4)])

    def across(x):
        return lax.ppermute(x, "tp", [(j, j ^ 2) for j in range(4)])

    def attention(blocks, tiles, after):
        sizes = (vertical.shape[1], slash.shape[1])
        return attend(
            blocks, tp, ctx, queries, table, near_kv, pairs, sizes, out_weight, tiles, after
        )

    def exchanged(send, keep):
        return add(keep, [sibling(x) for x in send])

    width = out_weight.shape[1]
    tiles = width // TILE
    assert local_blocks == 8
    attended, send, keep = attention((((3, 0), (2, 0)),), HEAD, ())
    total = (keep.astype(jnp.float32) + sibling(send).astype(jnp.float32)).astype(keep.dtype)
    arrived = [across(total)]
    total = exchanged(*project(attended, out_weight, HEAD * TILE, 4, (total,)))
    arrived.append(across(total))
    (attended,) = attention((((3, 1), (2, 1)),), 0, (total,))
    total = exchanged(*project(attended, out_weight, 0, 4, (arrived[0],)))
    arrived.append(across(total))
    (attended,) = attention((((1, 0), (1, 1)), ((0, 0), (0, 1))), 0, (total, arrived[1]))
    send, keep = project(attended, out_weight, 0, tiles, ())
    got = [sibling(x) for x in send]
    shape = (queries.shape[0] // 4, width)
    out = finish(keep[:HEAD], got[:HEAD], arrived[0], 0, 0, shape, None)
    out = finish(keep[HEAD:], got[HEAD:], arrived[1], HEAD, 0, shape, out)
    return finish(keep, got, arrived[2], 0, BLK, shape, out)


def solution(mesh):
    assert mesh.shape["tp"] == 4
    return jax.shard_map(
        functools.partial(shards, mesh.shape["ctx"]),
        mesh=mesh,
        in_specs=(
            P("ctx", "tp"),
            P("ctx", "tp"),
            P("ctx", "tp"),
            P("tp", None),
            P("tp", None),
            P("tp", None),
        ),
        out_specs=P(("ctx", "tp"), None),
        check_vma=False,
    )
```

```python
import functools

import jax
import jax.numpy as jnp
from jax import lax
from jax.experimental import pallas as pl
from jax.experimental.pallas import tpu as pltpu
from jax.sharding import PartitionSpec as P

HS = 128
BLK = 64
SPAN = 16
VMOST = 2
NEAR = 3
LANES = 128
MASKED = -1e30
EXP_SCALE = 1.4426950408889634 / (HS**0.5)
TILE = 1024
HEAD = 2
MIB = 1024 * 1024


SHORT = pl.CostEstimate(flops=0, bytes_accessed=0, transcendentals=0)


def vmem():
    return pl.BlockSpec(memory_space=pltpu.VMEM)


def smem():
    return pl.BlockSpec(memory_space=pltpu.SMEM)


def anywhere():
    return pl.BlockSpec(memory_space=pl.ANY)


def params(mib):
    return pltpu.CompilerParams(vmem_limit_bytes=mib * MIB)


def picked_blocks(vertical, shard, local_blocks):
    block = vertical - shard * local_blocks
    block = jnp.where((block >= 0) & (block < local_blocks), block, local_blocks)
    first = jnp.min(block)
    second = jnp.min(jnp.where(block > first, block, local_blocks))
    return [
        pl.ds(pl.multiple_of(jnp.minimum(x, local_blocks - 1) * BLK, BLK), BLK)
        for x in (first, second)
    ]


def pick_kernel(rank_ref, vert_ref, k_ref, v_ref, both_ref, late_ref, pair_ref):
    both_ref[:, :HS] = k_ref[...]
    both_ref[:, HS:] = v_ref[...]
    late_ref[...] = both_ref[both_ref.shape[0] - late_ref.shape[0] :, :]
    blocks = picked_blocks(vert_ref[...], rank_ref[0], k_ref.shape[0] // BLK)
    for slot, rows in enumerate(blocks):
        picked = both_ref[rows, :]
        for copy in range(pair_ref.shape[0]):
            pair_ref[copy, slot * BLK : (slot + 1) * BLK, :] = picked


def pick(rank, vertical, keys, values, copies):
    return pl.pallas_call(
        pick_kernel,
        out_shape=(
            jax.ShapeDtypeStruct((keys.shape[0], 2 * HS), keys.dtype),
            jax.ShapeDtypeStruct(((SPAN - 1) * BLK - keys.shape[0], 2 * HS), keys.dtype),
            jax.ShapeDtypeStruct((copies, VMOST * BLK, 2 * HS), keys.dtype),
        ),
        in_specs=[smem(), vmem(), vmem(), vmem()],
        out_specs=(vmem(),) * 3,
        compiler_params=params(60),
        name="pick",
    )(rank, vertical, keys, values)


def member(table, blocks):
    found = table[:, :1] == blocks
    for column in range(1, table.shape[1]):
        found = found | (table[:, column : column + 1] == blocks)
    return found


def pool_blocks(vertical, rank, slots, local_blocks):
    lane = lax.broadcasted_iota(jnp.int32, (vertical.shape[0], LANES), 1)
    slot = lane // VMOST
    shard = jnp.where(slot < slots, 2 * slot + (rank & 1), 2 * (slot - slots) + 1 - (rank & 1))
    shard = jnp.where(slot < 2 * slots, shard, -1)
    first = jnp.full((1, LANES), local_blocks, jnp.int32)
    second = first
    for j in reversed(range(local_blocks)):
        here = member(vertical, shard * local_blocks + j)
        here = jnp.max(jnp.where(here, 1, 0), axis=0, keepdims=True) == 1
        second = jnp.where(here, first, second)
        first = jnp.where(here, j, first)
    picked = jnp.where(lane % VMOST == 0, first, second)
    return jnp.where((picked < local_blocks) & (shard >= 0), shard * local_blocks + picked, -1)


def tables_kernel(slots, rank_ref, vert_ref, slash_ref, own_ref, table_ref, copy_ref, win_ref, pool_ref):
    copy_ref[...] = own_ref[...]
    key = lax.broadcasted_iota(jnp.int32, win_ref.shape, 0)
    lane = lax.broadcasted_iota(jnp.int32, win_ref.shape, 1)
    last = (key - (SPAN - 1) * BLK == lane - BLK) & (lane >= BLK)
    win_ref[...] = jnp.where((key // BLK == lane) | last, 1.0, 0.0).astype(win_ref.dtype)
    key = lax.broadcasted_iota(jnp.int32, pool_ref.shape, 0)
    lane = lax.broadcasted_iota(jnp.int32, pool_ref.shape, 1)
    pool_ref[...] = jnp.where(key // BLK == lane, 1.0, 0.0).astype(pool_ref.dtype)
    local_blocks = own_ref.shape[0] // BLK
    table_ref[0, :, : vert_ref.shape[1]] = vert_ref[...]
    table_ref[1, :, : slash_ref.shape[1]] = slash_ref[...]
    table_ref[2] = pool_blocks(vert_ref[...], rank_ref[0], slots, local_blocks)


def tables(rank, vertical, slash, own, slots):
    shape = (3, vertical.shape[0], LANES)
    return pl.pallas_call(
        functools.partial(tables_kernel, slots),
        out_shape=(
            jax.ShapeDtypeStruct(shape, jnp.int32),
            jax.ShapeDtypeStruct(own.shape, own.dtype),
            jax.ShapeDtypeStruct((SPAN * BLK, LANES), own.dtype),
            jax.ShapeDtypeStruct((2 * slots * VMOST * BLK, LANES), own.dtype),
        ),
        in_specs=[smem(), vmem(), vmem(), vmem()],
        out_specs=(vmem(),) * 4,
        compiler_params=params(4),
        cost_estimate=SHORT,
        name="tables",
    )(rank, vertical, slash, own)


def attend_kernel(
    slots, tiles, sizes, place, tp_ref, ctx_ref, q_0, q_1, table_ref, e_win, e_pool, own, kv_1, kv_2, *refs
):
    pairs = refs[:2]
    w_hbm = refs[2]
    kv_win, kv_pool, attended, weight, arrival, landed = refs[-6:]
    outs = refs[-9:-6] if tiles else refs[-7:-6]
    step = pl.program_id(0)
    heads = table_ref.shape[1]
    rows = own.shape[0]
    local_blocks = rows // BLK
    far_rows = e_pool.shape[0]
    dtype = q_0.dtype
    rank = ctx_ref[0]
    vert = table_ref[0][:, : sizes[0]]
    slash = table_ref[1][:, : sizes[1]]
    block = table_ref[2]

    def fetch(t):
        return pltpu.make_async_copy(
            w_hbm.at[:, pl.ds(t * TILE, TILE)], weight.at[t], arrival.at[t]
        )

    @pl.when(step == 0)
    def _():
        reach = kv_2.shape[0]
        places = ((kv_2, 0), (kv_1, reach), (own, reach + rows))
        copies = [
            pltpu.make_async_copy(x, kv_win.at[pl.ds(at, x.shape[0]), :], landed.at[s])
            for s, (x, at) in enumerate(places)
        ]
        copies += [
            pltpu.make_async_copy(
                x.at[pl.ds(0, slots)], kv_pool.at[pl.ds(p * slots, slots)], landed.at[NEAR + p]
            )
            for p, x in enumerate(pairs)
        ]
        for copy in copies:
            copy.start()
        for t in range(tiles):
            fetch(t).start()
        for copy in copies:
            copy.wait()

    lane = lax.broadcasted_iota(jnp.int32, (heads, LANES), 1)
    row = lax.broadcasted_iota(jnp.int32, (BLK, LANES), 0)
    above = lax.broadcasted_iota(jnp.int32, (BLK, LANES), 1) - BLK > row
    above = jnp.where(above, MASKED, 0.0).astype(jnp.float32)
    offset_ok = member(slash, SPAN - 1 - lane)
    pool_ok = member(vert, block) & (block >= 0)
    contract = (((1,), (1,)), ((), ()))

    def with_ones(values):
        return jnp.concatenate([values, jnp.ones((values.shape[0], LANES), dtype)], axis=1)

    near, far_q, windows = [], [], []
    for u, q_ref in enumerate((q_0, q_1)):
        here = place(u, step, tp_ref)
        q = q_ref[...]
        q = jnp.concatenate([q[:, h * HS : (h + 1) * HS] for h in range(heads)], axis=0)
        first = rank * local_blocks + here - (SPAN - 1)
        seen = first + lane
        ok = (seen >= 0) & (offset_ok | member(vert, seen))
        mask = jnp.where(ok | (lane >= SPAN), 0.0, MASKED).astype(jnp.float32)
        mask = (mask[:, None, :] + above[None]).reshape(heads * BLK, LANES).astype(dtype)
        far_mask = jnp.where(pool_ok & (block < first), 0.0, MASKED).astype(jnp.float32)
        far_mask = jnp.broadcast_to(far_mask[:, None, :], (heads, BLK, LANES))
        far_mask = far_mask.reshape(heads * BLK, LANES).astype(dtype)
        far_q.append(jnp.concatenate([q, far_mask], axis=1))
        window = pl.ds(pl.multiple_of(here * BLK, BLK), SPAN * BLK)
        windows.append(window)
        keys = jnp.concatenate([kv_win[window, :HS], e_win[...]], axis=1)
        near.append(
            lax.dot_general(
                jnp.concatenate([q, mask], axis=1),
                keys,
                contract,
                preferred_element_type=jnp.float32,
            )
        )
    far = lax.dot_general(
        jnp.concatenate(far_q, axis=0),
        jnp.concatenate([kv_pool[:, :, :HS].reshape(far_rows, HS), e_pool[...]], axis=1),
        contract,
        preferred_element_type=jnp.float32,
    )
    far_values = with_ones(kv_pool[:, :, HS:].reshape(far_rows, HS))
    for u in range(2):
        far_u = far[u * heads * BLK : (u + 1) * heads * BLK]
        top = jnp.maximum(
            jnp.max(near[u], axis=1, keepdims=True), jnp.max(far_u, axis=1, keepdims=True)
        )
        probs = jnp.exp2((near[u] - top) * EXP_SCALE).astype(dtype)
        values = with_ones(kv_win[windows[u], HS:])
        summed = jnp.dot(probs, values, preferred_element_type=jnp.float32)
        probs = jnp.exp2((far_u - top) * EXP_SCALE).astype(dtype)
        summed = summed + jnp.dot(probs, far_values, preferred_element_type=jnp.float32)
        out = (summed[:, :HS] / summed[:, HS:]).astype(dtype)
        at = pl.ds(pl.multiple_of((step * 2 + u) * BLK, BLK), BLK)
        for h in range(heads):
            attended[at, h * HS : (h + 1) * HS] = out[h * BLK : (h + 1) * BLK]

    @pl.when(step == pl.num_programs(0) - 1)
    def _():
        outs[0][...] = attended[...]
        half = attended.shape[0] // 2
        for t in range(tiles):
            fetch(t).wait()
            product = jnp.dot(attended[...], weight[t], preferred_element_type=jnp.float32)
            product = product.astype(dtype)
            outs[1][:, t * TILE : (t + 1) * TILE] = product[:half]
            outs[2][:, t * TILE : (t + 1) * TILE] = product[half:]


def attend(blocks, tp, ctx, queries, lanes, near_kv, pairs, sizes, out_weight, tiles, after):
    width = queries.shape[1]
    rows = near_kv[0].shape[0]
    assert near_kv[2].shape[0] + rows == (SPAN - 1) * BLK
    quarter = rows // BLK // 4
    steps = len(blocks)
    slots = pairs[1].shape[0]
    dtype = queries.dtype

    def place(u, g, tp):
        flip, block = blocks[-1][u]
        for step in range(steps - 1):
            flip = jnp.where(g == step, blocks[step][u][0], flip)
            block = jnp.where(g == step, blocks[step][u][1], block)
        return (tp[0] ^ flip) * quarter + block

    def whole(shape):
        return pl.BlockSpec(shape, lambda g, tp, ctx: (0,) * len(shape))

    out_shapes = [(steps * 2 * BLK, width)]
    if tiles:
        out_shapes += [(steps * BLK, tiles * TILE)] * 2
    return pl.pallas_call(
        functools.partial(attend_kernel, slots, tiles, sizes, place),
        out_shape=[jax.ShapeDtypeStruct(shape, dtype) for shape in out_shapes],
        grid_spec=pltpu.PrefetchScalarGridSpec(
            num_scalar_prefetch=2,
            grid=(steps,),
            in_specs=[
                pl.BlockSpec((BLK, width), lambda g, tp, ctx: (place(0, g, tp), 0)),
                pl.BlockSpec((BLK, width), lambda g, tp, ctx: (place(1, g, tp), 0)),
            ]
            + [whole(x.shape) for x in lanes]
            + [anywhere() for _ in [*near_kv, *pairs, out_weight, *after]],
            out_specs=[whole(shape) for shape in out_shapes],
            scratch_shapes=[
                pltpu.VMEM((near_kv[2].shape[0] + 2 * rows, 2 * HS), dtype),
                pltpu.VMEM((2 * slots, VMOST * BLK, 2 * HS), dtype),
                pltpu.VMEM((steps * 2 * BLK, width), dtype),
                pltpu.VMEM((max(tiles, 1), out_weight.shape[0], TILE), dtype),
                pltpu.SemaphoreType.DMA((max(tiles, 1),)),
                pltpu.SemaphoreType.DMA((NEAR + 2,)),
            ],
        ),
        compiler_params=params(50),
        cost_estimate=SHORT,
        name="attend",
    )(tp, ctx, queries, queries, *lanes, *near_kv, *pairs, out_weight, *after)


def project_kernel(first, a_ref, w_hbm, *refs):
    weight, arrival = refs[-2:]
    tiles, _, tile = weight.shape
    outs = refs[-2 - 2 * tiles : -2]
    half = outs[0].shape[0]

    parts = arrival.shape[1]
    rows = weight.shape[1] // parts

    def fetch(t):
        columns = pl.ds(first + t * tile, tile)
        ats = [pl.ds(p * rows, rows) for p in range(parts)]
        return [
            pltpu.make_async_copy(w_hbm.at[at, columns], weight.at[t, at], arrival.at[t, p])
            for p, at in enumerate(ats)
        ]

    for t in range(min(2, tiles)):
        for copy in fetch(t):
            copy.start()
    for t in range(tiles):
        for copy in fetch(t):
            copy.wait()
        if t + 2 < tiles:
            for copy in fetch(t + 2):
                copy.start()
        product = jnp.dot(a_ref[...], weight[t], preferred_element_type=jnp.float32)
        product = product.astype(a_ref.dtype)
        outs[t][...] = product[:half]
        outs[tiles + t][...] = product[half:]


def project(attended, out_weight, first, tiles, after):
    rows, depth = attended.shape
    tile = (out_weight.shape[1] - first) // tiles
    part = jax.ShapeDtypeStruct((rows // 2, tile), attended.dtype)
    outs = pl.pallas_call(
        functools.partial(project_kernel, first),
        out_shape=[part] * (2 * tiles),
        in_specs=[vmem(), anywhere()] + [anywhere() for _ in after],
        out_specs=[vmem()] * (2 * tiles),
        scratch_shapes=[
            pltpu.VMEM((tiles, depth, tile), attended.dtype),
            pltpu.SemaphoreType.DMA((tiles, 4)),
        ],
        compiler_params=params(50),
        cost_estimate=SHORT,
        name="project",
    )(attended, out_weight, *after)
    return outs[:tiles], outs[tiles:]


def add_kernel(*refs):
    out_ref = refs[-1]
    pieces = len(refs) // 2
    first = 0
    for t in range(pieces):
        total = refs[t][...].astype(jnp.float32) + refs[pieces + t][...].astype(jnp.float32)
        last = first + total.shape[1]
        out_ref[:, first:last] = total.astype(out_ref.dtype)
        first = last


def add(keep, got):
    rows, columns = keep[0].shape[0], sum(x.shape[1] for x in keep)
    return pl.pallas_call(
        add_kernel,
        out_shape=jax.ShapeDtypeStruct((rows, columns), keep[0].dtype),
        in_specs=[vmem()] * (2 * len(keep)),
        out_specs=vmem(),
        compiler_params=params(16),
        cost_estimate=SHORT,
        name="add",
    )(*keep, *got)


def finish_kernel(tiles, first, top, *refs):
    arrived_ref = refs[2 * tiles]
    out_ref, tiles_ref, sent = refs[-3:]
    rows = pl.ds(top, arrived_ref.shape[0])
    copies = []
    for t in range(tiles):
        total = refs[t][rows, :].astype(jnp.float32) + refs[tiles + t][rows, :].astype(jnp.float32)
        total = total + arrived_ref[:, t * TILE : (t + 1) * TILE].astype(jnp.float32)
        tiles_ref[t] = total.astype(out_ref.dtype)
        columns = pl.ds((first + t) * TILE, TILE)
        copies.append(
            pltpu.make_async_copy(tiles_ref.at[t], out_ref.at[rows, columns], sent.at[t])
        )
        copies[-1].start()
    for copy in copies:
        copy.wait()


def finish(keep, got, arrived, first, top, shape, out):
    tiles = len(keep)
    before = [] if out is None else [out]
    return pl.pallas_call(
        functools.partial(finish_kernel, tiles, first, top),
        out_shape=jax.ShapeDtypeStruct(shape, arrived.dtype),
        in_specs=[vmem()] * (2 * tiles + 1) + [anywhere() for _ in before],
        out_specs=anywhere(),
        input_output_aliases={2 * tiles + 1: 0} if before else {},
        scratch_shapes=[
            pltpu.VMEM((tiles, arrived.shape[0], TILE), arrived.dtype),
            pltpu.SemaphoreType.DMA((tiles,)),
        ],
        compiler_params=params(16),
        cost_estimate=SHORT,
        name="finish",
    )(*keep, *got, arrived, *before)


def shards(ctx_size, queries, keys, values, out_weight, vertical, slash):
    local_blocks = queries.shape[0] // BLK
    assert ctx_size % 2 == 0 and (NEAR - 1) * local_blocks >= SPAN - 1
    ctx = jnp.reshape(lax.axis_index("ctx"), (1,)).astype(jnp.int32)
    tp = jnp.reshape(lax.axis_index("tp"), (1,)).astype(jnp.int32)

    def shifted(x, by):
        return lax.ppermute(x, "ctx", [(r, r + by) for r in range(ctx_size - by)])

    half = ctx_size // 2
    own, late, pair = pick(ctx, vertical, keys, values, half)
    parities = [list(range(odd, ctx_size, 2)) for odd in (0, 1)]
    pairs = [lax.all_to_all(pair, "ctx", 0, 0, axis_index_groups=parities, tiled=True)]
    needed = pairs[0][: half - 1]
    pairs.append(lax.ppermute(needed, "ctx", [(r, r ^ 1) for r in range(ctx_size)]))
    table, own_copy, e_win, e_pool = tables(ctx, vertical, slash, own, half - 1)
    near_kv = [own_copy, shifted(own, 1), shifted(late, 2)]

    def sibling(x):
        return lax.ppermute(x, "tp", [(j, j ^ 1) for j in range(4)])

    def across(x):
        return lax.ppermute(x, "tp", [(j, j ^ 2) for j in range(4)])

    def attention(blocks, tiles, after):
        sizes = (vertical.shape[1], slash.shape[1])
        return attend(
            blocks, tp, ctx, queries, (table, e_win, e_pool), near_kv, pairs, sizes, out_weight, tiles, after
        )

    def exchanged(send, keep):
        return add(keep, [sibling(x) for x in send])

    width = out_weight.shape[1]
    tiles = width // TILE
    assert local_blocks == 8
    attended, send, keep = attention((((3, 0), (2, 0)),), HEAD, ())
    total = (keep.astype(jnp.float32) + sibling(send).astype(jnp.float32)).astype(keep.dtype)
    arrived = [across(total)]
    total = exchanged(*project(attended, out_weight, HEAD * TILE, 4, (total,)))
    arrived.append(across(total))
    (attended,) = attention((((3, 1), (2, 1)),), 0, (total,))
    total = exchanged(*project(attended, out_weight, 0, 4, (arrived[0],)))
    arrived.append(across(total))
    (attended,) = attention((((1, 0), (1, 1)), ((0, 0), (0, 1))), 0, (total, arrived[1]))
    send, keep = project(attended, out_weight, 0, tiles, ())
    got = [sibling(x) for x in send]
    shape = (queries.shape[0] // 4, width)
    out = finish(keep[:HEAD], got[:HEAD], arrived[0], 0, 0, shape, None)
    out = finish(keep[HEAD:], got[HEAD:], arrived[1], HEAD, 0, shape, out)
    return finish(keep, got, arrived[2], 0, BLK, shape, out)


def solution(mesh):
    assert mesh.shape["tp"] == 4
    return jax.shard_map(
        functools.partial(shards, mesh.shape["ctx"]),
        mesh=mesh,
        in_specs=(
            P("ctx", "tp"),
            P("ctx", "tp"),
            P("ctx", "tp"),
            P("tp", None),
            P("tp", None),
            P("tp", None),
        ),
        out_specs=P(("ctx", "tp"), None),
        check_vma=False,
    )
```

```python
import functools

import jax
import jax.numpy as jnp
from jax import lax
from jax.experimental import pallas as pl
from jax.experimental.pallas import tpu as pltpu
from jax.sharding import PartitionSpec as P

HS = 128
BLK = 64
SPAN = 16
VMOST = 2
NEAR = 3
LANES = 128
MASKED = -1e30
EXP_SCALE = 1.4426950408889634 / (HS**0.5)
TILE = 1024
HEAD = 2
MIB = 1024 * 1024


SHORT = pl.CostEstimate(flops=0, bytes_accessed=0, transcendentals=0)


def vmem():
    return pl.BlockSpec(memory_space=pltpu.VMEM)


def smem():
    return pl.BlockSpec(memory_space=pltpu.SMEM)


def anywhere():
    return pl.BlockSpec(memory_space=pl.ANY)


def params(mib):
    return pltpu.CompilerParams(vmem_limit_bytes=mib * MIB)


def picked_blocks(vertical, shard, local_blocks):
    block = vertical - shard * local_blocks
    block = jnp.where((block >= 0) & (block < local_blocks), block, local_blocks)
    first = jnp.min(block)
    second = jnp.min(jnp.where(block > first, block, local_blocks))
    return [
        pl.ds(pl.multiple_of(jnp.minimum(x, local_blocks - 1) * BLK, BLK), BLK)
        for x in (first, second)
    ]


def pick_kernel(rank_ref, vert_ref, k_ref, v_ref, both_ref, late_ref, pair_ref):
    both_ref[:, :HS] = k_ref[...]
    both_ref[:, HS:] = v_ref[...]
    late_ref[...] = both_ref[both_ref.shape[0] - late_ref.shape[0] :, :]
    blocks = picked_blocks(vert_ref[...], rank_ref[0], k_ref.shape[0] // BLK)
    for slot, rows in enumerate(blocks):
        picked = both_ref[rows, :]
        for copy in range(pair_ref.shape[0]):
            pair_ref[copy, slot * BLK : (slot + 1) * BLK, :] = picked


def pick(rank, vertical, keys, values, copies):
    return pl.pallas_call(
        pick_kernel,
        out_shape=(
            jax.ShapeDtypeStruct((keys.shape[0], 2 * HS), keys.dtype),
            jax.ShapeDtypeStruct(((SPAN - 1) * BLK - keys.shape[0], 2 * HS), keys.dtype),
            jax.ShapeDtypeStruct((copies, VMOST * BLK, 2 * HS), keys.dtype),
        ),
        in_specs=[smem(), vmem(), vmem(), vmem()],
        out_specs=(vmem(),) * 3,
        compiler_params=params(60),
        name="pick",
    )(rank, vertical, keys, values)


def member(table, blocks):
    found = table[:, :1] == blocks
    for column in range(1, table.shape[1]):
        found = found | (table[:, column : column + 1] == blocks)
    return found


def pool_blocks(vertical, rank, slots, local_blocks):
    lane = lax.broadcasted_iota(jnp.int32, (vertical.shape[0], LANES), 1)
    slot = lane // VMOST
    shard = jnp.where(slot < slots, 2 * slot + (rank & 1), 2 * (slot - slots) + 1 - (rank & 1))
    shard = jnp.where(slot < 2 * slots, shard, -1)
    first = jnp.full((1, LANES), local_blocks, jnp.int32)
    second = first
    for j in reversed(range(local_blocks)):
        here = member(vertical, shard * local_blocks + j)
        here = jnp.max(jnp.where(here, 1, 0), axis=0, keepdims=True) == 1
        second = jnp.where(here, first, second)
        first = jnp.where(here, j, first)
    picked = jnp.where(lane % VMOST == 0, first, second)
    return jnp.where((picked < local_blocks) & (shard >= 0), shard * local_blocks + picked, -1)


def tables_kernel(slots, rank_ref, vert_ref, slash_ref, own_ref, table_ref, copy_ref):
    copy_ref[...] = own_ref[...]
    local_blocks = own_ref.shape[0] // BLK
    table_ref[0, :, : vert_ref.shape[1]] = vert_ref[...]
    table_ref[1, :, : slash_ref.shape[1]] = slash_ref[...]
    table_ref[2] = pool_blocks(vert_ref[...], rank_ref[0], slots, local_blocks)


def tables(rank, vertical, slash, own, slots):
    shape = (3, vertical.shape[0], LANES)
    return pl.pallas_call(
        functools.partial(tables_kernel, slots),
        out_shape=(
            jax.ShapeDtypeStruct(shape, jnp.int32),
            jax.ShapeDtypeStruct(own.shape, own.dtype),
        ),
        in_specs=[smem(), vmem(), vmem(), vmem()],
        out_specs=(vmem(), vmem()),
        compiler_params=params(4),
        cost_estimate=SHORT,
        name="tables",
    )(rank, vertical, slash, own)


def attend_kernel(
    slots, tiles, sizes, place, tp_ref, ctx_ref, q_0, q_1, table_ref, own, kv_1, kv_2, *refs
):
    pairs = refs[:2]
    w_hbm = refs[2]
    kv_win, e_win, kv_pool, e_pool, attended, weight, arrival, landed = refs[-8:]
    outs = refs[-11:-8] if tiles else refs[-9:-8]
    step = pl.program_id(0)
    heads = table_ref.shape[1]
    rows = own.shape[0]
    local_blocks = rows // BLK
    far_rows = e_pool.shape[0]
    dtype = q_0.dtype
    rank = ctx_ref[0]
    vert = table_ref[0][:, : sizes[0]]
    slash = table_ref[1][:, : sizes[1]]
    block = table_ref[2]

    def fetch(t):
        return pltpu.make_async_copy(
            w_hbm.at[:, pl.ds(t * TILE, TILE)], weight.at[t], arrival.at[t]
        )

    @pl.when(step == 0)
    def _():
        reach = kv_2.shape[0]
        places = ((kv_2, 0), (kv_1, reach), (own, reach + rows))
        copies = [
            pltpu.make_async_copy(x, kv_win.at[pl.ds(at, x.shape[0]), :], landed.at[s])
            for s, (x, at) in enumerate(places)
        ]
        copies += [
            pltpu.make_async_copy(
                x.at[pl.ds(0, slots)], kv_pool.at[pl.ds(p * slots, slots)], landed.at[NEAR + p]
            )
            for p, x in enumerate(pairs)
        ]
        for copy in copies:
            copy.start()
        for t in range(tiles):
            fetch(t).start()
        key = lax.broadcasted_iota(jnp.int32, e_win.shape, 0)
        lane = lax.broadcasted_iota(jnp.int32, e_win.shape, 1)
        last = (key - (SPAN - 1) * BLK == lane - BLK) & (lane >= BLK)
        e_win[...] = jnp.where((key // BLK == lane) | last, 1.0, 0.0).astype(dtype)
        key = lax.broadcasted_iota(jnp.int32, e_pool.shape, 0)
        lane = lax.broadcasted_iota(jnp.int32, e_pool.shape, 1)
        e_pool[...] = jnp.where(key // BLK == lane, 1.0, 0.0).astype(dtype)
        for copy in copies:
            copy.wait()

    lane = lax.broadcasted_iota(jnp.int32, (heads, LANES), 1)
    row = lax.broadcasted_iota(jnp.int32, (BLK, LANES), 0)
    above = lax.broadcasted_iota(jnp.int32, (BLK, LANES), 1) - BLK > row
    above = jnp.where(above, MASKED, 0.0).astype(jnp.float32)
    offset_ok = member(slash, SPAN - 1 - lane)
    pool_ok = member(vert, block) & (block >= 0)
    contract = (((1,), (1,)), ((), ()))

    def with_ones(values):
        return jnp.concatenate([values, jnp.ones((values.shape[0], LANES), dtype)], axis=1)

    near, far_q, windows = [], [], []
    for u, q_ref in enumerate((q_0, q_1)):
        here = place(u, step, tp_ref)
        q = q_ref[...]
        q = jnp.concatenate([q[:, h * HS : (h + 1) * HS] for h in range(heads)], axis=0)
        first = rank * local_blocks + here - (SPAN - 1)
        seen = first + lane
        ok = (seen >= 0) & (offset_ok | member(vert, seen))
        mask = jnp.where(ok | (lane >= SPAN), 0.0, MASKED).astype(jnp.float32)
        mask = (mask[:, None, :] + above[None]).reshape(heads * BLK, LANES).astype(dtype)
        far_mask = jnp.where(pool_ok & (block < first), 0.0, MASKED).astype(jnp.float32)
        far_mask = jnp.broadcast_to(far_mask[:, None, :], (heads, BLK, LANES))
        far_mask = far_mask.reshape(heads * BLK, LANES).astype(dtype)
        far_q.append(jnp.concatenate([q, far_mask], axis=1))
        window = pl.ds(pl.multiple_of(here * BLK, BLK), SPAN * BLK)
        windows.append(window)
        keys = jnp.concatenate([kv_win[window, :HS], e_win[...]], axis=1)
        near.append(
            lax.dot_general(
                jnp.concatenate([q, mask], axis=1),
                keys,
                contract,
                preferred_element_type=jnp.float32,
            )
        )
    far = lax.dot_general(
        jnp.concatenate(far_q, axis=0),
        jnp.concatenate([kv_pool[:, :, :HS].reshape(far_rows, HS), e_pool[...]], axis=1),
        contract,
        preferred_element_type=jnp.float32,
    )
    far_values = with_ones(kv_pool[:, :, HS:].reshape(far_rows, HS))
    for u in range(2):
        far_u = far[u * heads * BLK : (u + 1) * heads * BLK]
        top = jnp.maximum(
            jnp.max(near[u], axis=1, keepdims=True), jnp.max(far_u, axis=1, keepdims=True)
        )
        probs = jnp.exp2((near[u] - top) * EXP_SCALE).astype(dtype)
        values = with_ones(kv_win[windows[u], HS:])
        summed = jnp.dot(probs, values, preferred_element_type=jnp.float32)
        probs = jnp.exp2((far_u - top) * EXP_SCALE).astype(dtype)
        summed = summed + jnp.dot(probs, far_values, preferred_element_type=jnp.float32)
        out = (summed[:, :HS] / summed[:, HS:]).astype(dtype)
        at = pl.ds(pl.multiple_of((step * 2 + u) * BLK, BLK), BLK)
        for h in range(heads):
            attended[at, h * HS : (h + 1) * HS] = out[h * BLK : (h + 1) * BLK]

    @pl.when(step == pl.num_programs(0) - 1)
    def _():
        outs[0][...] = attended[...]
        half = attended.shape[0] // 2
        for t in range(tiles):
            fetch(t).wait()
            product = jnp.dot(attended[...], weight[t], preferred_element_type=jnp.float32)
            product = product.astype(dtype)
            outs[1][:, t * TILE : (t + 1) * TILE] = product[:half]
            outs[2][:, t * TILE : (t + 1) * TILE] = product[half:]


def attend(blocks, tp, ctx, queries, table, near_kv, pairs, sizes, out_weight, tiles, after):
    width = queries.shape[1]
    rows = near_kv[0].shape[0]
    assert near_kv[2].shape[0] + rows == (SPAN - 1) * BLK
    quarter = rows // BLK // 4
    steps = len(blocks)
    slots = pairs[1].shape[0]
    dtype = queries.dtype
    far = 2 * slots * VMOST * BLK

    def place(u, g, tp):
        flip, block = blocks[-1][u]
        for step in range(steps - 1):
            flip = jnp.where(g == step, blocks[step][u][0], flip)
            block = jnp.where(g == step, blocks[step][u][1], block)
        return (tp[0] ^ flip) * quarter + block

    def whole(shape):
        return pl.BlockSpec(shape, lambda g, tp, ctx: (0,) * len(shape))

    out_shapes = [(steps * 2 * BLK, width)]
    if tiles:
        out_shapes += [(steps * BLK, tiles * TILE)] * 2
    return pl.pallas_call(
        functools.partial(attend_kernel, slots, tiles, sizes, place),
        out_shape=[jax.ShapeDtypeStruct(shape, dtype) for shape in out_shapes],
        grid_spec=pltpu.PrefetchScalarGridSpec(
            num_scalar_prefetch=2,
            grid=(steps,),
            in_specs=[
                pl.BlockSpec((BLK, width), lambda g, tp, ctx: (place(0, g, tp), 0)),
                pl.BlockSpec((BLK, width), lambda g, tp, ctx: (place(1, g, tp), 0)),
            ]
            + [whole(table.shape)]
            + [anywhere() for _ in [*near_kv, *pairs, out_weight, *after]],
            out_specs=[whole(shape) for shape in out_shapes],
            scratch_shapes=[
                pltpu.VMEM((near_kv[2].shape[0] + 2 * rows, 2 * HS), dtype),
                pltpu.VMEM((SPAN * BLK, LANES), dtype),
                pltpu.VMEM((2 * slots, VMOST * BLK, 2 * HS), dtype),
                pltpu.VMEM((far, LANES), dtype),
                pltpu.VMEM((steps * 2 * BLK, width), dtype),
                pltpu.VMEM((max(tiles, 1), out_weight.shape[0], TILE), dtype),
                pltpu.SemaphoreType.DMA((max(tiles, 1),)),
                pltpu.SemaphoreType.DMA((NEAR + 2,)),
            ],
        ),
        compiler_params=params(40),
        cost_estimate=SHORT,
        name="attend",
    )(tp, ctx, queries, queries, table, *near_kv, *pairs, out_weight, *after)


def project_staged_kernel(first, a_ref, w_ref, *refs):
    tiles = len(refs) // 2
    outs = refs[-2 * tiles :]
    half, tile = outs[0].shape
    for t in range(tiles):
        weight = w_ref[:, first + t * tile : first + (t + 1) * tile]
        product = jnp.dot(a_ref[...], weight, preferred_element_type=jnp.float32)
        product = product.astype(a_ref.dtype)
        outs[t][...] = product[:half]
        outs[tiles + t][...] = product[half:]


def project_staged(attended, weight, first, tiles, after):
    rows, depth = attended.shape
    tile = (weight.shape[1] - first) // tiles
    part = jax.ShapeDtypeStruct((rows // 2, tile), attended.dtype)
    outs = pl.pallas_call(
        functools.partial(project_staged_kernel, first),
        out_shape=[part] * (2 * tiles),
        in_specs=[vmem(), vmem(), anywhere()],
        out_specs=[vmem()] * (2 * tiles),
        compiler_params=params(24),
        cost_estimate=SHORT,
        name="project",
    )(attended, weight, after)
    return outs[:tiles], outs[tiles:]


def project_kernel(first, a_ref, w_hbm, *refs):
    weight, arrival = refs[-2:]
    tiles, _, tile = weight.shape
    outs = refs[-2 - 2 * tiles : -2]
    half = outs[0].shape[0]

    def fetch(t):
        return pltpu.make_async_copy(
            w_hbm.at[:, pl.ds(first + t * tile, tile)], weight.at[t], arrival.at[t]
        )

    for t in range(tiles):
        fetch(t).start()
    for t in range(tiles):
        fetch(t).wait()
        product = jnp.dot(a_ref[...], weight[t], preferred_element_type=jnp.float32)
        product = product.astype(a_ref.dtype)
        outs[t][...] = product[:half]
        outs[tiles + t][...] = product[half:]


def project(attended, out_weight, first, tiles, after):
    rows, depth = attended.shape
    tile = (out_weight.shape[1] - first) // tiles
    part = jax.ShapeDtypeStruct((rows // 2, tile), attended.dtype)
    outs = pl.pallas_call(
        functools.partial(project_kernel, first),
        out_shape=[part] * (2 * tiles),
        in_specs=[vmem(), anywhere()] + [anywhere() for _ in after],
        out_specs=[vmem()] * (2 * tiles),
        scratch_shapes=[
            pltpu.VMEM((tiles, depth, tile), attended.dtype),
            pltpu.SemaphoreType.DMA((tiles,)),
        ],
        compiler_params=params(50),
        cost_estimate=SHORT,
        name="project",
    )(attended, out_weight, *after)
    return outs[:tiles], outs[tiles:]


def add_kernel(*refs):
    out_ref = refs[-1]
    pieces = len(refs) // 2
    first = 0
    for t in range(pieces):
        total = refs[t][...].astype(jnp.float32) + refs[pieces + t][...].astype(jnp.float32)
        last = first + total.shape[1]
        out_ref[:, first:last] = total.astype(out_ref.dtype)
        first = last


def add(keep, got):
    rows, columns = keep[0].shape[0], sum(x.shape[1] for x in keep)
    return pl.pallas_call(
        add_kernel,
        out_shape=jax.ShapeDtypeStruct((rows, columns), keep[0].dtype),
        in_specs=[vmem()] * (2 * len(keep)),
        out_specs=vmem(),
        compiler_params=params(16),
        cost_estimate=SHORT,
        name="add",
    )(*keep, *got)


def finish_kernel(tiles, first, top, *refs):
    arrived_ref = refs[2 * tiles]
    out_ref, tiles_ref, sent = refs[-3:]
    rows = pl.ds(top, arrived_ref.shape[0])
    copies = []
    for t in range(tiles):
        total = refs[t][rows, :].astype(jnp.float32) + refs[tiles + t][rows, :].astype(jnp.float32)
        total = total + arrived_ref[:, t * TILE : (t + 1) * TILE].astype(jnp.float32)
        tiles_ref[t] = total.astype(out_ref.dtype)
        columns = pl.ds((first + t) * TILE, TILE)
        copies.append(
            pltpu.make_async_copy(tiles_ref.at[t], out_ref.at[rows, columns], sent.at[t])
        )
        copies[-1].start()
    for copy in copies:
        copy.wait()


def finish(keep, got, arrived, first, top, shape, out):
    tiles = len(keep)
    before = [] if out is None else [out]
    return pl.pallas_call(
        functools.partial(finish_kernel, tiles, first, top),
        out_shape=jax.ShapeDtypeStruct(shape, arrived.dtype),
        in_specs=[vmem()] * (2 * tiles + 1) + [anywhere() for _ in before],
        out_specs=anywhere(),
        input_output_aliases={2 * tiles + 1: 0} if before else {},
        scratch_shapes=[
            pltpu.VMEM((tiles, arrived.shape[0], TILE), arrived.dtype),
            pltpu.SemaphoreType.DMA((tiles,)),
        ],
        compiler_params=params(16),
        cost_estimate=SHORT,
        name="finish",
    )(*keep, *got, arrived, *before)


def shards(ctx_size, queries, keys, values, out_weight, vertical, slash):
    local_blocks = queries.shape[0] // BLK
    assert ctx_size % 2 == 0 and (NEAR - 1) * local_blocks >= SPAN - 1
    ctx = jnp.reshape(lax.axis_index("ctx"), (1,)).astype(jnp.int32)
    tp = jnp.reshape(lax.axis_index("tp"), (1,)).astype(jnp.int32)

    def shifted(x, by):
        return lax.ppermute(x, "ctx", [(r, r + by) for r in range(ctx_size - by)])

    half = ctx_size // 2
    own, late, pair = pick(ctx, vertical, keys, values, half)
    parities = [list(range(odd, ctx_size, 2)) for odd in (0, 1)]
    pairs = [lax.all_to_all(pair, "ctx", 0, 0, axis_index_groups=parities, tiled=True)]
    needed = pairs[0][: half - 1]
    pairs.append(lax.ppermute(needed, "ctx", [(r, r ^ 1) for r in range(ctx_size)]))
    table, own_copy = tables(ctx, vertical, slash, own, half - 1)
    near_kv = [own_copy, shifted(own, 1), shifted(late, 2)]

    def sibling(x):
        return lax.ppermute(x, "tp", [(j, j ^ 1) for j in range(4)])

    def across(x):
        return lax.ppermute(x, "tp", [(j, j ^ 2) for j in range(4)])

    def attention(blocks, tiles, after):
        sizes = (vertical.shape[1], slash.shape[1])
        return attend(
            blocks, tp, ctx, queries, table, near_kv, pairs, sizes, out_weight, tiles, after
        )

    def exchanged(send, keep):
        return add(keep, [sibling(x) for x in send])

    width = out_weight.shape[1]
    tiles = width // TILE
    assert local_blocks == 8
    attended, send, keep = attention((((3, 0), (2, 0)),), HEAD, ())
    total = (keep.astype(jnp.float32) + sibling(send).astype(jnp.float32)).astype(keep.dtype)
    arrived = [across(total)]
    total = exchanged(*project_staged(attended, out_weight, HEAD * TILE, 4, total))
    arrived.append(across(total))
    (attended,) = attention((((3, 1), (2, 1)),), 0, (total,))
    total = exchanged(*project(attended, out_weight, 0, 4, (arrived[0],)))
    arrived.append(across(total))
    (attended,) = attention((((1, 0), (1, 1)), ((0, 0), (0, 1))), 0, (total, arrived[1]))
    send, keep = project(attended, out_weight, 0, tiles, ())
    got = [sibling(x) for x in send]
    shape = (queries.shape[0] // 4, width)
    out = finish(keep[:HEAD], got[:HEAD], arrived[0], 0, 0, shape, None)
    out = finish(keep[HEAD:], got[HEAD:], arrived[1], HEAD, 0, shape, out)
    return finish(keep, got, arrived[2], 0, BLK, shape, out)


def solution(mesh):
    assert mesh.shape["tp"] == 4
    return jax.shard_map(
        functools.partial(shards, mesh.shape["ctx"]),
        mesh=mesh,
        in_specs=(
            P("ctx", "tp"),
            P("ctx", "tp"),
            P("ctx", "tp"),
            P("tp", None),
            P("tp", None),
            P("tp", None),
        ),
        out_specs=P(("ctx", "tp"), None),
        check_vma=False,
    )
```

```python
import functools

import jax
import jax.numpy as jnp
from jax import lax
from jax.experimental import pallas as pl
from jax.experimental.pallas import tpu as pltpu
from jax.sharding import PartitionSpec as P

HS = 128
BLK = 64
SPAN = 16
VMOST = 2
NEAR = 3
LANES = 128
MASKED = -1e30
EXP_SCALE = 1.4426950408889634 / (HS**0.5)
TILE = 1024
HEAD = 2
MIB = 1024 * 1024


SHORT = pl.CostEstimate(flops=0, bytes_accessed=0, transcendentals=0)


def vmem():
    return pl.BlockSpec(memory_space=pltpu.VMEM)


def smem():
    return pl.BlockSpec(memory_space=pltpu.SMEM)


def anywhere():
    return pl.BlockSpec(memory_space=pl.ANY)


def params(mib):
    return pltpu.CompilerParams(vmem_limit_bytes=mib * MIB)


def picked_blocks(vertical, shard, local_blocks):
    block = vertical - shard * local_blocks
    block = jnp.where((block >= 0) & (block < local_blocks), block, local_blocks)
    first = jnp.min(block)
    second = jnp.min(jnp.where(block > first, block, local_blocks))
    return [
        pl.ds(pl.multiple_of(jnp.minimum(x, local_blocks - 1) * BLK, BLK), BLK)
        for x in (first, second)
    ]


def pick_kernel(rank_ref, vert_ref, k_ref, v_ref, both_ref, late_ref, pair_ref):
    both_ref[:, :HS] = k_ref[...]
    both_ref[:, HS:] = v_ref[...]
    late_ref[...] = both_ref[both_ref.shape[0] - late_ref.shape[0] :, :]
    blocks = picked_blocks(vert_ref[...], rank_ref[0], k_ref.shape[0] // BLK)
    for slot, rows in enumerate(blocks):
        picked = both_ref[rows, :]
        for copy in range(pair_ref.shape[0]):
            pair_ref[copy, slot * BLK : (slot + 1) * BLK, :] = picked


def pick(rank, vertical, keys, values, copies):
    return pl.pallas_call(
        pick_kernel,
        out_shape=(
            jax.ShapeDtypeStruct((keys.shape[0], 2 * HS), keys.dtype),
            jax.ShapeDtypeStruct(((SPAN - 1) * BLK - keys.shape[0], 2 * HS), keys.dtype),
            jax.ShapeDtypeStruct((copies, VMOST * BLK, 2 * HS), keys.dtype),
        ),
        in_specs=[smem(), vmem(), vmem(), vmem()],
        out_specs=(vmem(),) * 3,
        compiler_params=params(60),
        name="pick",
    )(rank, vertical, keys, values)


def member(table, blocks):
    found = table[:, :1] == blocks
    for column in range(1, table.shape[1]):
        found = found | (table[:, column : column + 1] == blocks)
    return found


def pool_blocks(vertical, rank, slots, local_blocks):
    lane = lax.broadcasted_iota(jnp.int32, (vertical.shape[0], LANES), 1)
    slot = lane // VMOST
    shard = jnp.where(slot < slots, 2 * slot + (rank & 1), 2 * (slot - slots) + 1 - (rank & 1))
    shard = jnp.where(slot < 2 * slots, shard, -1)
    first = jnp.full((1, LANES), local_blocks, jnp.int32)
    second = first
    for j in reversed(range(local_blocks)):
        here = member(vertical, shard * local_blocks + j)
        here = jnp.max(jnp.where(here, 1, 0), axis=0, keepdims=True) == 1
        second = jnp.where(here, first, second)
        first = jnp.where(here, j, first)
    picked = jnp.where(lane % VMOST == 0, first, second)
    return jnp.where((picked < local_blocks) & (shard >= 0), shard * local_blocks + picked, -1)


def tables_kernel(slots, rank_ref, vert_ref, slash_ref, own_ref, table_ref, copy_ref):
    copy_ref[...] = own_ref[...]
    local_blocks = own_ref.shape[0] // BLK
    table_ref[0, :, : vert_ref.shape[1]] = vert_ref[...]
    table_ref[1, :, : slash_ref.shape[1]] = slash_ref[...]
    table_ref[2] = pool_blocks(vert_ref[...], rank_ref[0], slots, local_blocks)


def tables(rank, vertical, slash, own, slots):
    shape = (3, vertical.shape[0], LANES)
    return pl.pallas_call(
        functools.partial(tables_kernel, slots),
        out_shape=(
            jax.ShapeDtypeStruct(shape, jnp.int32),
            jax.ShapeDtypeStruct(own.shape, own.dtype),
        ),
        in_specs=[smem(), vmem(), vmem(), vmem()],
        out_specs=(vmem(), vmem()),
        compiler_params=params(4),
        cost_estimate=SHORT,
        name="tables",
    )(rank, vertical, slash, own)


def attend_kernel(
    slots, tiles, sizes, place, tp_ref, ctx_ref, q_0, q_1, table_ref, own, kv_1, kv_2, *refs
):
    pairs = refs[:2]
    w_hbm = refs[2]
    kv_win, e_win, kv_pool, e_pool, attended, weight, arrival, landed = refs[-8:]
    outs = refs[-11:-8] if tiles else refs[-9:-8]
    step = pl.program_id(0)
    heads = table_ref.shape[1]
    rows = own.shape[0]
    local_blocks = rows // BLK
    far_rows = e_pool.shape[0]
    dtype = q_0.dtype
    rank = ctx_ref[0]
    vert = table_ref[0][:, : sizes[0]]
    slash = table_ref[1][:, : sizes[1]]
    block = table_ref[2]

    def fetch(t):
        return pltpu.make_async_copy(
            w_hbm.at[:, pl.ds(t * TILE, TILE)], weight.at[t], arrival.at[t]
        )

    def window_copies():
        reach = kv_2.shape[0]
        places = ((kv_2, 0), (kv_1, reach), (own, reach + rows))
        return [
            pltpu.make_async_copy(x, kv_win.at[pl.ds(at, x.shape[0]), :], landed.at[s])
            for s, (x, at) in enumerate(places)
        ]

    def pool_copies():
        return [
            pltpu.make_async_copy(
                x.at[pl.ds(0, slots)], kv_pool.at[pl.ds(p * slots, slots)], landed.at[NEAR + p]
            )
            for p, x in enumerate(pairs)
        ]

    @pl.when(step == 0)
    def _():
        for copy in pool_copies() + window_copies():
            copy.start()
        for t in range(tiles):
            fetch(t).start()
        key = lax.broadcasted_iota(jnp.int32, e_win.shape, 0)
        lane = lax.broadcasted_iota(jnp.int32, e_win.shape, 1)
        last = (key - (SPAN - 1) * BLK == lane - BLK) & (lane >= BLK)
        e_win[...] = jnp.where((key // BLK == lane) | last, 1.0, 0.0).astype(dtype)
        key = lax.broadcasted_iota(jnp.int32, e_pool.shape, 0)
        lane = lax.broadcasted_iota(jnp.int32, e_pool.shape, 1)
        e_pool[...] = jnp.where(key // BLK == lane, 1.0, 0.0).astype(dtype)
        for copy in pool_copies():
            copy.wait()

    lane = lax.broadcasted_iota(jnp.int32, (heads, LANES), 1)
    row = lax.broadcasted_iota(jnp.int32, (BLK, LANES), 0)
    above = lax.broadcasted_iota(jnp.int32, (BLK, LANES), 1) - BLK > row
    above = jnp.where(above, MASKED, 0.0).astype(jnp.float32)
    offset_ok = member(slash, SPAN - 1 - lane)
    pool_ok = member(vert, block) & (block >= 0)
    contract = (((1,), (1,)), ((), ()))

    def with_ones(values):
        return jnp.concatenate([values, jnp.ones((values.shape[0], LANES), dtype)], axis=1)

    queries, far_q = [], []
    for u, q_ref in enumerate((q_0, q_1)):
        q = q_ref[...]
        q = jnp.concatenate([q[:, h * HS : (h + 1) * HS] for h in range(heads)], axis=0)
        queries.append(q)
        first = rank * local_blocks + place(u, step, tp_ref) - (SPAN - 1)
        far_mask = jnp.where(pool_ok & (block < first), 0.0, MASKED).astype(jnp.float32)
        far_mask = jnp.broadcast_to(far_mask[:, None, :], (heads, BLK, LANES))
        far_mask = far_mask.reshape(heads * BLK, LANES).astype(dtype)
        far_q.append(jnp.concatenate([q, far_mask], axis=1))
    far = lax.dot_general(
        jnp.concatenate(far_q, axis=0),
        jnp.concatenate([kv_pool[:, :, :HS].reshape(far_rows, HS), e_pool[...]], axis=1),
        contract,
        preferred_element_type=jnp.float32,
    )

    @pl.when(step == 0)
    def _():
        for copy in window_copies():
            copy.wait()

    near, windows = [], []
    for u, q in enumerate(queries):
        here = place(u, step, tp_ref)
        first = rank * local_blocks + here - (SPAN - 1)
        seen = first + lane
        ok = (seen >= 0) & (offset_ok | member(vert, seen))
        mask = jnp.where(ok | (lane >= SPAN), 0.0, MASKED).astype(jnp.float32)
        mask = (mask[:, None, :] + above[None]).reshape(heads * BLK, LANES).astype(dtype)
        window = pl.ds(pl.multiple_of(here * BLK, BLK), SPAN * BLK)
        windows.append(window)
        keys = jnp.concatenate([kv_win[window, :HS], e_win[...]], axis=1)
        near.append(
            lax.dot_general(
                jnp.concatenate([q, mask], axis=1),
                keys,
                contract,
                preferred_element_type=jnp.float32,
            )
        )
    far_values = with_ones(kv_pool[:, :, HS:].reshape(far_rows, HS))
    for u in range(2):
        far_u = far[u * heads * BLK : (u + 1) * heads * BLK]
        top = jnp.maximum(
            jnp.max(near[u], axis=1, keepdims=True), jnp.max(far_u, axis=1, keepdims=True)
        )
        probs = jnp.exp2((near[u] - top) * EXP_SCALE).astype(dtype)
        values = with_ones(kv_win[windows[u], HS:])
        summed = jnp.dot(probs, values, preferred_element_type=jnp.float32)
        probs = jnp.exp2((far_u - top) * EXP_SCALE).astype(dtype)
        summed = summed + jnp.dot(probs, far_values, preferred_element_type=jnp.float32)
        out = (summed[:, :HS] / summed[:, HS:]).astype(dtype)
        at = pl.ds(pl.multiple_of((step * 2 + u) * BLK, BLK), BLK)
        for h in range(heads):
            attended[at, h * HS : (h + 1) * HS] = out[h * BLK : (h + 1) * BLK]

    @pl.when(step == pl.num_programs(0) - 1)
    def _():
        outs[0][...] = attended[...]
        half = attended.shape[0] // 2
        for t in range(tiles):
            fetch(t).wait()
            product = jnp.dot(attended[...], weight[t], preferred_element_type=jnp.float32)
            product = product.astype(dtype)
            outs[1][:, t * TILE : (t + 1) * TILE] = product[:half]
            outs[2][:, t * TILE : (t + 1) * TILE] = product[half:]


def attend(blocks, tp, ctx, queries, table, near_kv, pairs, sizes, out_weight, tiles, after):
    width = queries.shape[1]
    rows = near_kv[0].shape[0]
    assert near_kv[2].shape[0] + rows == (SPAN - 1) * BLK
    quarter = rows // BLK // 4
    steps = len(blocks)
    slots = pairs[1].shape[0]
    dtype = queries.dtype
    far = 2 * slots * VMOST * BLK

    def place(u, g, tp):
        flip, block = blocks[-1][u]
        for step in range(steps - 1):
            flip = jnp.where(g == step, blocks[step][u][0], flip)
            block = jnp.where(g == step, blocks[step][u][1], block)
        return (tp[0] ^ flip) * quarter + block

    def whole(shape):
        return pl.BlockSpec(shape, lambda g, tp, ctx: (0,) * len(shape))

    out_shapes = [(steps * 2 * BLK, width)]
    if tiles:
        out_shapes += [(steps * BLK, tiles * TILE)] * 2
    return pl.pallas_call(
        functools.partial(attend_kernel, slots, tiles, sizes, place),
        out_shape=[jax.ShapeDtypeStruct(shape, dtype) for shape in out_shapes],
        grid_spec=pltpu.PrefetchScalarGridSpec(
            num_scalar_prefetch=2,
            grid=(steps,),
            in_specs=[
                pl.BlockSpec((BLK, width), lambda g, tp, ctx: (place(0, g, tp), 0)),
                pl.BlockSpec((BLK, width), lambda g, tp, ctx: (place(1, g, tp), 0)),
            ]
            + [whole(table.shape)]
            + [anywhere() for _ in [*near_kv, *pairs, out_weight, *after]],
            out_specs=[whole(shape) for shape in out_shapes],
            scratch_shapes=[
                pltpu.VMEM((near_kv[2].shape[0] + 2 * rows, 2 * HS), dtype),
                pltpu.VMEM((SPAN * BLK, LANES), dtype),
                pltpu.VMEM((2 * slots, VMOST * BLK, 2 * HS), dtype),
                pltpu.VMEM((far, LANES), dtype),
                pltpu.VMEM((steps * 2 * BLK, width), dtype),
                pltpu.VMEM((max(tiles, 1), out_weight.shape[0], TILE), dtype),
                pltpu.SemaphoreType.DMA((max(tiles, 1),)),
                pltpu.SemaphoreType.DMA((NEAR + 2,)),
            ],
        ),
        compiler_params=params(40),
        cost_estimate=SHORT,
        name="attend",
    )(tp, ctx, queries, queries, table, *near_kv, *pairs, out_weight, *after)


def project_staged_kernel(first, a_ref, w_ref, *refs):
    tiles = len(refs) // 2
    outs = refs[-2 * tiles :]
    half, tile = outs[0].shape
    for t in range(tiles):
        weight = w_ref[:, first + t * tile : first + (t + 1) * tile]
        product = jnp.dot(a_ref[...], weight, preferred_element_type=jnp.float32)
        product = product.astype(a_ref.dtype)
        outs[t][...] = product[:half]
        outs[tiles + t][...] = product[half:]


def project_staged(attended, weight, first, tiles, after):
    rows, depth = attended.shape
    tile = (weight.shape[1] - first) // tiles
    part = jax.ShapeDtypeStruct((rows // 2, tile), attended.dtype)
    outs = pl.pallas_call(
        functools.partial(project_staged_kernel, first),
        out_shape=[part] * (2 * tiles),
        in_specs=[vmem(), vmem(), anywhere()],
        out_specs=[vmem()] * (2 * tiles),
        compiler_params=params(24),
        cost_estimate=SHORT,
        name="project",
    )(attended, weight, after)
    return outs[:tiles], outs[tiles:]


def project_kernel(first, a_ref, w_hbm, *refs):
    weight, arrival = refs[-2:]
    tiles, _, tile = weight.shape
    outs = refs[-2 - 2 * tiles : -2]
    half = outs[0].shape[0]

    def fetch(t):
        return pltpu.make_async_copy(
            w_hbm.at[:, pl.ds(first + t * tile, tile)], weight.at[t], arrival.at[t]
        )

    for t in range(tiles):
        fetch(t).start()
    for t in range(tiles):
        fetch(t).wait()
        product = jnp.dot(a_ref[...], weight[t], preferred_element_type=jnp.float32)
        product = product.astype(a_ref.dtype)
        outs[t][...] = product[:half]
        outs[tiles + t][...] = product[half:]


def project(attended, out_weight, first, tiles, after):
    rows, depth = attended.shape
    tile = (out_weight.shape[1] - first) // tiles
    part = jax.ShapeDtypeStruct((rows // 2, tile), attended.dtype)
    outs = pl.pallas_call(
        functools.partial(project_kernel, first),
        out_shape=[part] * (2 * tiles),
        in_specs=[vmem(), anywhere()] + [anywhere() for _ in after],
        out_specs=[vmem()] * (2 * tiles),
        scratch_shapes=[
            pltpu.VMEM((tiles, depth, tile), attended.dtype),
            pltpu.SemaphoreType.DMA((tiles,)),
        ],
        compiler_params=params(50),
        cost_estimate=SHORT,
        name="project",
    )(attended, out_weight, *after)
    return outs[:tiles], outs[tiles:]


def add_kernel(*refs):
    out_ref = refs[-1]
    pieces = len(refs) // 2
    first = 0
    for t in range(pieces):
        total = refs[t][...].astype(jnp.float32) + refs[pieces + t][...].astype(jnp.float32)
        last = first + total.shape[1]
        out_ref[:, first:last] = total.astype(out_ref.dtype)
        first = last


def add(keep, got):
    rows, columns = keep[0].shape[0], sum(x.shape[1] for x in keep)
    return pl.pallas_call(
        add_kernel,
        out_shape=jax.ShapeDtypeStruct((rows, columns), keep[0].dtype),
        in_specs=[vmem()] * (2 * len(keep)),
        out_specs=vmem(),
        compiler_params=params(16),
        cost_estimate=SHORT,
        name="add",
    )(*keep, *got)


def finish_kernel(tiles, first, top, *refs):
    arrived_ref = refs[2 * tiles]
    out_ref, tiles_ref, sent = refs[-3:]
    rows = pl.ds(top, arrived_ref.shape[0])
    copies = []
    for t in range(tiles):
        total = refs[t][rows, :].astype(jnp.float32) + refs[tiles + t][rows, :].astype(jnp.float32)
        total = total + arrived_ref[:, t * TILE : (t + 1) * TILE].astype(jnp.float32)
        tiles_ref[t] = total.astype(out_ref.dtype)
        columns = pl.ds((first + t) * TILE, TILE)
        copies.append(
            pltpu.make_async_copy(tiles_ref.at[t], out_ref.at[rows, columns], sent.at[t])
        )
        copies[-1].start()
    for copy in copies:
        copy.wait()


def finish(keep, got, arrived, first, top, shape, out):
    tiles = len(keep)
    before = [] if out is None else [out]
    return pl.pallas_call(
        functools.partial(finish_kernel, tiles, first, top),
        out_shape=jax.ShapeDtypeStruct(shape, arrived.dtype),
        in_specs=[vmem()] * (2 * tiles + 1) + [anywhere() for _ in before],
        out_specs=anywhere(),
        input_output_aliases={2 * tiles + 1: 0} if before else {},
        scratch_shapes=[
            pltpu.VMEM((tiles, arrived.shape[0], TILE), arrived.dtype),
            pltpu.SemaphoreType.DMA((tiles,)),
        ],
        compiler_params=params(16),
        cost_estimate=SHORT,
        name="finish",
    )(*keep, *got, arrived, *before)


def shards(ctx_size, queries, keys, values, out_weight, vertical, slash):
    local_blocks = queries.shape[0] // BLK
    assert ctx_size % 2 == 0 and (NEAR - 1) * local_blocks >= SPAN - 1
    ctx = jnp.reshape(lax.axis_index("ctx"), (1,)).astype(jnp.int32)
    tp = jnp.reshape(lax.axis_index("tp"), (1,)).astype(jnp.int32)

    def shifted(x, by):
        return lax.ppermute(x, "ctx", [(r, r + by) for r in range(ctx_size - by)])

    half = ctx_size // 2
    own, late, pair = pick(ctx, vertical, keys, values, half)
    parities = [list(range(odd, ctx_size, 2)) for odd in (0, 1)]
    pairs = [lax.all_to_all(pair, "ctx", 0, 0, axis_index_groups=parities, tiled=True)]
    needed = pairs[0][: half - 1]
    pairs.append(lax.ppermute(needed, "ctx", [(r, r ^ 1) for r in range(ctx_size)]))
    table, own_copy = tables(ctx, vertical, slash, own, half - 1)
    near_kv = [own_copy, shifted(own, 1), shifted(late, 2)]

    def sibling(x):
        return lax.ppermute(x, "tp", [(j, j ^ 1) for j in range(4)])

    def across(x):
        return lax.ppermute(x, "tp", [(j, j ^ 2) for j in range(4)])

    def attention(blocks, tiles, after):
        sizes = (vertical.shape[1], slash.shape[1])
        return attend(
            blocks, tp, ctx, queries, table, near_kv, pairs, sizes, out_weight, tiles, after
        )

    def exchanged(send, keep):
        return add(keep, [sibling(x) for x in send])

    width = out_weight.shape[1]
    tiles = width // TILE
    assert local_blocks == 8
    attended, send, keep = attention((((3, 0), (2, 0)),), HEAD, ())
    total = (keep.astype(jnp.float32) + sibling(send).astype(jnp.float32)).astype(keep.dtype)
    arrived = [across(total)]
    total = exchanged(*project_staged(attended, out_weight, HEAD * TILE, 4, total))
    arrived.append(across(total))
    (attended,) = attention((((3, 1), (2, 1)),), 0, (total,))
    total = exchanged(*project(attended, out_weight, 0, 4, (arrived[0],)))
    arrived.append(across(total))
    (attended,) = attention((((1, 0), (1, 1)), ((0, 0), (0, 1))), 0, (total, arrived[1]))
    send, keep = project(attended, out_weight, 0, tiles, ())
    got = [sibling(x) for x in send]
    shape = (queries.shape[0] // 4, width)
    out = finish(keep[:HEAD], got[:HEAD], arrived[0], 0, 0, shape, None)
    out = finish(keep[HEAD:], got[HEAD:], arrived[1], HEAD, 0, shape, out)
    return finish(keep, got, arrived[2], 0, BLK, shape, out)


def solution(mesh):
    assert mesh.shape["tp"] == 4
    return jax.shard_map(
        functools.partial(shards, mesh.shape["ctx"]),
        mesh=mesh,
        in_specs=(
            P("ctx", "tp"),
            P("ctx", "tp"),
            P("ctx", "tp"),
            P("tp", None),
            P("tp", None),
            P("tp", None),
        ),
        out_specs=P(("ctx", "tp"), None),
        check_vma=False,
    )
```

```python
import functools

import jax
import jax.numpy as jnp
from jax import lax
from jax.experimental import pallas as pl
from jax.experimental.pallas import tpu as pltpu
from jax.sharding import PartitionSpec as P

HS = 128
BLK = 64
SPAN = 16
VMOST = 2
NEAR = 3
LANES = 128
MASKED = -1e30
EXP_SCALE = 1.4426950408889634 / (HS**0.5)
TILE = 1024
HEAD = 2
MIB = 1024 * 1024


SHORT = pl.CostEstimate(flops=0, bytes_accessed=0, transcendentals=0)


def vmem():
    return pl.BlockSpec(memory_space=pltpu.VMEM)


def smem():
    return pl.BlockSpec(memory_space=pltpu.SMEM)


def anywhere():
    return pl.BlockSpec(memory_space=pl.ANY)


def params(mib):
    return pltpu.CompilerParams(vmem_limit_bytes=mib * MIB)


def picked_blocks(vertical, shard, local_blocks):
    block = vertical - shard * local_blocks
    block = jnp.where((block >= 0) & (block < local_blocks), block, local_blocks)
    first = jnp.min(block)
    second = jnp.min(jnp.where(block > first, block, local_blocks))
    return [
        pl.ds(pl.multiple_of(jnp.minimum(x, local_blocks - 1) * BLK, BLK), BLK)
        for x in (first, second)
    ]


def pick_kernel(rank_ref, vert_ref, k_ref, v_ref, both_ref, late_ref, pair_ref):
    both_ref[:, :HS] = k_ref[...]
    both_ref[:, HS:] = v_ref[...]
    late_ref[...] = both_ref[both_ref.shape[0] - late_ref.shape[0] :, :]
    blocks = picked_blocks(vert_ref[...], rank_ref[0], k_ref.shape[0] // BLK)
    for slot, rows in enumerate(blocks):
        picked = both_ref[rows, :]
        for copy in range(pair_ref.shape[0]):
            pair_ref[copy, slot * BLK : (slot + 1) * BLK, :] = picked


def pick(rank, vertical, keys, values, copies):
    return pl.pallas_call(
        pick_kernel,
        out_shape=(
            jax.ShapeDtypeStruct((keys.shape[0], 2 * HS), keys.dtype),
            jax.ShapeDtypeStruct(((SPAN - 1) * BLK - keys.shape[0], 2 * HS), keys.dtype),
            jax.ShapeDtypeStruct((copies, VMOST * BLK, 2 * HS), keys.dtype),
        ),
        in_specs=[smem(), vmem(), vmem(), vmem()],
        out_specs=(vmem(),) * 3,
        compiler_params=params(60),
        name="pick",
    )(rank, vertical, keys, values)


def member(table, blocks):
    found = table[:, :1] == blocks
    for column in range(1, table.shape[1]):
        found = found | (table[:, column : column + 1] == blocks)
    return found


def pool_blocks(vertical, rank, slots, local_blocks):
    lane = lax.broadcasted_iota(jnp.int32, (vertical.shape[0], LANES), 1)
    slot = lane // VMOST
    shard = jnp.where(slot < slots, 2 * slot + (rank & 1), 2 * (slot - slots) + 1 - (rank & 1))
    shard = jnp.where(slot < 2 * slots, shard, -1)
    first = jnp.full((1, LANES), local_blocks, jnp.int32)
    second = first
    for j in reversed(range(local_blocks)):
        here = member(vertical, shard * local_blocks + j)
        here = jnp.max(jnp.where(here, 1, 0), axis=0, keepdims=True) == 1
        second = jnp.where(here, first, second)
        first = jnp.where(here, j, first)
    picked = jnp.where(lane % VMOST == 0, first, second)
    return jnp.where((picked < local_blocks) & (shard >= 0), shard * local_blocks + picked, -1)


def tables_kernel(slots, rank_ref, vert_ref, slash_ref, own_ref, table_ref, copy_ref):
    copy_ref[...] = own_ref[...]
    local_blocks = own_ref.shape[0] // BLK
    table_ref[0, :, : vert_ref.shape[1]] = vert_ref[...]
    table_ref[1, :, : slash_ref.shape[1]] = slash_ref[...]
    table_ref[2] = pool_blocks(vert_ref[...], rank_ref[0], slots, local_blocks)


def tables(rank, vertical, slash, own, slots):
    shape = (3, vertical.shape[0], LANES)
    return pl.pallas_call(
        functools.partial(tables_kernel, slots),
        out_shape=(
            jax.ShapeDtypeStruct(shape, jnp.int32),
            jax.ShapeDtypeStruct(own.shape, own.dtype),
        ),
        in_specs=[smem(), vmem(), vmem(), vmem()],
        out_specs=(vmem(), vmem()),
        compiler_params=params(4),
        cost_estimate=SHORT,
        name="tables",
    )(rank, vertical, slash, own)


def attend_kernel(
    slots, tiles, sizes, place, tp_ref, ctx_ref, q_0, q_1, table_ref, own, kv_1, kv_2, *refs
):
    pairs = refs[:2]
    w_hbm = refs[2]
    kv_win, e_win, kv_pool, e_pool, attended, weight, arrival, landed = refs[-8:]
    outs = refs[-11:-8] if tiles else refs[-9:-8]
    step = pl.program_id(0)
    heads = table_ref.shape[1]
    rows = own.shape[0]
    local_blocks = rows // BLK
    far_rows = e_pool.shape[0]
    dtype = q_0.dtype
    rank = ctx_ref[0]
    vert = table_ref[0][:, : sizes[0]]
    slash = table_ref[1][:, : sizes[1]]
    block = table_ref[2]

    def fetch(t):
        return pltpu.make_async_copy(
            w_hbm.at[:, pl.ds(t * TILE, TILE)], weight.at[t], arrival.at[t]
        )

    @pl.when(step == 0)
    def _():
        reach = kv_2.shape[0]
        places = ((kv_2, 0), (kv_1, reach), (own, reach + rows))
        copies = [
            pltpu.make_async_copy(x, kv_win.at[pl.ds(at, x.shape[0]), :], landed.at[s])
            for s, (x, at) in enumerate(places)
        ]
        copies += [
            pltpu.make_async_copy(
                x.at[pl.ds(0, slots)], kv_pool.at[pl.ds(p * slots, slots)], landed.at[NEAR + p]
            )
            for p, x in enumerate(pairs)
        ]
        for copy in copies:
            copy.start()
        for t in range(tiles):
            fetch(t).start()
        key = lax.broadcasted_iota(jnp.int32, e_win.shape, 0)
        lane = lax.broadcasted_iota(jnp.int32, e_win.shape, 1)
        last = (key - (SPAN - 1) * BLK == lane - BLK) & (lane >= BLK)
        e_win[...] = jnp.where((key // BLK == lane) | last, 1.0, 0.0).astype(dtype)
        key = lax.broadcasted_iota(jnp.int32, e_pool.shape, 0)
        lane = lax.broadcasted_iota(jnp.int32, e_pool.shape, 1)
        e_pool[...] = jnp.where(key // BLK == lane, 1.0, 0.0).astype(dtype)
        for copy in copies:
            copy.wait()

    lane = lax.broadcasted_iota(jnp.int32, (heads, LANES), 1)
    row = lax.broadcasted_iota(jnp.int32, (BLK, LANES), 0)
    above = lax.broadcasted_iota(jnp.int32, (BLK, LANES), 1) - BLK > row
    above = jnp.where(above, MASKED, 0.0).astype(jnp.float32)
    offset_ok = member(slash, SPAN - 1 - lane)
    pool_ok = member(vert, block) & (block >= 0)
    contract = (((1,), (1,)), ((), ()))

    def with_ones(values):
        return jnp.concatenate([values, jnp.ones((values.shape[0], LANES), dtype)], axis=1)

    near, far_q, windows = [], [], []
    for u, q_ref in enumerate((q_0, q_1)):
        here = place(u, step, tp_ref)
        q = q_ref[...]
        q = jnp.concatenate([q[:, h * HS : (h + 1) * HS] for h in range(heads)], axis=0)
        first = rank * local_blocks + here - (SPAN - 1)
        seen = first + lane
        ok = (seen >= 0) & (offset_ok | member(vert, seen))
        mask = jnp.where(ok | (lane >= SPAN), 0.0, MASKED).astype(jnp.float32)
        mask = (mask[:, None, :] + above[None]).reshape(heads * BLK, LANES).astype(dtype)
        far_mask = jnp.where(pool_ok & (block < first), 0.0, MASKED).astype(jnp.float32)
        far_mask = jnp.broadcast_to(far_mask[:, None, :], (heads, BLK, LANES))
        far_mask = far_mask.reshape(heads * BLK, LANES).astype(dtype)
        far_q.append(jnp.concatenate([q, far_mask], axis=1))
        window = pl.ds(pl.multiple_of(here * BLK, BLK), SPAN * BLK)
        windows.append(window)
        keys = jnp.concatenate([kv_win[window, :HS], e_win[...]], axis=1)
        near.append(
            lax.dot_general(
                jnp.concatenate([q, mask], axis=1),
                keys,
                contract,
                preferred_element_type=jnp.float32,
            )
        )
    far = lax.dot_general(
        jnp.concatenate(far_q, axis=0),
        jnp.concatenate([kv_pool[:, :, :HS].reshape(far_rows, HS), e_pool[...]], axis=1),
        contract,
        preferred_element_type=jnp.float32,
    )
    far_values = with_ones(kv_pool[:, :, HS:].reshape(far_rows, HS))
    for u in range(2):
        far_u = far[u * heads * BLK : (u + 1) * heads * BLK]
        top = jnp.maximum(
            jnp.max(near[u], axis=1, keepdims=True), jnp.max(far_u, axis=1, keepdims=True)
        )
        probs = jnp.exp2((near[u] - top) * EXP_SCALE).astype(dtype)
        values = with_ones(kv_win[windows[u], HS:])
        summed = jnp.dot(probs, values, preferred_element_type=jnp.float32)
        probs = jnp.exp2((far_u - top) * EXP_SCALE).astype(dtype)
        summed = summed + jnp.dot(probs, far_values, preferred_element_type=jnp.float32)
        out = (summed[:, :HS] / summed[:, HS:]).astype(dtype)
        at = pl.ds(pl.multiple_of((step * 2 + u) * BLK, BLK), BLK)
        for h in range(heads):
            attended[at, h * HS : (h + 1) * HS] = out[h * BLK : (h + 1) * BLK]

    @pl.when(step == pl.num_programs(0) - 1)
    def _():
        outs[0][...] = attended[...]
        half = attended.shape[0] // 2
        for t in range(tiles):
            fetch(t).wait()
            product = jnp.dot(attended[...], weight[t], preferred_element_type=jnp.float32)
            product = product.astype(dtype)
            outs[1][:, t * TILE : (t + 1) * TILE] = product[:half]
            outs[2][:, t * TILE : (t + 1) * TILE] = product[half:]


def attend(blocks, tp, ctx, queries, table, near_kv, pairs, sizes, out_weight, tiles, after):
    width = queries.shape[1]
    rows = near_kv[0].shape[0]
    assert near_kv[2].shape[0] + rows == (SPAN - 1) * BLK
    quarter = rows // BLK // 4
    steps = len(blocks)
    slots = pairs[1].shape[0]
    dtype = queries.dtype
    far = 2 * slots * VMOST * BLK

    def place(u, g, tp):
        flip, block = blocks[-1][u]
        for step in range(steps - 1):
            flip = jnp.where(g == step, blocks[step][u][0], flip)
            block = jnp.where(g == step, blocks[step][u][1], block)
        return (tp[0] ^ flip) * quarter + block

    def whole(shape):
        return pl.BlockSpec(shape, lambda g, tp, ctx: (0,) * len(shape))

    out_shapes = [(steps * 2 * BLK, width)]
    if tiles:
        out_shapes += [(steps * BLK, tiles * TILE)] * 2
    return pl.pallas_call(
        functools.partial(attend_kernel, slots, tiles, sizes, place),
        out_shape=[jax.ShapeDtypeStruct(shape, dtype) for shape in out_shapes],
        grid_spec=pltpu.PrefetchScalarGridSpec(
            num_scalar_prefetch=2,
            grid=(steps,),
            in_specs=[
                pl.BlockSpec((BLK, width), lambda g, tp, ctx: (place(0, g, tp), 0)),
                pl.BlockSpec((BLK, width), lambda g, tp, ctx: (place(1, g, tp), 0)),
            ]
            + [whole(table.shape)]
            + [anywhere() for _ in [*near_kv, *pairs, out_weight, *after]],
            out_specs=[whole(shape) for shape in out_shapes],
            scratch_shapes=[
                pltpu.VMEM((near_kv[2].shape[0] + 2 * rows, 2 * HS), dtype),
                pltpu.VMEM((SPAN * BLK, LANES), dtype),
                pltpu.VMEM((2 * slots, VMOST * BLK, 2 * HS), dtype),
                pltpu.VMEM((far, LANES), dtype),
                pltpu.VMEM((steps * 2 * BLK, width), dtype),
                pltpu.VMEM((max(tiles, 1), out_weight.shape[0], TILE), dtype),
                pltpu.SemaphoreType.DMA((max(tiles, 1),)),
                pltpu.SemaphoreType.DMA((NEAR + 2,)),
            ],
        ),
        compiler_params=params(40),
        cost_estimate=SHORT,
        name="attend",
    )(tp, ctx, queries, queries, table, *near_kv, *pairs, out_weight, *after)


def project_staged_kernel(first, a_ref, w_ref, *refs):
    tiles = len(refs) // 2
    outs = refs[-2 * tiles :]
    half, tile = outs[0].shape
    for t in range(tiles):
        weight = w_ref[:, first + t * tile : first + (t + 1) * tile]
        product = jnp.dot(a_ref[...], weight, preferred_element_type=jnp.float32)
        product = product.astype(a_ref.dtype)
        outs[t][...] = product[:half]
        outs[tiles + t][...] = product[half:]


def project_staged(attended, weight, first, tiles, after):
    rows, depth = attended.shape
    tile = (weight.shape[1] - first) // tiles
    part = jax.ShapeDtypeStruct((rows // 2, tile), attended.dtype)
    outs = pl.pallas_call(
        functools.partial(project_staged_kernel, first),
        out_shape=[part] * (2 * tiles),
        in_specs=[vmem(), vmem(), anywhere()],
        out_specs=[vmem()] * (2 * tiles),
        compiler_params=params(24),
        cost_estimate=SHORT,
        name="project",
    )(attended, weight, after)
    return outs[:tiles], outs[tiles:]


def project_kernel(first, a_ref, w_hbm, *refs):
    weight, arrival = refs[-2:]
    tiles, _, tile = weight.shape
    outs = refs[-2 - 2 * tiles : -2]
    half = outs[0].shape[0]

    def fetch(t):
        return pltpu.make_async_copy(
            w_hbm.at[:, pl.ds(first + t * tile, tile)], weight.at[t], arrival.at[t]
        )

    for t in range(tiles):
        fetch(t).start()
    for t in range(tiles):
        fetch(t).wait()
        product = jnp.dot(a_ref[...], weight[t], preferred_element_type=jnp.float32)
        product = product.astype(a_ref.dtype)
        outs[t][...] = product[:half]
        outs[tiles + t][...] = product[half:]


def project(attended, out_weight, first, tiles, after):
    rows, depth = attended.shape
    tile = (out_weight.shape[1] - first) // tiles
    part = jax.ShapeDtypeStruct((rows // 2, tile), attended.dtype)
    outs = pl.pallas_call(
        functools.partial(project_kernel, first),
        out_shape=[part] * (2 * tiles),
        in_specs=[vmem(), anywhere()] + [anywhere() for _ in after],
        out_specs=[vmem()] * (2 * tiles),
        scratch_shapes=[
            pltpu.VMEM((tiles, depth, tile), attended.dtype),
            pltpu.SemaphoreType.DMA((tiles,)),
        ],
        compiler_params=params(50),
        cost_estimate=SHORT,
        name="project",
    )(attended, out_weight, *after)
    return outs[:tiles], outs[tiles:]


def add_kernel(*refs):
    out_ref = refs[-1]
    pieces = len(refs) // 2
    first = 0
    for t in range(pieces):
        total = refs[t][...].astype(jnp.float32) + refs[pieces + t][...].astype(jnp.float32)
        last = first + total.shape[1]
        out_ref[:, first:last] = total.astype(out_ref.dtype)
        first = last


def add(keep, got):
    rows, columns = keep[0].shape[0], sum(x.shape[1] for x in keep)
    return pl.pallas_call(
        add_kernel,
        out_shape=jax.ShapeDtypeStruct((rows, columns), keep[0].dtype),
        in_specs=[vmem()] * (2 * len(keep)),
        out_specs=vmem(),
        compiler_params=params(16),
        cost_estimate=SHORT,
        name="add",
    )(*keep, *got)


def finish_kernel(tiles, first, top, *refs):
    arrived_ref = refs[2 * tiles]
    out_ref, tiles_ref, sent = refs[-3:]
    rows = pl.ds(top, arrived_ref.shape[0])
    copies = []
    for t in range(tiles):
        total = refs[t][rows, :].astype(jnp.float32) + refs[tiles + t][rows, :].astype(jnp.float32)
        total = total + arrived_ref[:, t * TILE : (t + 1) * TILE].astype(jnp.float32)
        tiles_ref[t] = total.astype(out_ref.dtype)
        columns = pl.ds((first + t) * TILE, TILE)
        copies.append(
            pltpu.make_async_copy(tiles_ref.at[t], out_ref.at[rows, columns], sent.at[t])
        )
        copies[-1].start()
    for copy in copies:
        copy.wait()


def finish(keep, got, arrived, first, top, shape, out):
    tiles = len(keep)
    before = [] if out is None else [out]
    return pl.pallas_call(
        functools.partial(finish_kernel, tiles, first, top),
        out_shape=jax.ShapeDtypeStruct(shape, arrived.dtype),
        in_specs=[vmem()] * (2 * tiles + 1) + [anywhere() for _ in before],
        out_specs=anywhere(),
        input_output_aliases={2 * tiles + 1: 0} if before else {},
        scratch_shapes=[
            pltpu.VMEM((tiles, arrived.shape[0], TILE), arrived.dtype),
            pltpu.SemaphoreType.DMA((tiles,)),
        ],
        compiler_params=params(16),
        cost_estimate=SHORT,
        name="finish",
    )(*keep, *got, arrived, *before)


def own_kernel(top, *refs):
    out_ref = refs[-1]
    tiles = len(refs) // 2
    rows = pl.ds(top, out_ref.shape[0])
    for t in range(tiles):
        total = refs[t][rows, :].astype(jnp.float32) + refs[tiles + t][rows, :].astype(jnp.float32)
        out_ref[:, t * TILE : (t + 1) * TILE] = total


def own_sum(keep, got, top):
    rows = keep[0].shape[0] - top
    return pl.pallas_call(
        functools.partial(own_kernel, top),
        out_shape=jax.ShapeDtypeStruct((rows, len(keep) * TILE), jnp.float32),
        in_specs=[vmem()] * (2 * len(keep)),
        out_specs=vmem(),
        compiler_params=params(16),
        cost_estimate=SHORT,
        name="own",
    )(*keep, *got)


def last_kernel(top, own_ref, arrived_ref, _, out_ref, tiles_ref, sent):
    rows = pl.ds(top, own_ref.shape[0])
    copies = []
    for t in range(tiles_ref.shape[0]):
        at = slice(t * TILE, (t + 1) * TILE)
        total = own_ref[:, at] + arrived_ref[:, at].astype(jnp.float32)
        tiles_ref[t] = total.astype(out_ref.dtype)
        columns = pl.ds(t * TILE, TILE)
        copies.append(
            pltpu.make_async_copy(tiles_ref.at[t], out_ref.at[rows, columns], sent.at[t])
        )
        copies[-1].start()
    for copy in copies:
        copy.wait()


def finish_last(own, arrived, top, out):
    rows, columns = arrived.shape
    tiles = columns // TILE
    return pl.pallas_call(
        functools.partial(last_kernel, top),
        out_shape=jax.ShapeDtypeStruct(out.shape, out.dtype),
        in_specs=[vmem(), vmem(), anywhere()],
        out_specs=anywhere(),
        input_output_aliases={2: 0},
        scratch_shapes=[
            pltpu.VMEM((tiles, rows, TILE), out.dtype),
            pltpu.SemaphoreType.DMA((tiles,)),
        ],
        compiler_params=params(16),
        cost_estimate=SHORT,
        name="last",
    )(own, arrived, out)


def shards(ctx_size, queries, keys, values, out_weight, vertical, slash):
    local_blocks = queries.shape[0] // BLK
    assert ctx_size % 2 == 0 and (NEAR - 1) * local_blocks >= SPAN - 1
    ctx = jnp.reshape(lax.axis_index("ctx"), (1,)).astype(jnp.int32)
    tp = jnp.reshape(lax.axis_index("tp"), (1,)).astype(jnp.int32)

    def shifted(x, by):
        return lax.ppermute(x, "ctx", [(r, r + by) for r in range(ctx_size - by)])

    half = ctx_size // 2
    own, late, pair = pick(ctx, vertical, keys, values, half)
    parities = [list(range(odd, ctx_size, 2)) for odd in (0, 1)]
    pairs = [lax.all_to_all(pair, "ctx", 0, 0, axis_index_groups=parities, tiled=True)]
    needed = pairs[0][: half - 1]
    pairs.append(lax.ppermute(needed, "ctx", [(r, r ^ 1) for r in range(ctx_size)]))
    table, own_copy = tables(ctx, vertical, slash, own, half - 1)
    near_kv = [own_copy, shifted(own, 1), shifted(late, 2)]

    def sibling(x):
        return lax.ppermute(x, "tp", [(j, j ^ 1) for j in range(4)])

    def across(x):
        return lax.ppermute(x, "tp", [(j, j ^ 2) for j in range(4)])

    def attention(blocks, tiles, after):
        sizes = (vertical.shape[1], slash.shape[1])
        return attend(
            blocks, tp, ctx, queries, table, near_kv, pairs, sizes, out_weight, tiles, after
        )

    def exchanged(send, keep):
        return add(keep, [sibling(x) for x in send])

    width = out_weight.shape[1]
    tiles = width // TILE
    assert local_blocks == 8
    attended, send, keep = attention((((3, 0), (2, 0)),), HEAD, ())
    total = (keep.astype(jnp.float32) + sibling(send).astype(jnp.float32)).astype(keep.dtype)
    arrived = [across(total)]
    total = exchanged(*project_staged(attended, out_weight, HEAD * TILE, 4, total))
    arrived.append(across(total))
    (attended,) = attention((((3, 1), (2, 1)),), 0, (total,))
    total = exchanged(*project(attended, out_weight, 0, 4, (arrived[0],)))
    arrived.append(across(total))
    (attended,) = attention((((1, 0), (1, 1)), ((0, 0), (0, 1))), 0, (total, arrived[1]))
    send, keep = project(attended, out_weight, 0, tiles, ())
    got = [sibling(x) for x in send]
    shape = (queries.shape[0] // 4, width)
    out = finish(keep[:HEAD], got[:HEAD], arrived[0], 0, 0, shape, None)
    out = finish(keep[HEAD:], got[HEAD:], arrived[1], HEAD, 0, shape, out)
    return finish_last(own_sum(keep, got, BLK), arrived[2], BLK, out)


def solution(mesh):
    assert mesh.shape["tp"] == 4
    return jax.shard_map(
        functools.partial(shards, mesh.shape["ctx"]),
        mesh=mesh,
        in_specs=(
            P("ctx", "tp"),
            P("ctx", "tp"),
            P("ctx", "tp"),
            P("tp", None),
            P("tp", None),
            P("tp", None),
        ),
        out_specs=P(("ctx", "tp"), None),
        check_vma=False,
    )
```

```python
import functools

import jax
import jax.numpy as jnp
from jax import lax
from jax.experimental import pallas as pl
from jax.experimental.pallas import tpu as pltpu
from jax.sharding import PartitionSpec as P

HS = 128
BLK = 64
SPAN = 16
VMOST = 2
NEAR = 3
LANES = 128
MASKED = -1e30
EXP_SCALE = 1.4426950408889634 / (HS**0.5)
TILE = 1024
HEAD = 2
MIB = 1024 * 1024


SHORT = pl.CostEstimate(flops=0, bytes_accessed=0, transcendentals=0)


def vmem():
    return pl.BlockSpec(memory_space=pltpu.VMEM)


def smem():
    return pl.BlockSpec(memory_space=pltpu.SMEM)


def anywhere():
    return pl.BlockSpec(memory_space=pl.ANY)


def params(mib):
    return pltpu.CompilerParams(vmem_limit_bytes=mib * MIB)


def picked_blocks(vertical, shard, local_blocks):
    block = vertical - shard * local_blocks
    block = jnp.where((block >= 0) & (block < local_blocks), block, local_blocks)
    first = jnp.min(block)
    second = jnp.min(jnp.where(block > first, block, local_blocks))
    return [
        pl.ds(pl.multiple_of(jnp.minimum(x, local_blocks - 1) * BLK, BLK), BLK)
        for x in (first, second)
    ]


def pick_kernel(rank_ref, vert_ref, k_ref, v_ref, both_ref, late_ref, pair_ref):
    both_ref[:, :HS] = k_ref[...]
    both_ref[:, HS:] = v_ref[...]
    late_ref[...] = both_ref[both_ref.shape[0] - late_ref.shape[0] :, :]
    blocks = picked_blocks(vert_ref[...], rank_ref[0], k_ref.shape[0] // BLK)
    for slot, rows in enumerate(blocks):
        picked = both_ref[rows, :]
        for copy in range(pair_ref.shape[0]):
            pair_ref[copy, slot * BLK : (slot + 1) * BLK, :] = picked


def pick(rank, vertical, keys, values, copies):
    return pl.pallas_call(
        pick_kernel,
        out_shape=(
            jax.ShapeDtypeStruct((keys.shape[0], 2 * HS), keys.dtype),
            jax.ShapeDtypeStruct(((SPAN - 1) * BLK - keys.shape[0], 2 * HS), keys.dtype),
            jax.ShapeDtypeStruct((copies, VMOST * BLK, 2 * HS), keys.dtype),
        ),
        in_specs=[smem(), vmem(), vmem(), vmem()],
        out_specs=(vmem(),) * 3,
        compiler_params=params(60),
        name="pick",
    )(rank, vertical, keys, values)


def member(table, blocks):
    found = table[:, :1] == blocks
    for column in range(1, table.shape[1]):
        found = found | (table[:, column : column + 1] == blocks)
    return found


def pool_blocks(vertical, rank, slots, local_blocks):
    lane = lax.broadcasted_iota(jnp.int32, (vertical.shape[0], LANES), 1)
    slot = lane // VMOST
    shard = jnp.where(slot < slots, 2 * slot + (rank & 1), 2 * (slot - slots) + 1 - (rank & 1))
    shard = jnp.where(slot < 2 * slots, shard, -1)
    first = jnp.full((1, LANES), local_blocks, jnp.int32)
    second = first
    for j in reversed(range(local_blocks)):
        here = member(vertical, shard * local_blocks + j)
        here = jnp.max(jnp.where(here, 1, 0), axis=0, keepdims=True) == 1
        second = jnp.where(here, first, second)
        first = jnp.where(here, j, first)
    picked = jnp.where(lane % VMOST == 0, first, second)
    return jnp.where((picked < local_blocks) & (shard >= 0), shard * local_blocks + picked, -1)


def tables_kernel(slots, rank_ref, vert_ref, slash_ref, own_ref, table_ref, copy_ref):
    copy_ref[...] = own_ref[...]
    local_blocks = own_ref.shape[0] // BLK
    table_ref[0, :, : vert_ref.shape[1]] = vert_ref[...]
    table_ref[1, :, : slash_ref.shape[1]] = slash_ref[...]
    table_ref[2] = pool_blocks(vert_ref[...], rank_ref[0], slots, local_blocks)


def tables(rank, vertical, slash, own, slots):
    shape = (3, vertical.shape[0], LANES)
    return pl.pallas_call(
        functools.partial(tables_kernel, slots),
        out_shape=(
            jax.ShapeDtypeStruct(shape, jnp.int32),
            jax.ShapeDtypeStruct(own.shape, own.dtype),
        ),
        in_specs=[smem(), vmem(), vmem(), vmem()],
        out_specs=(vmem(), vmem()),
        compiler_params=params(4),
        cost_estimate=SHORT,
        name="tables",
    )(rank, vertical, slash, own)


def attend_kernel(
    slots, tiles, sizes, place, tp_ref, ctx_ref, q_0, q_1, table_ref, own, kv_1, kv_2, *refs
):
    pairs = refs[:2]
    w_hbm = refs[2]
    kv_win, e_win, kv_pool, e_pool, attended, weight, arrival, landed = refs[-8:]
    outs = refs[-11:-8] if tiles else refs[-9:-8]
    step = pl.program_id(0)
    heads = table_ref.shape[1]
    rows = own.shape[0]
    local_blocks = rows // BLK
    far_rows = e_pool.shape[0]
    dtype = q_0.dtype
    rank = ctx_ref[0]
    vert = table_ref[0][:, : sizes[0]]
    slash = table_ref[1][:, : sizes[1]]
    block = table_ref[2]

    parts = arrival.shape[1]
    depth = weight.shape[1] // parts

    def fetch(t):
        ats = [pl.ds(p * depth, depth) for p in range(parts)]
        return [
            pltpu.make_async_copy(
                w_hbm.at[at, pl.ds(t * TILE, TILE)], weight.at[t, at], arrival.at[t, p]
            )
            for p, at in enumerate(ats)
        ]

    @pl.when(step == 0)
    def _():
        reach = kv_2.shape[0]
        places = ((kv_2, 0), (kv_1, reach), (own, reach + rows))
        copies = [
            pltpu.make_async_copy(x, kv_win.at[pl.ds(at, x.shape[0]), :], landed.at[s])
            for s, (x, at) in enumerate(places)
        ]
        copies += [
            pltpu.make_async_copy(
                x.at[pl.ds(0, slots)], kv_pool.at[pl.ds(p * slots, slots)], landed.at[NEAR + p]
            )
            for p, x in enumerate(pairs)
        ]
        for copy in copies:
            copy.start()
        for t in range(tiles):
            for copy in fetch(t):
                copy.start()
        key = lax.broadcasted_iota(jnp.int32, e_win.shape, 0)
        lane = lax.broadcasted_iota(jnp.int32, e_win.shape, 1)
        last = (key - (SPAN - 1) * BLK == lane - BLK) & (lane >= BLK)
        e_win[...] = jnp.where((key // BLK == lane) | last, 1.0, 0.0).astype(dtype)
        key = lax.broadcasted_iota(jnp.int32, e_pool.shape, 0)
        lane = lax.broadcasted_iota(jnp.int32, e_pool.shape, 1)
        e_pool[...] = jnp.where(key // BLK == lane, 1.0, 0.0).astype(dtype)
        for copy in copies:
            copy.wait()

    lane = lax.broadcasted_iota(jnp.int32, (heads, LANES), 1)
    row = lax.broadcasted_iota(jnp.int32, (BLK, LANES), 0)
    above = lax.broadcasted_iota(jnp.int32, (BLK, LANES), 1) - BLK > row
    above = jnp.where(above, MASKED, 0.0).astype(jnp.float32)
    offset_ok = member(slash, SPAN - 1 - lane)
    pool_ok = member(vert, block) & (block >= 0)
    contract = (((1,), (1,)), ((), ()))

    def with_ones(values):
        return jnp.concatenate([values, jnp.ones((values.shape[0], LANES), dtype)], axis=1)

    near, far_q, windows = [], [], []
    for u, q_ref in enumerate((q_0, q_1)):
        here = place(u, step, tp_ref)
        q = q_ref[...]
        q = jnp.concatenate([q[:, h * HS : (h + 1) * HS] for h in range(heads)], axis=0)
        first = rank * local_blocks + here - (SPAN - 1)
        seen = first + lane
        ok = (seen >= 0) & (offset_ok | member(vert, seen))
        mask = jnp.where(ok | (lane >= SPAN), 0.0, MASKED).astype(jnp.float32)
        mask = (mask[:, None, :] + above[None]).reshape(heads * BLK, LANES).astype(dtype)
        far_mask = jnp.where(pool_ok & (block < first), 0.0, MASKED).astype(jnp.float32)
        far_mask = jnp.broadcast_to(far_mask[:, None, :], (heads, BLK, LANES))
        far_mask = far_mask.reshape(heads * BLK, LANES).astype(dtype)
        far_q.append(jnp.concatenate([q, far_mask], axis=1))
        window = pl.ds(pl.multiple_of(here * BLK, BLK), SPAN * BLK)
        windows.append(window)
        keys = jnp.concatenate([kv_win[window, :HS], e_win[...]], axis=1)
        near.append(
            lax.dot_general(
                jnp.concatenate([q, mask], axis=1),
                keys,
                contract,
                preferred_element_type=jnp.float32,
            )
        )
    far = lax.dot_general(
        jnp.concatenate(far_q, axis=0),
        jnp.concatenate([kv_pool[:, :, :HS].reshape(far_rows, HS), e_pool[...]], axis=1),
        contract,
        preferred_element_type=jnp.float32,
    )
    far_values = with_ones(kv_pool[:, :, HS:].reshape(far_rows, HS))
    for u in range(2):
        far_u = far[u * heads * BLK : (u + 1) * heads * BLK]
        top = jnp.maximum(
            jnp.max(near[u], axis=1, keepdims=True), jnp.max(far_u, axis=1, keepdims=True)
        )
        probs = jnp.exp2((near[u] - top) * EXP_SCALE).astype(dtype)
        values = with_ones(kv_win[windows[u], HS:])
        summed = jnp.dot(probs, values, preferred_element_type=jnp.float32)
        probs = jnp.exp2((far_u - top) * EXP_SCALE).astype(dtype)
        summed = summed + jnp.dot(probs, far_values, preferred_element_type=jnp.float32)
        out = (summed[:, :HS] / summed[:, HS:]).astype(dtype)
        at = pl.ds(pl.multiple_of((step * 2 + u) * BLK, BLK), BLK)
        for h in range(heads):
            attended[at, h * HS : (h + 1) * HS] = out[h * BLK : (h + 1) * BLK]

    @pl.when(step == pl.num_programs(0) - 1)
    def _():
        outs[0][...] = attended[...]
        half = attended.shape[0] // 2
        for t in range(tiles):
            for copy in fetch(t):
                copy.wait()
            product = jnp.dot(attended[...], weight[t], preferred_element_type=jnp.float32)
            product = product.astype(dtype)
            outs[1][:, t * TILE : (t + 1) * TILE] = product[:half]
            outs[2][:, t * TILE : (t + 1) * TILE] = product[half:]


def attend(blocks, tp, ctx, queries, table, near_kv, pairs, sizes, out_weight, tiles, after):
    width = queries.shape[1]
    rows = near_kv[0].shape[0]
    assert near_kv[2].shape[0] + rows == (SPAN - 1) * BLK
    quarter = rows // BLK // 4
    steps = len(blocks)
    slots = pairs[1].shape[0]
    dtype = queries.dtype
    far = 2 * slots * VMOST * BLK

    def place(u, g, tp):
        flip, block = blocks[-1][u]
        for step in range(steps - 1):
            flip = jnp.where(g == step, blocks[step][u][0], flip)
            block = jnp.where(g == step, blocks[step][u][1], block)
        return (tp[0] ^ flip) * quarter + block

    def whole(shape):
        return pl.BlockSpec(shape, lambda g, tp, ctx: (0,) * len(shape))

    out_shapes = [(steps * 2 * BLK, width)]
    if tiles:
        out_shapes += [(steps * BLK, tiles * TILE)] * 2
    return pl.pallas_call(
        functools.partial(attend_kernel, slots, tiles, sizes, place),
        out_shape=[jax.ShapeDtypeStruct(shape, dtype) for shape in out_shapes],
        grid_spec=pltpu.PrefetchScalarGridSpec(
            num_scalar_prefetch=2,
            grid=(steps,),
            in_specs=[
                pl.BlockSpec((BLK, width), lambda g, tp, ctx: (place(0, g, tp), 0)),
                pl.BlockSpec((BLK, width), lambda g, tp, ctx: (place(1, g, tp), 0)),
            ]
            + [whole(table.shape)]
            + [anywhere() for _ in [*near_kv, *pairs, out_weight, *after]],
            out_specs=[whole(shape) for shape in out_shapes],
            scratch_shapes=[
                pltpu.VMEM((near_kv[2].shape[0] + 2 * rows, 2 * HS), dtype),
                pltpu.VMEM((SPAN * BLK, LANES), dtype),
                pltpu.VMEM((2 * slots, VMOST * BLK, 2 * HS), dtype),
                pltpu.VMEM((far, LANES), dtype),
                pltpu.VMEM((steps * 2 * BLK, width), dtype),
                pltpu.VMEM((max(tiles, 1), out_weight.shape[0], TILE), dtype),
                pltpu.SemaphoreType.DMA((max(tiles, 1), 4)),
                pltpu.SemaphoreType.DMA((NEAR + 2,)),
            ],
        ),
        compiler_params=params(40),
        cost_estimate=SHORT,
        name="attend",
    )(tp, ctx, queries, queries, table, *near_kv, *pairs, out_weight, *after)


def project_staged_kernel(first, a_ref, w_ref, *refs):
    tiles = len(refs) // 2
    outs = refs[-2 * tiles :]
    half, tile = outs[0].shape
    for t in range(tiles):
        weight = w_ref[:, first + t * tile : first + (t + 1) * tile]
        product = jnp.dot(a_ref[...], weight, preferred_element_type=jnp.float32)
        product = product.astype(a_ref.dtype)
        outs[t][...] = product[:half]
        outs[tiles + t][...] = product[half:]


def project_staged(attended, weight, first, tiles, after):
    rows, depth = attended.shape
    tile = (weight.shape[1] - first) // tiles
    part = jax.ShapeDtypeStruct((rows // 2, tile), attended.dtype)
    outs = pl.pallas_call(
        functools.partial(project_staged_kernel, first),
        out_shape=[part] * (2 * tiles),
        in_specs=[vmem(), vmem(), anywhere()],
        out_specs=[vmem()] * (2 * tiles),
        compiler_params=params(24),
        cost_estimate=SHORT,
        name="project",
    )(attended, weight, after)
    return outs[:tiles], outs[tiles:]


def project_kernel(first, a_ref, w_hbm, *refs):
    weight, arrival = refs[-2:]
    tiles, _, tile = weight.shape
    outs = refs[-2 - 2 * tiles : -2]
    half = outs[0].shape[0]

    def fetch(t):
        return pltpu.make_async_copy(
            w_hbm.at[:, pl.ds(first + t * tile, tile)], weight.at[t], arrival.at[t]
        )

    for t in range(tiles):
        fetch(t).start()
    for t in range(tiles):
        fetch(t).wait()
        product = jnp.dot(a_ref[...], weight[t], preferred_element_type=jnp.float32)
        product = product.astype(a_ref.dtype)
        outs[t][...] = product[:half]
        outs[tiles + t][...] = product[half:]


def project(attended, out_weight, first, tiles, after):
    rows, depth = attended.shape
    tile = (out_weight.shape[1] - first) // tiles
    part = jax.ShapeDtypeStruct((rows // 2, tile), attended.dtype)
    outs = pl.pallas_call(
        functools.partial(project_kernel, first),
        out_shape=[part] * (2 * tiles),
        in_specs=[vmem(), anywhere()] + [anywhere() for _ in after],
        out_specs=[vmem()] * (2 * tiles),
        scratch_shapes=[
            pltpu.VMEM((tiles, depth, tile), attended.dtype),
            pltpu.SemaphoreType.DMA((tiles,)),
        ],
        compiler_params=params(50),
        cost_estimate=SHORT,
        name="project",
    )(attended, out_weight, *after)
    return outs[:tiles], outs[tiles:]


def add_kernel(*refs):
    out_ref = refs[-1]
    pieces = len(refs) // 2
    first = 0
    for t in range(pieces):
        total = refs[t][...].astype(jnp.float32) + refs[pieces + t][...].astype(jnp.float32)
        last = first + total.shape[1]
        out_ref[:, first:last] = total.astype(out_ref.dtype)
        first = last


def add(keep, got):
    rows, columns = keep[0].shape[0], sum(x.shape[1] for x in keep)
    return pl.pallas_call(
        add_kernel,
        out_shape=jax.ShapeDtypeStruct((rows, columns), keep[0].dtype),
        in_specs=[vmem()] * (2 * len(keep)),
        out_specs=vmem(),
        compiler_params=params(16),
        cost_estimate=SHORT,
        name="add",
    )(*keep, *got)


def finish_kernel(tiles, first, top, *refs):
    arrived_ref = refs[2 * tiles]
    out_ref, tiles_ref, sent = refs[-3:]
    rows = pl.ds(top, arrived_ref.shape[0])
    copies = []
    for t in range(tiles):
        total = refs[t][rows, :].astype(jnp.float32) + refs[tiles + t][rows, :].astype(jnp.float32)
        total = total + arrived_ref[:, t * TILE : (t + 1) * TILE].astype(jnp.float32)
        tiles_ref[t] = total.astype(out_ref.dtype)
        columns = pl.ds((first + t) * TILE, TILE)
        copies.append(
            pltpu.make_async_copy(tiles_ref.at[t], out_ref.at[rows, columns], sent.at[t])
        )
        copies[-1].start()
    for copy in copies:
        copy.wait()


def finish(keep, got, arrived, first, top, shape, out):
    tiles = len(keep)
    before = [] if out is None else [out]
    return pl.pallas_call(
        functools.partial(finish_kernel, tiles, first, top),
        out_shape=jax.ShapeDtypeStruct(shape, arrived.dtype),
        in_specs=[vmem()] * (2 * tiles + 1) + [anywhere() for _ in before],
        out_specs=anywhere(),
        input_output_aliases={2 * tiles + 1: 0} if before else {},
        scratch_shapes=[
            pltpu.VMEM((tiles, arrived.shape[0], TILE), arrived.dtype),
            pltpu.SemaphoreType.DMA((tiles,)),
        ],
        compiler_params=params(16),
        cost_estimate=SHORT,
        name="finish",
    )(*keep, *got, arrived, *before)


def shards(ctx_size, queries, keys, values, out_weight, vertical, slash):
    local_blocks = queries.shape[0] // BLK
    assert ctx_size % 2 == 0 and (NEAR - 1) * local_blocks >= SPAN - 1
    ctx = jnp.reshape(lax.axis_index("ctx"), (1,)).astype(jnp.int32)
    tp = jnp.reshape(lax.axis_index("tp"), (1,)).astype(jnp.int32)

    def shifted(x, by):
        return lax.ppermute(x, "ctx", [(r, r + by) for r in range(ctx_size - by)])

    half = ctx_size // 2
    own, late, pair = pick(ctx, vertical, keys, values, half)
    parities = [list(range(odd, ctx_size, 2)) for odd in (0, 1)]
    pairs = [lax.all_to_all(pair, "ctx", 0, 0, axis_index_groups=parities, tiled=True)]
    needed = pairs[0][: half - 1]
    pairs.append(lax.ppermute(needed, "ctx", [(r, r ^ 1) for r in range(ctx_size)]))
    table, own_copy = tables(ctx, vertical, slash, own, half - 1)
    near_kv = [own_copy, shifted(own, 1), shifted(late, 2)]

    def sibling(x):
        return lax.ppermute(x, "tp", [(j, j ^ 1) for j in range(4)])

    def across(x):
        return lax.ppermute(x, "tp", [(j, j ^ 2) for j in range(4)])

    def attention(blocks, tiles, after):
        sizes = (vertical.shape[1], slash.shape[1])
        return attend(
            blocks, tp, ctx, queries, table, near_kv, pairs, sizes, out_weight, tiles, after
        )

    def exchanged(send, keep):
        return add(keep, [sibling(x) for x in send])

    width = out_weight.shape[1]
    tiles = width // TILE
    assert local_blocks == 8
    attended, send, keep = attention((((3, 0), (2, 0)),), HEAD, ())
    total = (keep.astype(jnp.float32) + sibling(send).astype(jnp.float32)).astype(keep.dtype)
    arrived = [across(total)]
    total = exchanged(*project_staged(attended, out_weight, HEAD * TILE, 4, total))
    arrived.append(across(total))
    (attended,) = attention((((3, 1), (2, 1)),), 0, (total,))
    total = exchanged(*project(attended, out_weight, 0, 4, (arrived[0],)))
    arrived.append(across(total))
    (attended,) = attention((((1, 0), (1, 1)), ((0, 0), (0, 1))), 0, (total, arrived[1]))
    send, keep = project(attended, out_weight, 0, tiles, ())
    got = [sibling(x) for x in send]
    shape = (queries.shape[0] // 4, width)
    out = finish(keep[:HEAD], got[:HEAD], arrived[0], 0, 0, shape, None)
    out = finish(keep[HEAD:], got[HEAD:], arrived[1], HEAD, 0, shape, out)
    return finish(keep, got, arrived[2], 0, BLK, shape, out)


def solution(mesh):
    assert mesh.shape["tp"] == 4
    return jax.shard_map(
        functools.partial(shards, mesh.shape["ctx"]),
        mesh=mesh,
        in_specs=(
            P("ctx", "tp"),
            P("ctx", "tp"),
            P("ctx", "tp"),
            P("tp", None),
            P("tp", None),
            P("tp", None),
        ),
        out_specs=P(("ctx", "tp"), None),
        check_vma=False,
    )
```

```python
import functools

import jax
import jax.numpy as jnp
from jax import lax
from jax.experimental import pallas as pl
from jax.experimental.pallas import tpu as pltpu
from jax.sharding import PartitionSpec as P

HS = 128
BLK = 64
SPAN = 16
VMOST = 2
NEAR = 3
LANES = 128
MASKED = -1e30
EXP_SCALE = 1.4426950408889634 / (HS**0.5)
TILE = 1024
HEAD = 2
MIB = 1024 * 1024


SHORT = pl.CostEstimate(flops=0, bytes_accessed=0, transcendentals=0)


def vmem():
    return pl.BlockSpec(memory_space=pltpu.VMEM)


def smem():
    return pl.BlockSpec(memory_space=pltpu.SMEM)


def anywhere():
    return pl.BlockSpec(memory_space=pl.ANY)


def params(mib):
    return pltpu.CompilerParams(vmem_limit_bytes=mib * MIB)


def picked_blocks(vertical, shard, local_blocks):
    block = vertical - shard * local_blocks
    block = jnp.where((block >= 0) & (block < local_blocks), block, local_blocks)
    first = jnp.min(block)
    second = jnp.min(jnp.where(block > first, block, local_blocks))
    return [
        pl.ds(pl.multiple_of(jnp.minimum(x, local_blocks - 1) * BLK, BLK), BLK)
        for x in (first, second)
    ]


def pick_kernel(rank_ref, vert_ref, k_ref, v_ref, both_ref, late_ref, pair_ref):
    both_ref[:, :HS] = k_ref[...]
    both_ref[:, HS:] = v_ref[...]
    late_ref[...] = both_ref[both_ref.shape[0] - late_ref.shape[0] :, :]
    blocks = picked_blocks(vert_ref[...], rank_ref[0], k_ref.shape[0] // BLK)
    for slot, rows in enumerate(blocks):
        picked = both_ref[rows, :]
        for copy in range(pair_ref.shape[0]):
            pair_ref[copy, slot * BLK : (slot + 1) * BLK, :] = picked


def pick(rank, vertical, keys, values, copies):
    return pl.pallas_call(
        pick_kernel,
        out_shape=(
            jax.ShapeDtypeStruct((keys.shape[0], 2 * HS), keys.dtype),
            jax.ShapeDtypeStruct(((SPAN - 1) * BLK - keys.shape[0], 2 * HS), keys.dtype),
            jax.ShapeDtypeStruct((copies, VMOST * BLK, 2 * HS), keys.dtype),
        ),
        in_specs=[smem(), vmem(), vmem(), vmem()],
        out_specs=(vmem(),) * 3,
        compiler_params=params(60),
        name="pick",
    )(rank, vertical, keys, values)


def member(table, blocks):
    found = table[:, :1] == blocks
    for column in range(1, table.shape[1]):
        found = found | (table[:, column : column + 1] == blocks)
    return found


def pool_blocks(vertical, rank, slots, local_blocks):
    lane = lax.broadcasted_iota(jnp.int32, (vertical.shape[0], LANES), 1)
    slot = lane // VMOST
    shard = jnp.where(slot < slots, 2 * slot + (rank & 1), 2 * (slot - slots) + 1 - (rank & 1))
    shard = jnp.where(slot < 2 * slots, shard, -1)
    first = jnp.full((1, LANES), local_blocks, jnp.int32)
    second = first
    for j in reversed(range(local_blocks)):
        here = member(vertical, shard * local_blocks + j)
        here = jnp.max(jnp.where(here, 1, 0), axis=0, keepdims=True) == 1
        second = jnp.where(here, first, second)
        first = jnp.where(here, j, first)
    picked = jnp.where(lane % VMOST == 0, first, second)
    return jnp.where((picked < local_blocks) & (shard >= 0), shard * local_blocks + picked, -1)


def tables_kernel(slots, rank_ref, vert_ref, slash_ref, own_ref, table_ref, copy_ref):
    copy_ref[...] = own_ref[...]
    local_blocks = own_ref.shape[0] // BLK
    table_ref[0, :, : vert_ref.shape[1]] = vert_ref[...]
    table_ref[1, :, : slash_ref.shape[1]] = slash_ref[...]
    table_ref[2] = pool_blocks(vert_ref[...], rank_ref[0], slots, local_blocks)


def tables(rank, vertical, slash, own, slots):
    shape = (3, vertical.shape[0], LANES)
    return pl.pallas_call(
        functools.partial(tables_kernel, slots),
        out_shape=(
            jax.ShapeDtypeStruct(shape, jnp.int32),
            jax.ShapeDtypeStruct(own.shape, own.dtype),
        ),
        in_specs=[smem(), vmem(), vmem(), vmem()],
        out_specs=(vmem(), vmem()),
        compiler_params=params(4),
        cost_estimate=SHORT,
        name="tables",
    )(rank, vertical, slash, own)


def attend_kernel(
    slots, tiles, sizes, place, tp_ref, ctx_ref, q_0, q_1, table_ref, own, kv_1, kv_2, *refs
):
    pairs = refs[:2]
    w_hbm = refs[2]
    kv_win, e_win, kv_pool, e_pool, attended, weight, arrival, landed = refs[-8:]
    outs = refs[-11:-8] if tiles else refs[-9:-8]
    step = pl.program_id(0)
    heads = table_ref.shape[1]
    rows = own.shape[0]
    local_blocks = rows // BLK
    far_rows = e_pool.shape[0]
    dtype = q_0.dtype
    rank = ctx_ref[0]
    vert = table_ref[0][:, : sizes[0]]
    slash = table_ref[1][:, : sizes[1]]
    block = table_ref[2]

    def fetch(t):
        return pltpu.make_async_copy(
            w_hbm.at[:, pl.ds(t * TILE, TILE)], weight.at[t], arrival.at[t]
        )

    @pl.when(step == 0)
    def _():
        reach = kv_2.shape[0]
        places = ((kv_2, 0), (kv_1, reach), (own, reach + rows))
        copies = [
            pltpu.make_async_copy(x, kv_win.at[pl.ds(at, x.shape[0]), :], landed.at[s])
            for s, (x, at) in enumerate(places)
        ]
        copies += [
            pltpu.make_async_copy(
                x.at[pl.ds(0, slots)], kv_pool.at[pl.ds(p * slots, slots)], landed.at[NEAR + p]
            )
            for p, x in enumerate(pairs)
        ]
        for copy in copies:
            copy.start()
        for t in range(tiles):
            fetch(t).start()
        key = lax.broadcasted_iota(jnp.int32, e_win.shape, 0)
        lane = lax.broadcasted_iota(jnp.int32, e_win.shape, 1)
        last = (key - (SPAN - 1) * BLK == lane - BLK) & (lane >= BLK)
        e_win[...] = jnp.where((key // BLK == lane) | last, 1.0, 0.0).astype(dtype)
        key = lax.broadcasted_iota(jnp.int32, e_pool.shape, 0)
        lane = lax.broadcasted_iota(jnp.int32, e_pool.shape, 1)
        e_pool[...] = jnp.where(key // BLK == lane, 1.0, 0.0).astype(dtype)
        for copy in copies:
            copy.wait()

    lane = lax.broadcasted_iota(jnp.int32, (heads, LANES), 1)
    row = lax.broadcasted_iota(jnp.int32, (BLK, LANES), 0)
    above = lax.broadcasted_iota(jnp.int32, (BLK, LANES), 1) - BLK > row
    above = jnp.where(above, MASKED, 0.0).astype(jnp.float32)
    offset_ok = member(slash, SPAN - 1 - lane)
    pool_ok = member(vert, block) & (block >= 0)
    contract = (((1,), (1,)), ((), ()))

    def with_ones(values):
        return jnp.concatenate([values, jnp.ones((values.shape[0], LANES), dtype)], axis=1)

    near, far_q, windows = [], [], []
    for u, q_ref in enumerate((q_0, q_1)):
        here = place(u, step, tp_ref)
        q = q_ref[...]
        q = jnp.concatenate([q[:, h * HS : (h + 1) * HS] for h in range(heads)], axis=0)
        first = rank * local_blocks + here - (SPAN - 1)
        seen = first + lane
        ok = (seen >= 0) & (offset_ok | member(vert, seen))
        mask = jnp.where(ok | (lane >= SPAN), 0.0, MASKED).astype(jnp.float32)
        mask = (mask[:, None, :] + above[None]).reshape(heads * BLK, LANES).astype(dtype)
        far_mask = jnp.where(pool_ok & (block < first), 0.0, MASKED).astype(jnp.float32)
        far_mask = jnp.broadcast_to(far_mask[:, None, :], (heads, BLK, LANES))
        far_mask = far_mask.reshape(heads * BLK, LANES).astype(dtype)
        far_q.append(jnp.concatenate([q, far_mask], axis=1))
        window = pl.ds(pl.multiple_of(here * BLK, BLK), SPAN * BLK)
        windows.append(window)
        keys = jnp.concatenate([kv_win[window, :HS], e_win[...]], axis=1)
        near.append(
            lax.dot_general(
                jnp.concatenate([q, mask], axis=1),
                keys,
                contract,
                preferred_element_type=jnp.float32,
            )
        )
    far = lax.dot_general(
        jnp.concatenate(far_q, axis=0),
        jnp.concatenate([kv_pool[:, :, :HS].reshape(far_rows, HS), e_pool[...]], axis=1),
        contract,
        preferred_element_type=jnp.float32,
    )
    far_values = with_ones(kv_pool[:, :, HS:].reshape(far_rows, HS))
    for u in range(2):
        far_u = far[u * heads * BLK : (u + 1) * heads * BLK]
        top = jnp.maximum(
            jnp.max(near[u], axis=1, keepdims=True), jnp.max(far_u, axis=1, keepdims=True)
        )
        probs = jnp.exp2((near[u] - top) * EXP_SCALE).astype(dtype)
        values = with_ones(kv_win[windows[u], HS:])
        summed = jnp.dot(probs, values, preferred_element_type=jnp.float32)
        probs = jnp.exp2((far_u - top) * EXP_SCALE).astype(dtype)
        summed = summed + jnp.dot(probs, far_values, preferred_element_type=jnp.float32)
        out = (summed[:, :HS] / summed[:, HS:]).astype(dtype)
        at = pl.ds(pl.multiple_of((step * 2 + u) * BLK, BLK), BLK)
        for h in range(heads):
            attended[at, h * HS : (h + 1) * HS] = out[h * BLK : (h + 1) * BLK]

    @pl.when(step == pl.num_programs(0) - 1)
    def _():
        outs[0][...] = attended[...]
        half = attended.shape[0] // 2
        for t in range(tiles):
            fetch(t).wait()
            product = jnp.dot(attended[...], weight[t], preferred_element_type=jnp.float32)
            product = product.astype(dtype)
            outs[1][:, t * TILE : (t + 1) * TILE] = product[:half]
            outs[2][:, t * TILE : (t + 1) * TILE] = product[half:]


def attend(blocks, tp, ctx, queries, table, near_kv, pairs, sizes, out_weight, tiles, after):
    width = queries.shape[1]
    rows = near_kv[0].shape[0]
    assert near_kv[2].shape[0] + rows == (SPAN - 1) * BLK
    quarter = rows // BLK // 4
    steps = len(blocks)
    slots = pairs[1].shape[0]
    dtype = queries.dtype
    far = 2 * slots * VMOST * BLK

    def place(u, g, tp):
        flip, block = blocks[-1][u]
        for step in range(steps - 1):
            flip = jnp.where(g == step, blocks[step][u][0], flip)
            block = jnp.where(g == step, blocks[step][u][1], block)
        return (tp[0] ^ flip) * quarter + block

    def whole(shape):
        return pl.BlockSpec(shape, lambda g, tp, ctx: (0,) * len(shape))

    out_shapes = [(steps * 2 * BLK, width)]
    if tiles:
        out_shapes += [(steps * BLK, tiles * TILE)] * 2
    return pl.pallas_call(
        functools.partial(attend_kernel, slots, tiles, sizes, place),
        out_shape=[jax.ShapeDtypeStruct(shape, dtype) for shape in out_shapes],
        grid_spec=pltpu.PrefetchScalarGridSpec(
            num_scalar_prefetch=2,
            grid=(steps,),
            in_specs=[
                pl.BlockSpec((BLK, width), lambda g, tp, ctx: (place(0, g, tp), 0)),
                pl.BlockSpec((BLK, width), lambda g, tp, ctx: (place(1, g, tp), 0)),
            ]
            + [whole(table.shape)]
            + [anywhere() for _ in [*near_kv, *pairs, out_weight, *after]],
            out_specs=[whole(shape) for shape in out_shapes],
            scratch_shapes=[
                pltpu.VMEM((near_kv[2].shape[0] + 2 * rows, 2 * HS), dtype),
                pltpu.VMEM((SPAN * BLK, LANES), dtype),
                pltpu.VMEM((2 * slots, VMOST * BLK, 2 * HS), dtype),
                pltpu.VMEM((far, LANES), dtype),
                pltpu.VMEM((steps * 2 * BLK, width), dtype),
                pltpu.VMEM((max(tiles, 1), out_weight.shape[0], TILE), dtype),
                pltpu.SemaphoreType.DMA((max(tiles, 1),)),
                pltpu.SemaphoreType.DMA((NEAR + 2,)),
            ],
        ),
        compiler_params=params(40),
        cost_estimate=SHORT,
        name="attend",
    )(tp, ctx, queries, queries, table, *near_kv, *pairs, out_weight, *after)


def project_staged_kernel(first, a_ref, w_ref, *refs):
    tiles = len(refs) // 2
    outs = refs[-2 * tiles :]
    half, tile = outs[0].shape
    for t in range(tiles):
        weight = w_ref[:, first + t * tile : first + (t + 1) * tile]
        product = jnp.dot(a_ref[...], weight, preferred_element_type=jnp.float32)
        product = product.astype(a_ref.dtype)
        outs[t][...] = product[:half]
        outs[tiles + t][...] = product[half:]


def project_staged(attended, weight, first, tiles, after):
    rows, depth = attended.shape
    tile = (weight.shape[1] - first) // tiles
    part = jax.ShapeDtypeStruct((rows // 2, tile), attended.dtype)
    outs = pl.pallas_call(
        functools.partial(project_staged_kernel, first),
        out_shape=[part] * (2 * tiles),
        in_specs=[vmem(), vmem(), anywhere()],
        out_specs=[vmem()] * (2 * tiles),
        compiler_params=params(24),
        cost_estimate=SHORT,
        name="project",
    )(attended, weight, after)
    return outs[:tiles], outs[tiles:]


def project_kernel(first, a_ref, w_hbm, *refs):
    weight, arrival = refs[-2:]
    tiles, _, tile = weight.shape
    outs = refs[-2 - 2 * tiles : -2]
    half = outs[0].shape[0]

    def fetch(t):
        return pltpu.make_async_copy(
            w_hbm.at[:, pl.ds(first + t * tile, tile)], weight.at[t], arrival.at[t]
        )

    for t in range(tiles):
        fetch(t).start()
    for t in range(tiles):
        fetch(t).wait()
        product = jnp.dot(a_ref[...], weight[t], preferred_element_type=jnp.float32)
        product = product.astype(a_ref.dtype)
        outs[t][...] = product[:half]
        outs[tiles + t][...] = product[half:]


def project(attended, out_weight, first, tiles, after):
    rows, depth = attended.shape
    tile = (out_weight.shape[1] - first) // tiles
    part = jax.ShapeDtypeStruct((rows // 2, tile), attended.dtype)
    outs = pl.pallas_call(
        functools.partial(project_kernel, first),
        out_shape=[part] * (2 * tiles),
        in_specs=[vmem(), anywhere()] + [anywhere() for _ in after],
        out_specs=[vmem()] * (2 * tiles),
        scratch_shapes=[
            pltpu.VMEM((tiles, depth, tile), attended.dtype),
            pltpu.SemaphoreType.DMA((tiles,)),
        ],
        compiler_params=params(50),
        cost_estimate=SHORT,
        name="project",
    )(attended, out_weight, *after)
    return outs[:tiles], outs[tiles:]


def add_kernel(*refs):
    out_ref = refs[-1]
    pieces = len(refs) // 2
    first = 0
    for t in range(pieces):
        total = refs[t][...].astype(jnp.float32) + refs[pieces + t][...].astype(jnp.float32)
        last = first + total.shape[1]
        out_ref[:, first:last] = total.astype(out_ref.dtype)
        first = last


def add(keep, got):
    rows, columns = keep[0].shape[0], sum(x.shape[1] for x in keep)
    return pl.pallas_call(
        add_kernel,
        out_shape=jax.ShapeDtypeStruct((rows, columns), keep[0].dtype),
        in_specs=[vmem()] * (2 * len(keep)),
        out_specs=vmem(),
        compiler_params=params(16),
        cost_estimate=SHORT,
        name="add",
    )(*keep, *got)


def finish_kernel(tiles, first, top, *refs):
    arrived_ref = refs[2 * tiles]
    out_ref, tiles_ref, sent = refs[-3:]
    rows = pl.ds(top, arrived_ref.shape[0])
    copies = []
    for t in range(tiles):
        total = refs[t][rows, :].astype(jnp.float32) + refs[tiles + t][rows, :].astype(jnp.float32)
        total = total + arrived_ref[:, t * TILE : (t + 1) * TILE].astype(jnp.float32)
        tiles_ref[t] = total.astype(out_ref.dtype)
        columns = pl.ds((first + t) * TILE, TILE)
        copies.append(
            pltpu.make_async_copy(tiles_ref.at[t], out_ref.at[rows, columns], sent.at[t])
        )
        copies[-1].start()
    for copy in copies:
        copy.wait()


def finish(keep, got, arrived, first, top, shape, out):
    tiles = len(keep)
    before = [] if out is None else [out]
    return pl.pallas_call(
        functools.partial(finish_kernel, tiles, first, top),
        out_shape=jax.ShapeDtypeStruct(shape, arrived.dtype),
        in_specs=[vmem()] * (2 * tiles + 1) + [anywhere() for _ in before],
        out_specs=anywhere(),
        input_output_aliases={2 * tiles + 1: 0} if before else {},
        scratch_shapes=[
            pltpu.VMEM((tiles, arrived.shape[0], TILE), arrived.dtype),
            pltpu.SemaphoreType.DMA((tiles,)),
        ],
        compiler_params=params(16),
        cost_estimate=SHORT,
        name="finish",
    )(*keep, *got, arrived, *before)


def shards(ctx_size, queries, keys, values, out_weight, vertical, slash):
    local_blocks = queries.shape[0] // BLK
    assert ctx_size % 2 == 0 and (NEAR - 1) * local_blocks >= SPAN - 1
    ctx = jnp.reshape(lax.axis_index("ctx"), (1,)).astype(jnp.int32)
    tp = jnp.reshape(lax.axis_index("tp"), (1,)).astype(jnp.int32)

    def shifted(x, by):
        return lax.ppermute(x, "ctx", [(r, r + by) for r in range(ctx_size - by)])

    half = ctx_size // 2
    own, late, pair = pick(ctx, vertical, keys, values, half)
    parities = [list(range(odd, ctx_size, 2)) for odd in (0, 1)]
    pairs = [lax.all_to_all(pair, "ctx", 0, 0, axis_index_groups=parities, tiled=True)]
    needed = pairs[0][: half - 1]
    pairs.append(lax.ppermute(needed, "ctx", [(r, r ^ 1) for r in range(ctx_size)]))
    table, own_copy = tables(ctx, vertical, slash, own, half - 1)
    near_kv = [own_copy, shifted(own, 1), shifted(late, 2)]

    def sibling(x):
        return lax.ppermute(x, "tp", [(j, j ^ 1) for j in range(4)])

    def across(x):
        return lax.ppermute(x, "tp", [(j, j ^ 2) for j in range(4)])

    def attention(blocks, tiles, after):
        sizes = (vertical.shape[1], slash.shape[1])
        return attend(
            blocks, tp, ctx, queries, table, near_kv, pairs, sizes, out_weight, tiles, after
        )

    def exchanged(send, keep):
        return add(keep, [sibling(x) for x in send])

    width = out_weight.shape[1]
    tiles = width // TILE
    assert local_blocks == 8
    attended, send, keep = attention((((3, 0), (2, 0)),), HEAD, ())
    total = (keep.astype(jnp.float32) + sibling(send).astype(jnp.float32)).astype(keep.dtype)
    arrived = [across(total)]
    total = exchanged(*project_staged(attended, out_weight, HEAD * TILE, 4, total))
    arrived.append(across(total))
    (attended,) = attention((((3, 1), (2, 1)),), 0, (total,))
    total = exchanged(*project(attended, out_weight, 0, 4, (arrived[0],)))
    arrived.append(across(total))
    (attended,) = attention((((1, 0), (1, 1)), ((0, 0), (0, 1))), 0, (total,))
    send, keep = project(attended, out_weight, 0, tiles, (arrived[1],))
    got = [sibling(x) for x in send]
    shape = (queries.shape[0] // 4, width)
    out = finish(keep[:HEAD], got[:HEAD], arrived[0], 0, 0, shape, None)
    out = finish(keep[HEAD:], got[HEAD:], arrived[1], HEAD, 0, shape, out)
    return finish(keep, got, arrived[2], 0, BLK, shape, out)


def solution(mesh):
    assert mesh.shape["tp"] == 4
    return jax.shard_map(
        functools.partial(shards, mesh.shape["ctx"]),
        mesh=mesh,
        in_specs=(
            P("ctx", "tp"),
            P("ctx", "tp"),
            P("ctx", "tp"),
            P("tp", None),
            P("tp", None),
            P("tp", None),
        ),
        out_specs=P(("ctx", "tp"), None),
        check_vma=False,
    )
```
